128 devices in a mesh: ctx: 16 (over z_lo, x, core), ep: 8 (over z_hi, y).
Axes of the slice: x: 4, y: 4, z: 4 (z_hi: 2, z_lo: 2; z = z_hi * 2 + z_lo), core: 2. Of those that a mesh axis runs over, the one named last changes fastest.
Arguments:
- layer_in: bfloat16 [16384, 1024], P(('ctx', 'ep')), may hold values from -6 to 6
- pair_of: int32 [16], replicated, may hold values from 0 to 15, each once
- routes: int32 [16384, 8], P(('ctx', 'ep')), may hold values from 0 to 31, all different within a row; in each aligned block of 128 rows (0 to 127, 128 to 255, ...) at most 48 rows name the same one
- gate_weights: float32 [16384, 8], P(('ctx', 'ep')), may hold values from 0.06 to 0.19
- capacity: int32 [32], replicated, may hold values from 24 to 48, as said below
- attn_gain: float32 [1024], replicated, may hold values from 0.1 to 1.9
- query_weight: bfloat16 [1024, 1024], P(None, 'ep'), may hold values from -0.5 to 0.5
- key_value_weight: bfloat16 [1024, 8, 128], P(None, 'ep'), may hold values from -0.5 to 0.5
- output_weight: bfloat16 [1024, 1024], P('ep'), may hold values from -1.5 to 1.5
- moe_gain: float32 [1024], replicated, may hold values from 0.1 to 1.9
- expert_in: bfloat16 [32, 1024, 1024], P('ep'), may hold values from -0.1875 to 0.1875
- expert_out: bfloat16 [32, 512, 1024], P('ep'), may hold values from -1 to 1
- out_grad: bfloat16 [16384, 1024], P(('ctx', 'ep')), may hold values from -6 to 6
Outputs:
- layer_out: bfloat16 [16384, 1024], P(('ctx', 'ep'))
- input_grad: float32 [16384, 1024], P(('ctx', 'ep'))
- attn_gain_grad: float32 [1024], replicated
- query_grad: float32 [1024, 1024], P('ctx', 'ep')
- keyval_grad: float32 [1024, 8, 128], P('ctx', 'ep')
- output_grad: float32 [1024, 1024], P('ep', 'ctx')
- moe_gain_grad: float32 [1024], replicated
- expert_in_grad: float32 [32, 1024, 1024], P('ep', 'ctx')
- expert_out_grad: float32 [32, 512, 1024], P('ep', 'ctx')
The draws below stay inside these ranges and needn't reach their ends.
Inputs may be any that keep to these rules, and one draw needn't show every extreme that they name: `pair_of`: a permutation of the context devices' indices. `routes`: each row names 8 different experts; no expert is named by more than 48 rows of one device's tokens. `capacity`: at least 24; some expert has exactly 48.
All inputs are finite; a program needn't handle non-finite values.
Results may differ from the reference program's by a relative error of at most 0.028.
Values may be sent and summed in bfloat16 or wider, within the bound.
No kernel may reach another device: no remote copies, remote signals or barrier semaphores. Data moves between devices by JAX's collectives and lax.ppermute only.
A program may use at most 256 MiB of HBM per device.

```python
import math
import jax
import jax.numpy as jnp
import numpy as np
from jax import lax

MODEL_DIMENSION = 1024
QUERY_HEADS = 16
KEY_VALUE_HEADS = 8
HEAD_DIMENSION = 64
FF = 512
EXPERTS = 32
TOP = 8
SEQUENCE_COUNT = 2
TOK_DEV = 128
TOKEN_COUNT = 16384
CAP = 48
N_CTX = 16
N_EP = 8


def draw_capacity(key, part):
    key = jax.random.fold_in(key, 11)
    key_draw, key_pick = jax.random.split(key)
    drawn_caps = jax.random.randint(key_draw, (EXPERTS,), CAP // 2, CAP + 1)
    chosen = jax.random.randint(key_pick, (), 0, EXPERTS)
    return jnp.where(jnp.arange(EXPERTS) == chosen, CAP, drawn_caps).astype(jnp.int32)


def level_of(stream_key, dims, pieces, smallest, top_value):
    level, own = 1.0, jax.random.fold_in(stream_key, 6)
    for position, shards_of in pieces:
        heights = jnp.exp(jax.random.uniform(jax.random.fold_in(own, position), (shards_of,), jnp.float32, smallest / len(pieces), top_value / len(pieces)))
        level = level * jnp.repeat(heights, dims[position] // shards_of).reshape([-1 if axis == position else 1 for axis in range(len(dims))])
    return level


def deal_out(key, own, number, rows, amount, top, reach, lean):
    sequence = jax.random.permutation(key, amount)
    crowded, ordinary = portions_of(amount, rows * top, reach, lean, True), portions_of(amount, rows * top, reach, lean, False)
    places = jnp.arange(amount)

    def named(tallies, offset_by):
        used = int((tallies > 0).sum())
        fixed = max(1, used // 4)
        moved = fixed + (places - fixed + offset_by * (used - fixed)) % max(1, amount - fixed)
        return jnp.zeros((amount,), jnp.int32).at[sequence[jnp.where(places < fixed, places, moved)]].set(jnp.asarray(tallies, jnp.int32))

    tallies = jnp.where(number % 4 == 0, named(crowded, number // 4), named(ordinary, number - number // 4 - 1))
    mixed = jax.random.permutation(jax.random.fold_in(own, 3), amount)
    giver, taker = mixed[0:amount // 2 * 2:2], mixed[1:amount // 2 * 2:2]
    room = jnp.minimum(tallies[giver] - 1, reach - tallies[taker]) // 2
    room = jnp.where((giver == sequence[0]) | (taker == sequence[0]) | (tallies[taker] == 0), 0, jnp.maximum(room, 0))
    moved = jax.random.randint(jax.random.fold_in(own, 4), (amount // 2,), 0, 1 << 20) % (room + 1)
    tallies = tallies.at[giver].add(-moved).at[taker].add(moved)
    items = jnp.searchsorted(jnp.cumsum(tallies), jnp.arange(rows * top), side="right").astype(jnp.int32)
    table = items.reshape(top, rows).T
    table = table[jax.random.permutation(jax.random.fold_in(own, 1), rows)]
    offset_by = jax.random.randint(jax.random.fold_in(own, 2), (rows, 1), 0, top)
    return jnp.take_along_axis(table, (jnp.arange(top)[None, :] + offset_by) % top, axis=1)


def portions_of(count, total, bound, lean, full):
    weights = [(1 << 20) // math.isqrt(grade ** lean) + 1 for grade in range(1, count + 1)]
    largest = bound if full else min(bound, max(-(-total // count), total * weights[0] // sum(weights)))
    least = 1 if total - largest >= count - 1 else 0
    holding, surplus = [largest] + [least] * (count - 1), total - largest - least * (count - 1)
    while surplus > 0:
        movable = [i for i in range(1, count) if holding[i] < largest] or [i for i in range(1, count) if holding[i] < bound]
        pool, budget = sum([weights[i] for i in movable]), surplus
        for i in movable:
            extra = min(bound - holding[i], max(1, budget * weights[i] // pool), surplus)
            holding[i] = holding[i] + extra
            surplus = surplus - extra
    return np.array(holding)


def noise(rng, extent, scale, bound, shards=(), held_as=jnp.bfloat16):
    entries = jax.random.normal(rng, extent, jnp.float32) * scale
    if len(shards) > 0:
        entries = level_of(rng, extent, shards, -0.22, 0.18) * entries
    return jnp.clip(entries, min=-bound, max=bound).astype(held_as)


def setup_inputs(seed: int = 0) -> dict:
    key_list = jax.random.split(jax.random.key(seed), 14)
    layer_in = noise(key_list[0], (TOKEN_COUNT, MODEL_DIMENSION), 1.0, 6.0, ((0, 128),))
    pair_of = jax.random.permutation(key_list[1], N_CTX).astype(jnp.int32)
    routes_keys = jax.random.split(jax.random.fold_in(key_list[2], 1), TOKEN_COUNT // TOK_DEV)
    routes_turns = jax.random.permutation(jax.random.fold_in(key_list[2], 3), TOKEN_COUNT // TOK_DEV)
    routes = jax.vmap(lambda own, number: deal_out(jax.random.fold_in(key_list[2], 2), own, number, TOK_DEV, EXPERTS, TOP, CAP, 1))(routes_keys, routes_turns).reshape((TOKEN_COUNT, TOP))
    gate_weights = jnp.clip(0.06 + 0.13 * jax.random.uniform(key_list[3], (TOKEN_COUNT, TOP), jnp.float32) ** level_of(key_list[3], (TOKEN_COUNT, TOP), ((0, 128),), -0.2, 0.2), 0.06, 0.19)
    capacity = draw_capacity(jax.random.fold_in(key_list[13], 71), 0)
    attn_gain = jnp.clip(1.0 + 0.18 * jax.random.normal(key_list[5], (MODEL_DIMENSION,), jnp.float32), 0.1, 1.9)
    query_weight = noise(key_list[6], (MODEL_DIMENSION, QUERY_HEADS * HEAD_DIMENSION), (MODEL_DIMENSION // 8) ** -0.5, 0.5, ((1, 8),))
    key_value_weight = noise(key_list[7], (MODEL_DIMENSION, KEY_VALUE_HEADS, 2 * HEAD_DIMENSION), (MODEL_DIMENSION // 8) ** -0.5, 0.5, ((1, 8),))
    output_weight = noise(key_list[8], (QUERY_HEADS * HEAD_DIMENSION, MODEL_DIMENSION), (HEAD_DIMENSION // 4) ** -0.5, 1.5, ((0, 8),))
    moe_gain = jnp.clip(1.0 + 0.18 * jax.random.normal(key_list[9], (MODEL_DIMENSION,), jnp.float32), 0.1, 1.9)
    expert_in = noise(key_list[10], (EXPERTS, MODEL_DIMENSION, 2 * FF), MODEL_DIMENSION ** -0.5, 0.1875, ((0, 8),))
    expert_out = noise(key_list[11], (EXPERTS, FF, MODEL_DIMENSION), (FF // 16) ** -0.5, 1.0, ((0, 8),))
    out_grad = noise(key_list[12], (TOKEN_COUNT, MODEL_DIMENSION), 1.0, 6.0, ((0, 128),))
    return dict(layer_in=layer_in, pair_of=pair_of, routes=routes, gate_weights=gate_weights, capacity=capacity, attn_gain=attn_gain, query_weight=query_weight, key_value_weight=key_value_weight, output_weight=output_weight, moe_gain=moe_gain, expert_in=expert_in, expert_out=expert_out, out_grad=out_grad)


NORM_EPS = 1e-06
ROPE_BASE = 10000.0
SCORE_SCALE = 1.0 / 64.0
MASK_FILL = -1e+30

@jax.custom_vjp
def low(v):
    return lax.optimization_barrier(v.astype(jnp.bfloat16)).astype(jnp.float32)

@jax.custom_vjp
def low_back(v):
    return v

def low_keep(v):
    return (low(v), None)

def low_pass(kept, grad):
    return (grad,)

def back_keep(v):
    return (v, None)

def back_low(kept, grad):
    return (low(grad),)
low.defvjp(low_keep, low_pass)
low_back.defvjp(back_keep, back_low)

def matrix_multiply(left, right):
    return jnp.dot(left, right, precision=lax.Precision.HIGHEST)

def rms_norm(values, gain):
    factor = lax.rsqrt(lax.optimization_barrier(jnp.mean(values * values, axis=-1, keepdims=True)) + NORM_EPS)
    return values * factor * gain

def rotate(values, cosine_tab, sine_tab):
    half_dim = values.shape[-1] // 2
    turned = jnp.concatenate([-values[..., half_dim:], values[..., :half_dim]], axis=-1)
    return values * cosine_tab + turned * sine_tab

def angle_tables(positions, head_dim):
    steps_idx = jnp.arange(head_dim // 2, dtype=jnp.float32)
    freqs = ROPE_BASE ** (-2.0 * steps_idx / head_dim)
    angles = positions.astype(jnp.float32)[:, None] * freqs[None, :]
    angles = jnp.concatenate([angles, angles], axis=-1)
    return (jnp.cos(angles), jnp.sin(angles))

def block_positions(pair_ids, block_len, ctx_count):
    upper = 2 * ctx_count - 1 - pair_ids
    blocks = jnp.stack([pair_ids, upper], axis=-1)
    return blocks[..., None] * block_len + jnp.arange(block_len, dtype=jnp.int32)

def reference(layer_in, pair_of, routes, gate_weights, capacity, attn_gain, query_weight, key_value_weight, output_weight, moe_gain, expert_in, expert_out, out_grad):
    device_count = N_CTX * N_EP
    ctx_rows = TOK_DEV * N_EP
    block_len = ctx_rows // (2 * SEQUENCE_COUNT)
    sequence_length = N_CTX * 2 * block_len
    head_grouping = QUERY_HEADS // KEY_VALUE_HEADS
    key_pos = block_positions(pair_of.astype(jnp.int32), block_len, N_CTX)
    seq_pos = key_pos.reshape(sequence_length)
    allowed = seq_pos[:, None] >= seq_pos[None, :]
    token_pos = jnp.broadcast_to(key_pos[:, None], (N_CTX, SEQUENCE_COUNT, 2, block_len)).reshape(TOKEN_COUNT)
    cosine_tab, sine_tab = angle_tables(token_pos, HEAD_DIMENSION)
    cosine_tab = cosine_tab[:, None, :]
    sine_tab = sine_tab[:, None, :]
    dev_routes = routes.reshape(device_count, TOK_DEV * TOP).astype(jnp.int32)
    one_hot = (dev_routes[..., None] == jnp.arange(EXPERTS, dtype=jnp.int32)).astype(jnp.int32)
    earlier = jnp.cumsum(one_hot, axis=1) - one_hot
    rank_in = lax.optimization_barrier(jnp.sum(earlier * one_hot, axis=-1))
    limits = capacity[dev_routes]
    device_ids = jnp.arange(device_count, dtype=jnp.int32)[:, None]
    slot_total = EXPERTS * device_count * CAP
    slot_ids = jnp.where(rank_in < limits, dev_routes * (device_count * CAP) + device_ids * CAP + rank_in, slot_total).reshape(-1)
    token_ids = jnp.arange(TOKEN_COUNT * TOP, dtype=jnp.int32) // TOP
    slot_tokens = jnp.full((slot_total,), TOKEN_COUNT, dtype=jnp.int32).at[slot_ids].set(token_ids, mode='drop')
    slot_gates = jnp.zeros((slot_total,), jnp.float32).at[slot_ids].set(gate_weights.reshape(-1), mode='drop')
    slot_tokens = slot_tokens.reshape(EXPERTS, device_count * CAP)
    slot_gates = slot_gates.reshape(EXPERTS, device_count * CAP)

    def into_sequences(values):
        tail_shape = values.shape[1:]
        shaped = values.reshape((N_CTX, SEQUENCE_COUNT, 2 * block_len) + tail_shape)
        shaped = jnp.swapaxes(shaped, 0, 1)
        return shaped.reshape((SEQUENCE_COUNT, sequence_length) + tail_shape)

    def from_seqs(values):
        tail_shape = values.shape[2:]
        shaped = values.reshape((SEQUENCE_COUNT, N_CTX, 2 * block_len) + tail_shape)
        shaped = jnp.swapaxes(shaped, 0, 1)
        return shaped.reshape((TOKEN_COUNT,) + tail_shape)

    def attend(inputs):
        queries, key_rows, value_rows = inputs
        raw_scores = jnp.einsum('gqd,kd->gqk', queries, key_rows, precision=lax.Precision.HIGHEST) * SCORE_SCALE
        scores = jnp.where(allowed, low_back(raw_scores), MASK_FILL)
        top_score = lax.optimization_barrier(jnp.max(scores, axis=-1, keepdims=True))
        exp_terms = jnp.exp(scores - top_score)
        prob_low = low(exp_terms / lax.optimization_barrier(jnp.sum(exp_terms, axis=-1, keepdims=True)))
        return jnp.einsum('gqk,kd->gqd', prob_low, value_rows, precision=lax.Precision.HIGHEST)

    def forward(x_float, gain_attn, w_query, key_value_matrix, w_output, gain_moe, w_expert_in, w_expert_out):
        normalized_rows = low(rms_norm(x_float, gain_attn))
        queries = matrix_multiply(normalized_rows, w_query).reshape(TOKEN_COUNT, QUERY_HEADS, HEAD_DIMENSION)
        key_value_rows = matrix_multiply(normalized_rows, key_value_matrix.reshape(MODEL_DIMENSION, KEY_VALUE_HEADS * 2 * HEAD_DIMENSION)).reshape(TOKEN_COUNT, KEY_VALUE_HEADS, 2, HEAD_DIMENSION)
        query_rotated = low(rotate(low_back(queries), cosine_tab, sine_tab))
        key_rotated = low(rotate(low_back(key_value_rows[:, :, 0]), cosine_tab, sine_tab))
        value_reduced = low(low_back(key_value_rows[:, :, 1]))
        query_sequence = into_sequences(query_rotated).reshape(SEQUENCE_COUNT, sequence_length, KEY_VALUE_HEADS, head_grouping, HEAD_DIMENSION).transpose(0, 2, 3, 1, 4).reshape(SEQUENCE_COUNT * KEY_VALUE_HEADS, head_grouping, sequence_length, HEAD_DIMENSION)
        key_sequence = into_sequences(key_rotated).transpose(0, 2, 1, 3).reshape(SEQUENCE_COUNT * KEY_VALUE_HEADS, sequence_length, HEAD_DIMENSION)
        value_sequence = into_sequences(value_reduced).transpose(0, 2, 1, 3).reshape(SEQUENCE_COUNT * KEY_VALUE_HEADS, sequence_length, HEAD_DIMENSION)
        attention_result = lax.map(jax.checkpoint(attend), (query_sequence, key_sequence, value_sequence))
        attention_result = attention_result.reshape(SEQUENCE_COUNT, KEY_VALUE_HEADS, head_grouping, sequence_length, HEAD_DIMENSION).transpose(0, 3, 1, 2, 4).reshape(SEQUENCE_COUNT, sequence_length, QUERY_HEADS * HEAD_DIMENSION)
        merged = low(low_back(from_seqs(attention_result)))
        residual = x_float + low_back(matrix_multiply(merged, w_output))
        normed_moe = low(rms_norm(residual, gain_moe))

        def expert_step(totals, inputs):
            weight_in, weight_out, members, weights = inputs
            rows_in = low_back(jnp.take(normed_moe, members, axis=0, mode='fill', fill_value=0.0))
            gate_up = low_back(matrix_multiply(rows_in, weight_in))
            activated = low(jax.nn.silu(gate_up[:, :FF]) * gate_up[:, FF:])
            produced = low(low_back(matrix_multiply(activated, weight_out)))
            totals = totals.at[members].add(weights[:, None] * produced, mode='drop')
            return (totals, None)
        moe_sum, unused = lax.scan(jax.checkpoint(expert_step), jnp.zeros((TOKEN_COUNT, MODEL_DIMENSION), jnp.float32), (w_expert_in, w_expert_out, slot_tokens, slot_gates))
        return residual + moe_sum
    result, pullback = jax.vjp(forward, layer_in.astype(jnp.float32), attn_gain, query_weight.astype(jnp.float32), key_value_weight.astype(jnp.float32), output_weight.astype(jnp.float32), moe_gain, expert_in.astype(jnp.float32), expert_out.astype(jnp.float32))
    grads = pullback(out_grad.astype(jnp.float32))
    return (result.astype(jnp.bfloat16), grads[0], grads[1], grads[2], grads[3], grads[4], grads[5], grads[6], grads[7])
```

```python
import jax
import jax.numpy as jnp
from jax import lax
from jax.experimental import pallas as pl
from jax.experimental.pallas import tpu as pltpu
from jax.sharding import PartitionSpec as P

VMEM_LIMIT = 56 * 1024 * 1024
CAP = 48

HEAD_DIMENSION = 64
SCORE_SCALE = 1.0 / 64.0
MASK_FILL = -1e30
LOG2E = 1.4426950408889634
BLOCK = 256


def causal_mask(width):
    key_at = lax.broadcasted_iota(jnp.int32, (BLOCK, width), 0)
    query_at = lax.broadcasted_iota(jnp.int32, (BLOCK, width), 1) % BLOCK
    return key_at <= query_at


def turn_rows(u, cosine, sine):
    half = HEAD_DIMENSION // 2
    u1, u2 = u[:half], u[half:]
    return jnp.concatenate([u1 * cosine - u2 * sine, u2 * cosine + u1 * sine], axis=0)


def forward_kernel(slots, query_t, cosine, sine, *refs):
    pieces, (out_rows, out_full, out_lse, q_pad, keyval, arrived, top, total, acc) = refs[:-9], refs[-9:]
    copies = start_copies(pieces, keyval, arrived)
    seqs = keyval.shape[1]
    heads = query_t.shape[0] // HEAD_DIMENSION
    width = heads * BLOCK
    blocks = 2 * keyval.shape[0]
    factor = SCORE_SCALE * LOG2E
    low, high = slots[0], blocks - 1 - slots[0]

    for s in range(seqs):
        q_pad[s, HEAD_DIMENSION:, :] = jnp.zeros((HEAD_DIMENSION, 2 * width), jnp.bfloat16)
        for h in range(2):
            for g in range(heads):
                rows = slice(g * HEAD_DIMENSION, (g + 1) * HEAD_DIMENSION)
                at = (s * 2 + h) * BLOCK
                turned = turn_rows(
                    query_t[rows, at : at + BLOCK],
                    cosine[:, h * BLOCK : (h + 1) * BLOCK],
                    sine[:, h * BLOCK : (h + 1) * BLOCK],
                )
                to = h * width + g * BLOCK
                q_pad[s, :HEAD_DIMENSION, to : to + BLOCK] = turned.astype(jnp.bfloat16)
    top[...] = jnp.full(top.shape, MASK_FILL, jnp.float32)
    total[...] = jnp.zeros(total.shape, jnp.float32)
    acc[...] = jnp.zeros(acc.shape, jnp.float32)
    for copy in copies:
        copy.wait()

    def tile(s, start, size, kv, v_t, masked):
        cols = slice(start, start + size)
        scores = jnp.dot(kv, q_pad[s, :, cols], preferred_element_type=jnp.float32)
        if masked:
            scores = jnp.where(causal_mask(size), scores, MASK_FILL)
        before = top[s, :, cols]
        now = jnp.maximum(before, jnp.max(scores, axis=0, keepdims=True))
        probs = jnp.exp2(scores * factor - now * factor)
        shrink = jnp.exp2((before - now) * factor)
        top[s, :, cols] = now
        total[s, :, cols] = total[s, :, cols] * shrink + jnp.sum(probs, axis=0, keepdims=True)
        acc[s, :, cols] = acc[s, :, cols] * shrink + jnp.dot(
            v_t, probs.astype(jnp.bfloat16), preferred_element_type=jnp.float32
        )

    def step(block, low_mode, high_mode):
        half = jnp.where(block >= blocks // 2, 1, 0)
        for s in range(seqs):
            kv = keyval[slots[1 + block], s, half]
            v_t = kv.T[HEAD_DIMENSION:]
            for start, mode in ((0, low_mode), (width, high_mode)):
                if mode:
                    tile(s, start, width, kv, v_t, mode == "diagonal")

    @pl.loop(0, low)
    def _(block):
        step(block, "full", "full")

    step(low, "diagonal", "full")

    @pl.loop(low + 1, high)
    def _(block):
        step(block, None, "full")

    step(high, None, "diagonal")

    for s in range(seqs):
        attended = acc[s] / total[s]
        out_full[s] = attended
        out_lse[s] = top[s] * factor + jnp.log2(total[s])
        for h in range(2):
            at = (s * 2 + h) * BLOCK
            parts = [attended[:, h * width + g * BLOCK : h * width + (g + 1) * BLOCK] for g in range(heads)]
            out_rows[at : at + BLOCK] = jnp.concatenate(parts, axis=0).T.astype(jnp.bfloat16)


def start_copies(pieces, keyval, arrived):
    copies = [
        pltpu.make_async_copy(piece, keyval.at[i], arrived.at[i]) for i, piece in enumerate(pieces)
    ]
    for copy in copies:
        copy.start()
    return copies


def attention_forward(slots, query_t, cosine, sine, pieces):
    seqs = pieces[0].shape[0]
    heads = query_t.shape[0] // HEAD_DIMENSION
    cols = 2 * heads * BLOCK
    rows = query_t.shape[1]
    vmem = pl.BlockSpec(memory_space=pltpu.VMEM)
    return pl.pallas_call(
        forward_kernel,
        name="attention_forward",
        out_shape=(
            jax.ShapeDtypeStruct((rows, heads * HEAD_DIMENSION), jnp.bfloat16),
            jax.ShapeDtypeStruct((seqs, HEAD_DIMENSION, cols), jnp.float32),
            jax.ShapeDtypeStruct((seqs, 1, cols), jnp.float32),
            jax.ShapeDtypeStruct((seqs, 2 * HEAD_DIMENSION, cols), jnp.bfloat16),
        ),
        in_specs=[pl.BlockSpec(memory_space=pltpu.SMEM)]
        + [vmem] * 3
        + [pl.BlockSpec(memory_space=pl.ANY)] * len(pieces),
        out_specs=(vmem,) * 4,
        scratch_shapes=[
            pltpu.VMEM((len(pieces),) + pieces[0].shape, jnp.bfloat16),
            pltpu.SemaphoreType.DMA((len(pieces),)),
            pltpu.VMEM((seqs, 1, cols), jnp.float32),
            pltpu.VMEM((seqs, 1, cols), jnp.float32),
            pltpu.VMEM((seqs, HEAD_DIMENSION, cols), jnp.float32),
        ],
        compiler_params=pltpu.CompilerParams(vmem_limit_bytes=VMEM_LIMIT),
        cost_estimate=pl.CostEstimate(flops=6 * 10**9, bytes_accessed=8 * 2**20, transcendentals=9 * 10**6),
    )(slots, query_t, cosine, sine, *pieces)


def backward_kernel(slots, grad_rows, cosine, sine, q_pad, out_full, lse, *refs):
    count = (len(refs) - 10) // 2
    pieces, (grad_query_t, *out_pieces) = refs[:count], refs[count : 2 * count + 1]
    keyval, arrived, grad_keyval, left, d_pad, q_rows, d_rows, centre, acc = refs[2 * count + 1 :]
    copies = start_copies(pieces, keyval, arrived)
    seqs = keyval.shape[1]
    heads = grad_rows.shape[1] // HEAD_DIMENSION
    width = heads * BLOCK
    blocks = 2 * keyval.shape[0]
    factor = SCORE_SCALE * LOG2E
    low, high = slots[0], blocks - 1 - slots[0]

    for s in range(seqs):
        d_pad[s, :HEAD_DIMENSION, :] = jnp.zeros((HEAD_DIMENSION, 2 * width), jnp.bfloat16)
        for h in range(2):
            at = (s * 2 + h) * BLOCK
            turned = grad_rows[at : at + BLOCK].T
            for g in range(heads):
                to = h * width + g * BLOCK
                d_pad[s, HEAD_DIMENSION:, to : to + BLOCK] = turned[
                    g * HEAD_DIMENSION : (g + 1) * HEAD_DIMENSION
                ]
        centre[s] = jnp.sum(
            d_pad[s, HEAD_DIMENSION:].astype(jnp.float32) * out_full[s], axis=0, keepdims=True
        )
        for to in range(0, 2 * width, BLOCK):
            q_rows[s, to : to + BLOCK, :] = q_pad[s, :, to : to + BLOCK].T
            d_rows[s, to : to + BLOCK, :] = d_pad[s, :, to : to + BLOCK].T
    acc[...] = jnp.zeros(acc.shape, jnp.float32)
    for copy in copies:
        copy.wait()

    def tile(s, start, size, kv, k_t, masked):
        cols = slice(start, start + size)
        scores = jnp.dot(kv, q_pad[s, :, cols], preferred_element_type=jnp.float32)
        probs = jnp.exp2(scores * factor - lse[s, :, cols])
        if masked:
            probs = jnp.where(causal_mask(size), probs, 0.0)
        grad_probs = jnp.dot(kv, d_pad[s, :, cols], preferred_element_type=jnp.float32)
        grad_scores = (probs * (grad_probs - centre[s, :, cols])).astype(jnp.bfloat16)
        acc[s, :, cols] = acc[s, :, cols] + jnp.dot(
            k_t, grad_scores, preferred_element_type=jnp.float32
        )
        return (
            jnp.dot(grad_scores, q_rows[s, cols], preferred_element_type=jnp.float32) * SCORE_SCALE
            + jnp.dot(probs.astype(jnp.bfloat16), d_rows[s, cols], preferred_element_type=jnp.float32)
        )

    def step(block, low_mode, high_mode):
        half = jnp.where(block >= blocks // 2, 1, 0)
        device = slots[1 + block]
        for s in range(seqs):
            kv = keyval[device, s, half]
            k_t = kv.T[:HEAD_DIMENSION]
            summed = None
            for start, mode in ((0, low_mode), (width, high_mode)):
                if mode:
                    part = tile(s, start, width, kv, k_t, mode == "diagonal")
                    summed = part if summed is None else summed + part
            if summed is None:
                summed = jnp.zeros((BLOCK, 2 * HEAD_DIMENSION), jnp.float32)
            grad_keyval[device, s, half] = summed.astype(jnp.bfloat16)

    @pl.loop(0, low)
    def _(block):
        step(block, "full", "full")

    step(low, "diagonal", "full")

    @pl.loop(low + 1, high)
    def _(block):
        step(block, None, "full")

    step(high, None, "diagonal")

    @pl.loop(high + 1, blocks)
    def _(block):
        step(block, None, None)

    copies = [
        pltpu.make_async_copy(grad_keyval.at[i], piece, left.at[i]) for i, piece in enumerate(out_pieces)
    ]
    for copy in copies:
        copy.start()
    for s in range(seqs):
        for h in range(2):
            for g in range(heads):
                to = h * width + g * BLOCK
                at = (s * 2 + h) * BLOCK
                turned = turn_rows(
                    acc[s, :, to : to + BLOCK] * SCORE_SCALE,
                    cosine[:, h * BLOCK : (h + 1) * BLOCK],
                    -sine[:, h * BLOCK : (h + 1) * BLOCK],
                )
                grad_query_t[g * HEAD_DIMENSION : (g + 1) * HEAD_DIMENSION, at : at + BLOCK] = (
                    turned.astype(jnp.bfloat16)
                )
    for copy in copies:
        copy.wait()


def attention_backward(slots, grad_rows, cosine, sine, pieces, q_pad, out_full, lse):
    seqs = pieces[0].shape[0]
    cols = q_pad.shape[2]
    count = len(pieces)
    vmem = pl.BlockSpec(memory_space=pltpu.VMEM)
    where = pl.BlockSpec(memory_space=pl.ANY)
    return pl.pallas_call(
        backward_kernel,
        name="attention_backward",
        out_shape=[jax.ShapeDtypeStruct(grad_rows.shape[::-1], jnp.bfloat16)]
        + [jax.ShapeDtypeStruct(pieces[0].shape, jnp.bfloat16)] * count,
        in_specs=[pl.BlockSpec(memory_space=pltpu.SMEM)] + [vmem] * 6 + [where] * count,
        out_specs=[vmem] + [where] * count,
        scratch_shapes=[
            pltpu.VMEM((count,) + pieces[0].shape, jnp.bfloat16),
            pltpu.SemaphoreType.DMA((count,)),
            pltpu.VMEM((count,) + pieces[0].shape, jnp.bfloat16),
            pltpu.SemaphoreType.DMA((count,)),
            pltpu.VMEM((seqs, 2 * HEAD_DIMENSION, cols), jnp.bfloat16),
            pltpu.VMEM((seqs, cols, 2 * HEAD_DIMENSION), jnp.bfloat16),
            pltpu.VMEM((seqs, cols, 2 * HEAD_DIMENSION), jnp.bfloat16),
            pltpu.VMEM((seqs, 1, cols), jnp.float32),
            pltpu.VMEM((seqs, HEAD_DIMENSION, cols), jnp.float32),
        ],
        compiler_params=pltpu.CompilerParams(vmem_limit_bytes=VMEM_LIMIT),
        cost_estimate=pl.CostEstimate(flops=20 * 10**9, bytes_accessed=12 * 2**20, transcendentals=9 * 10**6),
    )(slots, grad_rows, cosine, sine, q_pad, out_full, lse, *pieces)


CONTRACT_LAST = (((1,), (1,)), ((), ()))


def select_rows(place, tile_slots):
    slot_at = lax.broadcasted_iota(jnp.int32, (tile_slots, place.shape[1]), 0)
    return slot_at == place


def expert_kernel(moe, carried, place, gates, w_in, w_out, kept_in, kept_act, kept_grad, kept_gu, out, back):
    expert = pl.program_id(0)
    tiles, tile_tokens, width = moe.shape
    experts = place.shape[0]
    slots = kept_in.shape[1] // tiles

    x_tiles, g_tiles = [], []
    for j in range(tiles):
        hit = select_rows(place[expert, j], slots)
        pick = jnp.where(hit, 1.0, 0.0).astype(jnp.bfloat16)
        weight = jnp.sum(jnp.where(hit, gates[expert, j], 0.0), axis=1, keepdims=True)
        rows = jnp.dot(pick, moe[j], preferred_element_type=jnp.float32).astype(jnp.bfloat16)
        kept_in[0, j * slots : (j + 1) * slots, :] = rows
        pair = [carried[2 * j + i, : tile_tokens // 2] for i in range(2)]
        rows = jnp.dot(pick, jnp.concatenate(pair, axis=0), preferred_element_type=jnp.float32)
        kept_grad[0, j * slots : (j + 1) * slots, :] = (rows * weight).astype(jnp.bfloat16)
    hidden = w_out.shape[1]
    gate_up = jnp.dot(kept_in[0], w_in[0], preferred_element_type=jnp.float32)
    grad_act = lax.dot_general(
        kept_grad[0], w_out[0], CONTRACT_LAST, preferred_element_type=jnp.float32
    )
    gate, up = gate_up[:, :hidden], gate_up[:, hidden:]
    sigmoid = 1.0 / (1.0 + jnp.exp(-gate))
    silu = gate * sigmoid
    kept_act[0] = (silu * up).astype(jnp.bfloat16)
    kept_gu[0, :, :hidden] = (grad_act * up * (sigmoid * (1.0 + gate * (1.0 - sigmoid)))).astype(jnp.bfloat16)
    kept_gu[0, :, hidden:] = (grad_act * silu).astype(jnp.bfloat16)
    grad_rows = lax.dot_general(
        kept_gu[0], w_in[0], CONTRACT_LAST, preferred_element_type=jnp.float32
    ).astype(jnp.bfloat16)
    for j in range(tiles):
        back[expert, j] = grad_rows[j * slots : (j + 1) * slots]

    @pl.when(expert == experts - 1)
    def _():
        for j in range(tiles):
            scatter_rows(place, [back[e, j] for e in range(experts)], j, slots, out)


def scatter_rows(place, rows, j, slots, out):
    picks = [
        jnp.where(select_rows(place[e, j], slots), 1.0, 0.0) for e in range(len(rows))
    ]
    pick = jnp.concatenate(picks, axis=0).T.astype(jnp.bfloat16)
    stacked = jnp.concatenate(rows, axis=0)
    out[j] = jnp.dot(pick, stacked, preferred_element_type=jnp.float32).astype(jnp.bfloat16)


def expert_pass(moe, carried, place, gates, w_in, w_out):
    tiles, tile_tokens, width = moe.shape
    experts, _, hidden2 = w_in.shape
    hidden = hidden2 // 2
    slots = CAP * tile_tokens // 128
    rows = tiles * slots
    whole = pl.BlockSpec(memory_space=pltpu.VMEM)
    each = lambda shape: pl.BlockSpec((1,) + shape, lambda e: (e, 0, 0))
    return pl.pallas_call(
        expert_kernel,
        name="expert_pass",
        grid=(experts,),
        out_shape=(
            jax.ShapeDtypeStruct((experts, rows, width), jnp.bfloat16),
            jax.ShapeDtypeStruct((experts, rows, hidden), jnp.bfloat16),
            jax.ShapeDtypeStruct((experts, rows, width), jnp.bfloat16),
            jax.ShapeDtypeStruct((experts, rows, hidden2), jnp.bfloat16),
            jax.ShapeDtypeStruct(moe.shape, jnp.bfloat16),
        ),
        in_specs=[whole] * 4 + [each((width, hidden2)), each((hidden, width))],
        out_specs=(
            each((rows, width)),
            each((rows, hidden)),
            each((rows, width)),
            each((rows, hidden2)),
            whole,
        ),
        scratch_shapes=[pltpu.VMEM((experts, tiles, slots, width), jnp.bfloat16)],
        compiler_params=pltpu.CompilerParams(vmem_limit_bytes=VMEM_LIMIT),
        cost_estimate=pl.CostEstimate(flops=12 * 10**9, bytes_accessed=28 * 2**20, transcendentals=10**6),
    )(moe, carried, place, gates, w_in, w_out)


def weight_kernel(own_z, place, gates, kept_in, kept_act, kept_grad, kept_gu, w_out, out, grads, back):
    expert = pl.program_id(0)
    experts, tiles = place.shape[:2]
    slots = kept_in.shape[1] // tiles
    made = jnp.dot(kept_act[0], w_out[0], preferred_element_type=jnp.float32)
    for j in range(tiles):
        hit = select_rows(place[expert, j], slots)
        weight = jnp.sum(jnp.where(hit, gates[expert, j], 0.0), axis=1, keepdims=True)
        back[expert, j] = (made[j * slots : (j + 1) * slots] * weight).astype(jnp.bfloat16)
    line, _, _, _, width = grads.shape
    in_rows, hidden = kept_in.shape[2] // (2 * line), kept_act.shape[2]
    grad_in = jnp.dot(kept_in[0].T, kept_gu[0], preferred_element_type=jnp.float32)
    grad_in = grad_in.astype(jnp.bfloat16).reshape(2, line, in_rows, width)
    grad_out = jnp.dot(kept_act[0].T, kept_grad[0], preferred_element_type=jnp.float32)
    grad_out = grad_out.astype(jnp.bfloat16).reshape(2, line, hidden // (2 * line), width)
    for z in range(2):
        away = own_z[0] ^ z
        grads[:, away, 0, :in_rows] = grad_in[z]
        grads[:, away, 0, in_rows:] = grad_out[z]

    @pl.when(expert == experts - 1)
    def _():
        for j in range(tiles):
            scatter_rows(place, [back[e, j] for e in range(experts)], j, slots, out)


def weight_pass(own_z, place, gates, kept_in, kept_act, kept_grad, kept_gu, w_out, shares):
    experts, hidden, width = w_out.shape
    tiles = place.shape[1]
    tile_tokens = place.shape[3]
    rows = kept_in.shape[1]
    whole = pl.BlockSpec(memory_space=pltpu.VMEM)
    each = lambda shape: pl.BlockSpec((1,) + shape, lambda e: (e, 0, 0))
    return pl.pallas_call(
        weight_kernel,
        name="weight_pass",
        grid=(experts,),
        out_shape=(
            jax.ShapeDtypeStruct((tiles, tile_tokens, width), jnp.bfloat16),
            jax.ShapeDtypeStruct((shares // 2, 2, experts, (width + hidden) // shares, width), jnp.bfloat16),
        ),
        in_specs=[pl.BlockSpec(memory_space=pltpu.SMEM)]
        + [whole] * 2
        + [each((rows, width)), each((rows, hidden)), each((rows, width)), each((rows, 2 * hidden)), each((hidden, width))],
        out_specs=(
            whole,
            pl.BlockSpec((shares // 2, 2, 1, (width + hidden) // shares, width), lambda e: (0, 0, e, 0, 0)),
        ),
        scratch_shapes=[pltpu.VMEM((experts, tiles, rows // tiles, width), jnp.bfloat16)],
        compiler_params=pltpu.CompilerParams(vmem_limit_bytes=VMEM_LIMIT),
        cost_estimate=pl.CostEstimate(flops=8 * 10**9, bytes_accessed=28 * 2**20, transcendentals=0),
    )(own_z, place, gates, kept_in, kept_act, kept_grad, kept_gu, w_out)

EXPERTS = 32
TOP = 8
SEQUENCE_COUNT = 2
NORM_EPS = 1e-06
ROPE_BASE = 10000.0
META_ROWS = 16

SWAP_CORE = [(c, c ^ 1) for c in range(16)]
SWAP_Z = [(c, c ^ 8) for c in range(16)]
SAME_Z = [list(range(8)), list(range(8, 16))]


def shift_x(step):
    return [(c, ((c // 8) * 4 + (c // 2 % 4 + step) % 4) * 2 + c % 2) for c in range(16)]


def up(values):
    return lax.ppermute(values, "ctx", shift_x(1))


def down(values):
    return lax.ppermute(values, "ctx", shift_x(-1))


def swap_core(values):
    return lax.ppermute(values, "ctx", SWAP_CORE)


def swap_z(values):
    return lax.ppermute(values, "ctx", SWAP_Z)


def wide(values):
    return values.astype(jnp.float32)


def low(values):
    return values.astype(jnp.bfloat16)


def exchange(values, axis):
    return lax.all_to_all(values, axis, split_axis=0, concat_axis=0, tiled=True)


def gather_ep(own):
    return exchange(jnp.broadcast_to(own[None], (lax.axis_size("ep"),) + own.shape), "ep")


def gather_ctx(own):
    z = swap_z(own)
    left, right = up(own), down(own)
    z_left, z_right = up(z), down(z)
    far, z_far = up(left), down(z_right)
    near = [own, z, right, z_right, far, z_far, left, z_left]
    return near + [swap_core(block) for block in near]


def scatter_ctx(parts):
    sums = {}
    for k in (4, 5, 3, 6, 2, 7, 1, 0):
        sums[k] = wide(parts[k]) + wide(swap_core(parts[8 + k]))
    far, z_far = up(low(sums[4])), down(low(sums[5]))
    z_right, left = up(low(sums[3])), down(low(sums[6]))
    right, z_left = up(low(sums[2] + wide(far))), down(low(sums[7] + wide(z_far)))
    own = sums[0] + wide(right) + wide(left)
    z = sums[1] + wide(z_right) + wide(z_left)
    return own + wide(swap_z(low(z)))


def two_terms(values):
    high = low(values)
    return jnp.stack([high, low(values - wide(high))])


def turn_lanes(u, cosine, sine):
    half = HEAD_DIMENSION // 2
    u1, u2 = u[:, :half], u[:, half:]
    return jnp.concatenate([u1 * cosine - u2 * sine, u2 * cosine + u1 * sine], axis=-1)


def body(
    layer_in,
    pair_of,
    routes,
    gate_weights,
    capacity,
    attn_gain,
    query_weight,
    key_value_weight,
    output_weight,
    moe_gain,
    expert_in,
    expert_out,
    out_grad,
):
    tok_rows, width = layer_in.shape
    ep_count = lax.axis_size("ep")
    ctx_count = lax.axis_size("ctx")
    ctx_rows = tok_rows * ep_count
    f32, bf16 = jnp.float32, jnp.bfloat16
    ctx_index = lax.axis_index("ctx")
    ep_index = lax.axis_index("ep")
    head_cols = query_weight.shape[1]
    flat_keyval = key_value_weight.reshape(width, 2 * HEAD_DIMENSION)

    device_ids = jnp.arange(ctx_count, dtype=jnp.int32)
    own_pair = jnp.sum(jnp.where(device_ids == ctx_index, pair_of, 0))
    holder = jnp.sum(jnp.where(pair_of[:, None] == device_ids[None, :], device_ids[:, None], 0), axis=0)
    holder = jnp.concatenate([holder, holder[::-1]])
    relative = (
        ((holder % 2) ^ (ctx_index % 2)) * 8
        + ((holder // 2 % 4 - ctx_index // 2 % 4) % 4) * 2
        + ((holder // 8) ^ (ctx_index // 8))
    )
    slots = jnp.concatenate([own_pair[None], relative]).astype(jnp.int32)
    starts = jnp.stack([own_pair, 2 * ctx_count - 1 - own_pair]) * BLOCK
    own_pos = (starts[:, None] + jnp.arange(BLOCK, dtype=jnp.int32)[None, :]).reshape(2 * BLOCK)
    freqs = ROPE_BASE ** (-2.0 * jnp.arange(HEAD_DIMENSION // 2, dtype=f32) / HEAD_DIMENSION)
    angles = freqs[:, None] * own_pos.astype(f32)[None, :]
    cosine, sine = jnp.cos(angles), jnp.sin(angles)
    cosine_rows = jnp.tile(cosine.T, (SEQUENCE_COUNT, 1))
    sine_rows = jnp.tile(sine.T, (SEQUENCE_COUNT, 1))

    x_float = layer_in.astype(f32)
    rms_attn = lax.rsqrt(jnp.mean(x_float * x_float, axis=-1, keepdims=True) + NORM_EPS)
    normed = gather_ep((x_float * rms_attn * attn_gain).astype(bf16)).reshape(ctx_rows, width)
    query_t = jnp.einsum("dq,rd->qr", query_weight, normed, preferred_element_type=f32)
    keyval = jnp.dot(normed, flat_keyval, preferred_element_type=f32)
    key = turn_lanes(keyval[:, :HEAD_DIMENSION], cosine_rows, sine_rows)
    keyval_low = jnp.concatenate([key, keyval[:, HEAD_DIMENSION:]], axis=-1).astype(bf16)

    expert_ids = jnp.arange(EXPERTS, dtype=jnp.int32)
    named = routes[:, :, None] == expert_ids
    member = jnp.sum(named.astype(f32), axis=1)
    before = jnp.tril(jnp.ones((tok_rows, tok_rows), bf16), -1)
    rank = jnp.dot(before, member.astype(bf16), preferred_element_type=f32)
    kept = (member > 0) & (rank < capacity.astype(f32)[None, :])
    place = jnp.where(kept, rank, -1.0).T
    gates = jnp.sum(jnp.where(named, gate_weights[:, :, None], 0.0), axis=1).T
    gates_high = gates.astype(bf16)
    gates_low = (gates - gates_high.astype(f32)).astype(bf16)
    meta = jnp.stack([place.astype(bf16), gates_high, gates_low]).reshape(-1, width)
    meta = jnp.pad(meta, ((0, META_ROWS - meta.shape[0]), (0, 0)))
    carried = jnp.concatenate([out_grad, meta], axis=0)

    keyval_low, projection = lax.optimization_barrier((keyval_low, output_weight))
    projection = lax.all_gather(projection, "ep", axis=0, tiled=True)
    pieces = gather_ctx(keyval_low.reshape(SEQUENCE_COUNT, 2, BLOCK, 2 * HEAD_DIMENSION))
    pieces[-1], carried = lax.optimization_barrier((pieces[-1], carried))
    carried_all = gather_ep(carried)
    attended, attended_full, lse, query_pad = attention_forward(slots, query_t, cosine, sine, pieces)

    merged = exchange(attended.reshape(ep_count, tok_rows, head_cols), "ep")
    merged = merged.transpose(1, 0, 2).reshape(tok_rows, ep_count * head_cols)
    residual = x_float + jnp.dot(merged, projection, preferred_element_type=f32)
    rms_moe = lax.rsqrt(jnp.mean(residual * residual, axis=-1, keepdims=True) + NORM_EPS)
    moe_in = gather_ep((residual * rms_moe * moe_gain).astype(bf16))

    tiles = ep_count // 2
    tile_tokens = 2 * tok_rows
    local_experts = expert_in.shape[0]
    meta_all = carried_all[:, tok_rows : tok_rows + 3 * EXPERTS * tok_rows // width]
    meta_all = meta_all.reshape(tiles, 2, 3, EXPERTS, tok_rows)
    meta_all = wide(lax.dynamic_slice_in_dim(meta_all, ep_index * local_experts, local_experts, axis=3))
    place_all = meta_all[:, :, 0].astype(jnp.int32)
    place_all = jnp.where(place_all >= 0, place_all + jnp.arange(2, dtype=jnp.int32)[None, :, None, None] * CAP, -1)
    gates_all = meta_all[:, :, 1] + meta_all[:, :, 2]
    by_expert = lambda v: v.transpose(2, 0, 1, 3).reshape(local_experts, tiles, 1, tile_tokens)
    place_all, gates_all = by_expert(place_all), by_expert(gates_all)
    kept_in, kept_act, kept_grad, kept_gu, grad_moe = expert_pass(
        moe_in.reshape(tiles, tile_tokens, width), carried_all, place_all, gates_all, expert_in, expert_out
    )
    grad_moe_in = jnp.sum(wide(exchange(grad_moe.reshape(ep_count, tok_rows, width), "ep")), axis=0)
    made, expert_grads = weight_pass(
        (ctx_index // 8)[None].astype(jnp.int32), place_all, gates_all, kept_in, kept_act, kept_grad, kept_gu, expert_out, ctx_count
    )

    grad_top = out_grad.astype(f32)
    scaled = grad_moe_in * moe_gain
    moe_gain_part = jnp.sum(grad_moe_in * residual * rms_moe, axis=0)
    inner = jnp.mean(scaled * residual, axis=-1, keepdims=True)
    grad_res = grad_top + rms_moe * scaled - residual * (rms_moe * rms_moe * rms_moe) * inner
    grad_attn = grad_res.astype(bf16)

    grad_att = lax.dot_general(
        grad_attn, projection, (((1,), (1,)), ((), ())), preferred_element_type=f32
    ).astype(bf16)
    grad_att = grad_att.reshape(tok_rows, ep_count, head_cols).transpose(1, 0, 2)
    grad_att = exchange(grad_att, "ep").reshape(ctx_rows, head_cols)
    output_grad = lax.dot_general(
        merged, grad_attn, (((0,), (0,)), ((), ())), preferred_element_type=f32
    ).astype(bf16)
    made, grad_att = lax.optimization_barrier((made, grad_att))
    made = jnp.sum(wide(exchange(made.reshape(ep_count, tok_rows, width), "ep")), axis=0)
    layer_out = (residual + made).astype(bf16)
    grad_query_t, *grad_pieces = attention_backward(
        slots, grad_att, cosine, sine, pieces, query_pad, attended_full, lse
    )
    output_grad, grad_query_t = lax.optimization_barrier((output_grad, grad_query_t))
    output_grad = jnp.sum(wide(exchange(output_grad.reshape(ep_count, head_cols, width), "ep")), axis=0)
    from_query = jnp.einsum("qr,dq->rd", grad_query_t, query_weight, preferred_element_type=f32)
    grad_keyval = scatter_ctx(grad_pieces).reshape(ctx_rows, 2 * HEAD_DIMENSION)
    expert_grads = lax.psum_scatter(
        expert_grads, "ctx", scatter_dimension=0, tiled=True, axis_index_groups=SAME_Z
    )[0]
    grad_keyval, expert_grads = lax.optimization_barrier((grad_keyval, expert_grads))
    grad_key = turn_lanes(grad_keyval[:, :HEAD_DIMENSION], cosine_rows, -sine_rows)
    grad_kv_low = jnp.concatenate([grad_key, grad_keyval[:, HEAD_DIMENSION:]], axis=-1).astype(bf16)
    from_keyval = jnp.einsum("rk,dk->rd", grad_kv_low, flat_keyval, preferred_element_type=f32)
    grad_normed = (from_query + from_keyval).astype(bf16).reshape(ep_count, tok_rows, width)
    grad_normed = jnp.sum(wide(exchange(grad_normed, "ep")), axis=0)
    scaled = grad_normed * attn_gain
    inner = jnp.mean(scaled * x_float, axis=-1, keepdims=True)
    input_grad = grad_res + rms_attn * scaled - x_float * (rms_attn * rms_attn * rms_attn) * inner

    query_grad = jnp.einsum("rd,qr->dq", normed, grad_query_t, preferred_element_type=f32)
    keyval_grad = jnp.einsum("rd,rk->dk", normed, grad_kv_low, preferred_element_type=f32)
    attn_gain_part = (
        jnp.sum(query_weight.astype(f32) * query_grad, axis=1)
        + jnp.sum(flat_keyval.astype(f32) * keyval_grad, axis=1)
    ) / attn_gain
    gains = two_terms(jnp.stack([attn_gain_part, moe_gain_part])).reshape(-1, head_cols)
    small = jnp.stack([low(query_grad), low(keyval_grad), low(output_grad).T])
    small = small.reshape(3, ctx_count, -1, head_cols).transpose(1, 0, 2, 3).reshape(ctx_count, -1, head_cols)
    in_rows = width // ctx_count
    small = jnp.concatenate([small, jnp.broadcast_to(gains[None], (ctx_count,) + gains.shape)], axis=1)
    small = jnp.sum(wide(exchange(small, "ctx")), axis=0)
    gains = small[3 * in_rows :].reshape(2, 2, width)
    gains = two_terms(gains[0] + gains[1]).reshape(4, width)
    gains = jnp.sum(wide(gather_ep(gains)), axis=0)
    gains = gains[:2] + gains[2:]
    small = small[: 3 * in_rows].reshape(3, in_rows, head_cols)
    expert_grads = wide(expert_grads[0]) + wide(swap_z(expert_grads[1]))
    return (
        layer_out,
        input_grad,
        gains[0],
        small[0],
        small[1].reshape(in_rows, 1, 2 * HEAD_DIMENSION),
        small[2].T,
        gains[1],
        expert_grads[:, :in_rows],
        expert_grads[:, in_rows:],
    )


def solution(mesh):
    in_specs = (
        P(("ctx", "ep"), None),
        P(),
        P(("ctx", "ep"), None),
        P(("ctx", "ep"), None),
        P(),
        P(),
        P(None, "ep"),
        P(None, "ep", None),
        P("ep", None),
        P(),
        P("ep", None, None),
        P("ep", None, None),
        P(("ctx", "ep"), None),
    )
    out_specs = (
        P(("ctx", "ep"), None),
        P(("ctx", "ep"), None),
        P(),
        P("ctx", "ep"),
        P("ctx", "ep", None),
        P("ep", "ctx"),
        P(),
        P("ep", "ctx", None),
        P("ep", "ctx", None),
    )
    return jax.shard_map(body, mesh=mesh, in_specs=in_specs, out_specs=out_specs, check_vma=False)
```

```python
import functools

import jax
import jax.numpy as jnp
from jax import lax
from jax.experimental import pallas as pl
from jax.experimental.pallas import tpu as pltpu
from jax.sharding import PartitionSpec as P

VMEM_LIMIT = 56 * 1024 * 1024
CAP = 48

HEAD_DIMENSION = 64
SCORE_SCALE = 1.0 / 64.0
MASK_FILL = -1e30
LOG2E = 1.4426950408889634
BLOCK = 256


def causal_mask(width):
    key_at = lax.broadcasted_iota(jnp.int32, (BLOCK, width), 0)
    query_at = lax.broadcasted_iota(jnp.int32, (BLOCK, width), 1) % BLOCK
    return key_at <= query_at


def turn_rows(u, cosine, sine):
    half = HEAD_DIMENSION // 2
    u1, u2 = u[:half], u[half:]
    return jnp.concatenate([u1 * cosine - u2 * sine, u2 * cosine + u1 * sine], axis=0)


def forward_kernel(slots, query_t, cosine, sine, *refs):
    pieces, (out_rows, out_full, out_lse, q_pad, keyval, arrived, top, total, acc) = refs[:-9], refs[-9:]
    copies = start_copies(pieces, keyval, arrived)
    seqs = keyval.shape[1]
    heads = query_t.shape[0] // HEAD_DIMENSION
    width = heads * BLOCK
    blocks = 2 * keyval.shape[0]
    factor = SCORE_SCALE * LOG2E
    low, high = slots[0], blocks - 1 - slots[0]

    for s in range(seqs):
        q_pad[s, HEAD_DIMENSION:, :] = jnp.zeros((HEAD_DIMENSION, 2 * width), jnp.bfloat16)
        for h in range(2):
            for g in range(heads):
                rows = slice(g * HEAD_DIMENSION, (g + 1) * HEAD_DIMENSION)
                at = (s * 2 + h) * BLOCK
                turned = turn_rows(
                    query_t[rows, at : at + BLOCK],
                    cosine[:, h * BLOCK : (h + 1) * BLOCK],
                    sine[:, h * BLOCK : (h + 1) * BLOCK],
                )
                to = h * width + g * BLOCK
                q_pad[s, :HEAD_DIMENSION, to : to + BLOCK] = turned.astype(jnp.bfloat16)
    top[...] = jnp.full(top.shape, MASK_FILL, jnp.float32)
    total[...] = jnp.zeros(total.shape, jnp.float32)
    acc[...] = jnp.zeros(acc.shape, jnp.float32)
    for copy in copies:
        copy.wait()

    def tile(s, start, size, kv, v_t, masked):
        cols = slice(start, start + size)
        scores = jnp.dot(kv, q_pad[s, :, cols], preferred_element_type=jnp.float32)
        if masked:
            scores = jnp.where(causal_mask(size), scores, MASK_FILL)
        before = top[s, :, cols]
        now = jnp.maximum(before, jnp.max(scores, axis=0, keepdims=True))
        probs = jnp.exp2(scores * factor - now * factor)
        shrink = jnp.exp2((before - now) * factor)
        top[s, :, cols] = now
        total[s, :, cols] = total[s, :, cols] * shrink + jnp.sum(probs, axis=0, keepdims=True)
        acc[s, :, cols] = acc[s, :, cols] * shrink + jnp.dot(
            v_t, probs.astype(jnp.bfloat16), preferred_element_type=jnp.float32
        )

    def step(block, low_mode, high_mode):
        half = jnp.where(block >= blocks // 2, 1, 0)
        for s in range(seqs):
            kv = keyval[slots[1 + block], s, half]
            v_t = kv.T[HEAD_DIMENSION:]
            for start, mode in ((0, low_mode), (width, high_mode)):
                if mode:
                    tile(s, start, width, kv, v_t, mode == "diagonal")

    @pl.loop(0, low)
    def _(block):
        step(block, "full", "full")

    step(low, "diagonal", "full")

    @pl.loop(low + 1, high)
    def _(block):
        step(block, None, "full")

    step(high, None, "diagonal")

    for s in range(seqs):
        attended = acc[s] / total[s]
        out_full[s] = attended
        out_lse[s] = top[s] * factor + jnp.log2(total[s])
        for h in range(2):
            at = (s * 2 + h) * BLOCK
            parts = [attended[:, h * width + g * BLOCK : h * width + (g + 1) * BLOCK] for g in range(heads)]
            out_rows[at : at + BLOCK] = jnp.concatenate(parts, axis=0).T.astype(jnp.bfloat16)


def start_copies(pieces, keyval, arrived):
    copies = [
        pltpu.make_async_copy(piece, keyval.at[i], arrived.at[i]) for i, piece in enumerate(pieces)
    ]
    for copy in copies:
        copy.start()
    return copies


def attention_forward(slots, query_t, cosine, sine, pieces):
    seqs = pieces[0].shape[0]
    heads = query_t.shape[0] // HEAD_DIMENSION
    cols = 2 * heads * BLOCK
    rows = query_t.shape[1]
    vmem = pl.BlockSpec(memory_space=pltpu.VMEM)
    return pl.pallas_call(
        forward_kernel,
        name="attention_forward",
        out_shape=(
            jax.ShapeDtypeStruct((rows, heads * HEAD_DIMENSION), jnp.bfloat16),
            jax.ShapeDtypeStruct((seqs, HEAD_DIMENSION, cols), jnp.float32),
            jax.ShapeDtypeStruct((seqs, 1, cols), jnp.float32),
            jax.ShapeDtypeStruct((seqs, 2 * HEAD_DIMENSION, cols), jnp.bfloat16),
        ),
        in_specs=[pl.BlockSpec(memory_space=pltpu.SMEM)]
        + [vmem] * 3
        + [pl.BlockSpec(memory_space=pl.ANY)] * len(pieces),
        out_specs=(vmem,) * 4,
        scratch_shapes=[
            pltpu.VMEM((len(pieces),) + pieces[0].shape, jnp.bfloat16),
            pltpu.SemaphoreType.DMA((len(pieces),)),
            pltpu.VMEM((seqs, 1, cols), jnp.float32),
            pltpu.VMEM((seqs, 1, cols), jnp.float32),
            pltpu.VMEM((seqs, HEAD_DIMENSION, cols), jnp.float32),
        ],
        compiler_params=pltpu.CompilerParams(vmem_limit_bytes=VMEM_LIMIT),
        cost_estimate=pl.CostEstimate(flops=6 * 10**9, bytes_accessed=8 * 2**20, transcendentals=9 * 10**6),
    )(slots, query_t, cosine, sine, *pieces)


def backward_kernel(slots, grad_rows, cosine, sine, q_pad, out_full, lse, *refs):
    count = (len(refs) - 10) // 2
    pieces, (grad_query_t, *out_pieces) = refs[:count], refs[count : 2 * count + 1]
    keyval, arrived, grad_keyval, left, d_pad, q_rows, d_rows, centre, acc = refs[2 * count + 1 :]
    copies = start_copies(pieces, keyval, arrived)
    seqs = keyval.shape[1]
    heads = grad_rows.shape[1] // HEAD_DIMENSION
    width = heads * BLOCK
    blocks = 2 * keyval.shape[0]
    factor = SCORE_SCALE * LOG2E
    low, high = slots[0], blocks - 1 - slots[0]

    for s in range(seqs):
        d_pad[s, :HEAD_DIMENSION, :] = jnp.zeros((HEAD_DIMENSION, 2 * width), jnp.bfloat16)
        for h in range(2):
            at = (s * 2 + h) * BLOCK
            turned = grad_rows[at : at + BLOCK].T
            for g in range(heads):
                to = h * width + g * BLOCK
                d_pad[s, HEAD_DIMENSION:, to : to + BLOCK] = turned[
                    g * HEAD_DIMENSION : (g + 1) * HEAD_DIMENSION
                ]
        centre[s] = jnp.sum(
            d_pad[s, HEAD_DIMENSION:].astype(jnp.float32) * out_full[s], axis=0, keepdims=True
        )
        for to in range(0, 2 * width, BLOCK):
            q_rows[s, to : to + BLOCK, :] = q_pad[s, :, to : to + BLOCK].T
            d_rows[s, to : to + BLOCK, :] = d_pad[s, :, to : to + BLOCK].T
    acc[...] = jnp.zeros(acc.shape, jnp.float32)
    for copy in copies:
        copy.wait()

    def tile(s, start, size, kv, k_t, masked):
        cols = slice(start, start + size)
        scores = jnp.dot(kv, q_pad[s, :, cols], preferred_element_type=jnp.float32)
        probs = jnp.exp2(scores * factor - lse[s, :, cols])
        if masked:
            probs = jnp.where(causal_mask(size), probs, 0.0)
        grad_probs = jnp.dot(kv, d_pad[s, :, cols], preferred_element_type=jnp.float32)
        grad_scores = (probs * (grad_probs - centre[s, :, cols])).astype(jnp.bfloat16)
        acc[s, :, cols] = acc[s, :, cols] + jnp.dot(
            k_t, grad_scores, preferred_element_type=jnp.float32
        )
        return (
            jnp.dot(grad_scores, q_rows[s, cols], preferred_element_type=jnp.float32) * SCORE_SCALE
            + jnp.dot(probs.astype(jnp.bfloat16), d_rows[s, cols], preferred_element_type=jnp.float32)
        )

    def step(block, low_mode, high_mode):
        half = jnp.where(block >= blocks // 2, 1, 0)
        device = slots[1 + block]
        for s in range(seqs):
            kv = keyval[device, s, half]
            k_t = kv.T[:HEAD_DIMENSION]
            summed = None
            for start, mode in ((0, low_mode), (width, high_mode)):
                if mode:
                    part = tile(s, start, width, kv, k_t, mode == "diagonal")
                    summed = part if summed is None else summed + part
            if summed is None:
                summed = jnp.zeros((BLOCK, 2 * HEAD_DIMENSION), jnp.float32)
            grad_keyval[device, s, half] = summed.astype(jnp.bfloat16)

    @pl.loop(0, low)
    def _(block):
        step(block, "full", "full")

    step(low, "diagonal", "full")

    @pl.loop(low + 1, high)
    def _(block):
        step(block, None, "full")

    step(high, None, "diagonal")

    @pl.loop(high + 1, blocks)
    def _(block):
        step(block, None, None)

    copies = [
        pltpu.make_async_copy(grad_keyval.at[i], piece, left.at[i]) for i, piece in enumerate(out_pieces)
    ]
    for copy in copies:
        copy.start()
    for s in range(seqs):
        for h in range(2):
            for g in range(heads):
                to = h * width + g * BLOCK
                at = (s * 2 + h) * BLOCK
                turned = turn_rows(
                    acc[s, :, to : to + BLOCK] * SCORE_SCALE,
                    cosine[:, h * BLOCK : (h + 1) * BLOCK],
                    -sine[:, h * BLOCK : (h + 1) * BLOCK],
                )
                grad_query_t[g * HEAD_DIMENSION : (g + 1) * HEAD_DIMENSION, at : at + BLOCK] = (
                    turned.astype(jnp.bfloat16)
                )
    for copy in copies:
        copy.wait()


def attention_backward(slots, grad_rows, cosine, sine, pieces, q_pad, out_full, lse):
    seqs = pieces[0].shape[0]
    cols = q_pad.shape[2]
    count = len(pieces)
    vmem = pl.BlockSpec(memory_space=pltpu.VMEM)
    where = pl.BlockSpec(memory_space=pl.ANY)
    return pl.pallas_call(
        backward_kernel,
        name="attention_backward",
        out_shape=[jax.ShapeDtypeStruct(grad_rows.shape[::-1], jnp.bfloat16)]
        + [jax.ShapeDtypeStruct(pieces[0].shape, jnp.bfloat16)] * count,
        in_specs=[pl.BlockSpec(memory_space=pltpu.SMEM)] + [vmem] * 6 + [where] * count,
        out_specs=[vmem] + [where] * count,
        scratch_shapes=[
            pltpu.VMEM((count,) + pieces[0].shape, jnp.bfloat16),
            pltpu.SemaphoreType.DMA((count,)),
            pltpu.VMEM((count,) + pieces[0].shape, jnp.bfloat16),
            pltpu.SemaphoreType.DMA((count,)),
            pltpu.VMEM((seqs, 2 * HEAD_DIMENSION, cols), jnp.bfloat16),
            pltpu.VMEM((seqs, cols, 2 * HEAD_DIMENSION), jnp.bfloat16),
            pltpu.VMEM((seqs, cols, 2 * HEAD_DIMENSION), jnp.bfloat16),
            pltpu.VMEM((seqs, 1, cols), jnp.float32),
            pltpu.VMEM((seqs, HEAD_DIMENSION, cols), jnp.float32),
        ],
        compiler_params=pltpu.CompilerParams(vmem_limit_bytes=VMEM_LIMIT),
        cost_estimate=pl.CostEstimate(flops=20 * 10**9, bytes_accessed=12 * 2**20, transcendentals=9 * 10**6),
    )(slots, grad_rows, cosine, sine, q_pad, out_full, lse, *pieces)


CONTRACT_LAST = (((1,), (1,)), ((), ()))


def select_rows(place, tile_slots):
    slot_at = lax.broadcasted_iota(jnp.int32, (tile_slots, place.shape[1]), 0)
    return slot_at == place


def expert_kernel(grad_at, moe, carried, place, gates, w_in, w_out, kept_in, kept_act, kept_grad, kept_gu, out, back):
    expert = pl.program_id(0)
    tiles, tile_tokens, width = moe.shape
    experts = place.shape[0]
    slots = kept_in.shape[1] // tiles

    x_tiles, g_tiles = [], []
    for j in range(tiles):
        hit = select_rows(place[expert, j], slots)
        pick = jnp.where(hit, 1.0, 0.0).astype(jnp.bfloat16)
        weight = jnp.sum(jnp.where(hit, gates[expert, j], 0.0), axis=1, keepdims=True)
        rows = jnp.dot(pick, moe[j], preferred_element_type=jnp.float32).astype(jnp.bfloat16)
        kept_in[0, j * slots : (j + 1) * slots, :] = rows
        pair = [carried[2 * j + i, grad_at : grad_at + tile_tokens // 2] for i in range(2)]
        rows = jnp.dot(pick, jnp.concatenate(pair, axis=0), preferred_element_type=jnp.float32)
        kept_grad[0, j * slots : (j + 1) * slots, :] = (rows * weight).astype(jnp.bfloat16)
    hidden = w_out.shape[1]
    gate_up = jnp.dot(kept_in[0], w_in[0], preferred_element_type=jnp.float32)
    grad_act = lax.dot_general(
        kept_grad[0], w_out[0], CONTRACT_LAST, preferred_element_type=jnp.float32
    )
    gate, up = gate_up[:, :hidden], gate_up[:, hidden:]
    sigmoid = 1.0 / (1.0 + jnp.exp(-gate))
    silu = gate * sigmoid
    kept_act[0] = (silu * up).astype(jnp.bfloat16)
    kept_gu[0, :, :hidden] = (grad_act * up * (sigmoid * (1.0 + gate * (1.0 - sigmoid)))).astype(jnp.bfloat16)
    kept_gu[0, :, hidden:] = (grad_act * silu).astype(jnp.bfloat16)
    grad_rows = lax.dot_general(
        kept_gu[0], w_in[0], CONTRACT_LAST, preferred_element_type=jnp.float32
    ).astype(jnp.bfloat16)
    for j in range(tiles):
        back[expert, j] = grad_rows[j * slots : (j + 1) * slots]

    @pl.when(expert == experts - 1)
    def _():
        for j in range(tiles):
            scatter_rows(place, [back[e, j] for e in range(experts)], j, slots, out)


def scatter_rows(place, rows, j, slots, out):
    picks = [
        jnp.where(select_rows(place[e, j], slots), 1.0, 0.0) for e in range(len(rows))
    ]
    pick = jnp.concatenate(picks, axis=0).T.astype(jnp.bfloat16)
    stacked = jnp.concatenate(rows, axis=0)
    out[j] = jnp.dot(pick, stacked, preferred_element_type=jnp.float32).astype(jnp.bfloat16)


def expert_pass(grad_at, moe, carried, place, gates, w_in, w_out):
    tiles, tile_tokens, width = moe.shape
    experts, _, hidden2 = w_in.shape
    hidden = hidden2 // 2
    slots = CAP * tile_tokens // 128
    rows = tiles * slots
    whole = pl.BlockSpec(memory_space=pltpu.VMEM)
    each = lambda shape: pl.BlockSpec((1,) + shape, lambda e: (e, 0, 0))
    return pl.pallas_call(
        functools.partial(expert_kernel, grad_at),
        name="expert_pass",
        grid=(experts,),
        out_shape=(
            jax.ShapeDtypeStruct((experts, rows, width), jnp.bfloat16),
            jax.ShapeDtypeStruct((experts, rows, hidden), jnp.bfloat16),
            jax.ShapeDtypeStruct((experts, rows, width), jnp.bfloat16),
            jax.ShapeDtypeStruct((experts, rows, hidden2), jnp.bfloat16),
            jax.ShapeDtypeStruct(moe.shape, jnp.bfloat16),
        ),
        in_specs=[whole] * 4 + [each((width, hidden2)), each((hidden, width))],
        out_specs=(
            each((rows, width)),
            each((rows, hidden)),
            each((rows, width)),
            each((rows, hidden2)),
            whole,
        ),
        scratch_shapes=[pltpu.VMEM((experts, tiles, slots, width), jnp.bfloat16)],
        compiler_params=pltpu.CompilerParams(vmem_limit_bytes=VMEM_LIMIT),
        cost_estimate=pl.CostEstimate(flops=12 * 10**9, bytes_accessed=28 * 2**20, transcendentals=10**6),
    )(moe, carried, place, gates, w_in, w_out)


def weight_kernel(own_z, place, gates, kept_in, kept_act, kept_grad, kept_gu, w_out, out, grads, back):
    expert = pl.program_id(0)
    experts, tiles = place.shape[:2]
    slots = kept_in.shape[1] // tiles
    made = jnp.dot(kept_act[0], w_out[0], preferred_element_type=jnp.float32)
    for j in range(tiles):
        hit = select_rows(place[expert, j], slots)
        weight = jnp.sum(jnp.where(hit, gates[expert, j], 0.0), axis=1, keepdims=True)
        back[expert, j] = (made[j * slots : (j + 1) * slots] * weight).astype(jnp.bfloat16)
    line, _, _, _, width = grads.shape
    in_rows, hidden = kept_in.shape[2] // (2 * line), kept_act.shape[2]
    grad_in = jnp.dot(kept_in[0].T, kept_gu[0], preferred_element_type=jnp.float32)
    grad_in = grad_in.astype(jnp.bfloat16).reshape(2, line, in_rows, width)
    grad_out = jnp.dot(kept_act[0].T, kept_grad[0], preferred_element_type=jnp.float32)
    grad_out = grad_out.astype(jnp.bfloat16).reshape(2, line, hidden // (2 * line), width)
    for z in range(2):
        away = own_z[0] ^ z
        grads[:, away, 0, :in_rows] = grad_in[z]
        grads[:, away, 0, in_rows:] = grad_out[z]

    @pl.when(expert == experts - 1)
    def _():
        for j in range(tiles):
            scatter_rows(place, [back[e, j] for e in range(experts)], j, slots, out)


def weight_pass(own_z, place, gates, kept_in, kept_act, kept_grad, kept_gu, w_out, shares):
    experts, hidden, width = w_out.shape
    tiles = place.shape[1]
    tile_tokens = place.shape[3]
    rows = kept_in.shape[1]
    whole = pl.BlockSpec(memory_space=pltpu.VMEM)
    each = lambda shape: pl.BlockSpec((1,) + shape, lambda e: (e, 0, 0))
    return pl.pallas_call(
        weight_kernel,
        name="weight_pass",
        grid=(experts,),
        out_shape=(
            jax.ShapeDtypeStruct((tiles, tile_tokens, width), jnp.bfloat16),
            jax.ShapeDtypeStruct((shares // 2, 2, experts, (width + hidden) // shares, width), jnp.bfloat16),
        ),
        in_specs=[pl.BlockSpec(memory_space=pltpu.SMEM)]
        + [whole] * 2
        + [each((rows, width)), each((rows, hidden)), each((rows, width)), each((rows, 2 * hidden)), each((hidden, width))],
        out_specs=(
            whole,
            pl.BlockSpec((shares // 2, 2, 1, (width + hidden) // shares, width), lambda e: (0, 0, e, 0, 0)),
        ),
        scratch_shapes=[pltpu.VMEM((experts, tiles, rows // tiles, width), jnp.bfloat16)],
        compiler_params=pltpu.CompilerParams(vmem_limit_bytes=VMEM_LIMIT),
        cost_estimate=pl.CostEstimate(flops=8 * 10**9, bytes_accessed=28 * 2**20, transcendentals=0),
    )(own_z, place, gates, kept_in, kept_act, kept_grad, kept_gu, w_out)

EXPERTS = 32
TOP = 8
SEQUENCE_COUNT = 2
NORM_EPS = 1e-06
ROPE_BASE = 10000.0
META_ROWS = 16

SWAP_CORE = [(c, c ^ 1) for c in range(16)]
SWAP_Z = [(c, c ^ 8) for c in range(16)]
SAME_Z = [list(range(8)), list(range(8, 16))]


def shift_x(step):
    return [(c, ((c // 8) * 4 + (c // 2 % 4 + step) % 4) * 2 + c % 2) for c in range(16)]


def up(values):
    return lax.ppermute(values, "ctx", shift_x(1))


def down(values):
    return lax.ppermute(values, "ctx", shift_x(-1))


def swap_core(values):
    return lax.ppermute(values, "ctx", SWAP_CORE)


def swap_z(values):
    return lax.ppermute(values, "ctx", SWAP_Z)


def wide(values):
    return values.astype(jnp.float32)


def low(values):
    return values.astype(jnp.bfloat16)


SWAP_EP = [(e, e ^ 4) for e in range(8)]


def shift_y(step):
    return [(e, (e // 4) * 4 + (e % 4 + step) % 4) for e in range(8)]


def fold(parts, gains, axis, keep, table):
    size = parts.shape[axis]
    sent = lax.dynamic_index_in_dim(parts, 1 - keep, axis, keepdims=False)
    own = wide(lax.dynamic_index_in_dim(parts, keep, axis, keepdims=False))
    width = own.shape[-1]
    rows = own.size // width
    sent = jnp.concatenate([low(sent).reshape(rows, width), two_terms(gains).reshape(-1, width)], axis=0)
    got = wide(lax.ppermute(sent, "ctx", table))
    extra = got[rows:].reshape((2,) + gains.shape)
    return own + got[:rows].reshape(own.shape), gains + extra[0] + extra[1]


def exchange(values, axis):
    return lax.all_to_all(values, axis, split_axis=0, concat_axis=0, tiled=True)


def gather_ep(own):
    return exchange(jnp.broadcast_to(own[None], (lax.axis_size("ep"),) + own.shape), "ep")


def gather_ctx(own):
    z = swap_z(own)
    left, right = up(own), down(own)
    z_left, z_right = up(z), down(z)
    far, z_far = up(left), down(z_right)
    near = [own, z, right, z_right, far, z_far, left, z_left]
    return near + [swap_core(block) for block in near]


def scatter_ctx(parts):
    sums = {}
    for k in (4, 5, 3, 6, 2, 7, 1, 0):
        sums[k] = wide(parts[k]) + wide(swap_core(parts[8 + k]))
    far, z_far = up(low(sums[4])), down(low(sums[5]))
    z_right, left = up(low(sums[3])), down(low(sums[6]))
    right, z_left = up(low(sums[2] + wide(far))), down(low(sums[7] + wide(z_far)))
    own = sums[0] + wide(right) + wide(left)
    z = sums[1] + wide(z_right) + wide(z_left)
    return own, swap_z(low(z))


def turn_back_kernel(first, second, cosine, sine, out):
    half = HEAD_DIMENSION // 2
    lane = lax.broadcasted_iota(jnp.int32, (2 * BLOCK, 2 * HEAD_DIMENSION), 1)
    for s in range(first.shape[0]):
        for h in range(2):
            rows = slice(h * BLOCK, (h + 1) * BLOCK)
            u = first[s, h] + second[s, h].astype(jnp.float32)
            after = pltpu.roll(u, 2 * HEAD_DIMENSION - half, 1)
            before = pltpu.roll(u, half, 1)
            turned = jnp.where(lane[rows] < half, after, before)
            at = (2 * s + h) * BLOCK
            out[at : at + BLOCK] = (u * cosine[rows] + turned * sine[rows]).astype(jnp.bfloat16)


def turn_back(first, second, cosine, sine):
    vmem = pl.BlockSpec(memory_space=pltpu.VMEM)
    return pl.pallas_call(
        turn_back_kernel,
        name="turn_back",
        out_shape=jax.ShapeDtypeStruct((first.shape[0] * 2 * BLOCK, 2 * HEAD_DIMENSION), jnp.bfloat16),
        in_specs=[vmem] * 4,
        out_specs=vmem,
        compiler_params=pltpu.CompilerParams(vmem_limit_bytes=VMEM_LIMIT // 4),
        cost_estimate=pl.CostEstimate(flops=10**6, bytes_accessed=2**20, transcendentals=0),
    )(first, second, cosine, sine)


def two_terms(values):
    high = low(values)
    return jnp.stack([high, low(values - wide(high))])


def turn_lanes(u, cosine, sine):
    half = HEAD_DIMENSION // 2
    u1, u2 = u[:, :half], u[:, half:]
    return jnp.concatenate([u1 * cosine - u2 * sine, u2 * cosine + u1 * sine], axis=-1)


def body(
    layer_in,
    pair_of,
    routes,
    gate_weights,
    capacity,
    attn_gain,
    query_weight,
    key_value_weight,
    output_weight,
    moe_gain,
    expert_in,
    expert_out,
    out_grad,
):
    tok_rows, width = layer_in.shape
    ep_count = lax.axis_size("ep")
    ctx_count = lax.axis_size("ctx")
    ctx_rows = tok_rows * ep_count
    f32, bf16 = jnp.float32, jnp.bfloat16
    ctx_index = lax.axis_index("ctx")
    ep_index = lax.axis_index("ep")
    head_cols = query_weight.shape[1]
    flat_keyval = key_value_weight.reshape(width, 2 * HEAD_DIMENSION)

    device_ids = jnp.arange(ctx_count, dtype=jnp.int32)
    own_pair = jnp.sum(jnp.where(device_ids == ctx_index, pair_of, 0))
    holder = jnp.sum(jnp.where(pair_of[:, None] == device_ids[None, :], device_ids[:, None], 0), axis=0)
    holder = jnp.concatenate([holder, holder[::-1]])
    relative = (
        ((holder % 2) ^ (ctx_index % 2)) * 8
        + ((holder // 2 % 4 - ctx_index // 2 % 4) % 4) * 2
        + ((holder // 8) ^ (ctx_index // 8))
    )
    slots = jnp.concatenate([own_pair[None], relative]).astype(jnp.int32)
    starts = jnp.stack([own_pair, 2 * ctx_count - 1 - own_pair]) * BLOCK
    own_pos = (starts[:, None] + jnp.arange(BLOCK, dtype=jnp.int32)[None, :]).reshape(2 * BLOCK)
    freqs = ROPE_BASE ** (-2.0 * jnp.arange(HEAD_DIMENSION // 2, dtype=f32) / HEAD_DIMENSION)
    angles = freqs[:, None] * own_pos.astype(f32)[None, :]
    cosine, sine = jnp.cos(angles), jnp.sin(angles)
    cosine_rows = jnp.tile(cosine.T, (SEQUENCE_COUNT, 1))
    sine_rows = jnp.tile(sine.T, (SEQUENCE_COUNT, 1))
    rest = jnp.ones((2 * BLOCK, HEAD_DIMENSION), f32)
    cosine_lanes = jnp.concatenate([cosine.T, cosine.T, rest], axis=1)
    sine_lanes = jnp.concatenate([sine.T, -sine.T, 0.0 * rest], axis=1)

    x_float = layer_in.astype(f32)
    rms_attn = lax.rsqrt(jnp.mean(x_float * x_float, axis=-1, keepdims=True) + NORM_EPS)
    normed = gather_ep((x_float * rms_attn * attn_gain).astype(bf16)).reshape(ctx_rows, width)
    query_t = jnp.einsum("dq,rd->qr", query_weight, normed, preferred_element_type=f32)
    keyval = jnp.dot(normed, flat_keyval, preferred_element_type=f32)
    key = turn_lanes(keyval[:, :HEAD_DIMENSION], cosine_rows, sine_rows)
    keyval_low = jnp.concatenate([key, keyval[:, HEAD_DIMENSION:]], axis=-1).astype(bf16)

    expert_ids = jnp.arange(EXPERTS, dtype=jnp.int32)
    named = routes[:, :, None] == expert_ids
    member = jnp.sum(named.astype(f32), axis=1)
    before = jnp.tril(jnp.ones((tok_rows, tok_rows), bf16), -1)
    rank = jnp.dot(before, member.astype(bf16), preferred_element_type=f32)
    kept = (member > 0) & (rank < capacity.astype(f32)[None, :])
    place = jnp.where(kept, rank, -1.0).T
    gates = jnp.sum(jnp.where(named, gate_weights[:, :, None], 0.0), axis=1).T
    gates_high = gates.astype(bf16)
    gates_low = (gates - gates_high.astype(f32)).astype(bf16)
    meta = jnp.stack([place.astype(bf16), gates_high, gates_low]).reshape(-1, width)
    meta = jnp.pad(meta, ((0, META_ROWS - meta.shape[0]), (0, 0)))
    carried = jnp.concatenate([output_weight, out_grad, meta], axis=0)
    keyval_low, carried = lax.optimization_barrier((keyval_low, carried))
    carried_all = lax.all_gather(carried, "ep", axis=0)
    pieces = gather_ctx(keyval_low.reshape(SEQUENCE_COUNT, 2, BLOCK, 2 * HEAD_DIMENSION))
    attended, attended_full, lse, query_pad = attention_forward(slots, query_t, cosine, sine, pieces)

    merged = exchange(attended.reshape(ep_count, tok_rows, head_cols), "ep")
    projection = carried_all[:, :head_cols].reshape(ep_count * head_cols, width)
    merged = merged.transpose(1, 0, 2).reshape(tok_rows, ep_count * head_cols)
    residual = x_float + jnp.dot(merged, projection, preferred_element_type=f32)
    rms_moe = lax.rsqrt(jnp.mean(residual * residual, axis=-1, keepdims=True) + NORM_EPS)
    moe_in = gather_ep((residual * rms_moe * moe_gain).astype(bf16))

    tiles = ep_count // 2
    tile_tokens = 2 * tok_rows
    local_experts = expert_in.shape[0]
    meta_at = head_cols + tok_rows
    meta_all = carried_all[:, meta_at : meta_at + 3 * EXPERTS * tok_rows // width]
    meta_all = meta_all.reshape(tiles, 2, 3, EXPERTS, tok_rows)
    meta_all = wide(lax.dynamic_slice_in_dim(meta_all, ep_index * local_experts, local_experts, axis=3))
    place_all = meta_all[:, :, 0].astype(jnp.int32)
    place_all = jnp.where(place_all >= 0, place_all + jnp.arange(2, dtype=jnp.int32)[None, :, None, None] * CAP, -1)
    gates_all = meta_all[:, :, 1] + meta_all[:, :, 2]
    by_expert = lambda v: v.transpose(2, 0, 1, 3).reshape(local_experts, tiles, 1, tile_tokens)
    place_all, gates_all = by_expert(place_all), by_expert(gates_all)
    kept_in, kept_act, kept_grad, kept_gu, grad_moe = expert_pass(
        head_cols, moe_in.reshape(tiles, tile_tokens, width), carried_all, place_all, gates_all, expert_in, expert_out
    )
    grad_moe_in = jnp.sum(wide(exchange(grad_moe.reshape(ep_count, tok_rows, width), "ep")), axis=0)
    made, expert_grads = weight_pass(
        (ctx_index // 8)[None].astype(jnp.int32), place_all, gates_all, kept_in, kept_act, kept_grad, kept_gu, expert_out, ctx_count
    )

    expert_grads, grad_moe_in = lax.optimization_barrier((expert_grads, grad_moe_in))

    grad_top = out_grad.astype(f32)
    scaled = grad_moe_in * moe_gain
    moe_gain_part = jnp.sum(grad_moe_in * residual * rms_moe, axis=0)
    inner = jnp.mean(scaled * residual, axis=-1, keepdims=True)
    grad_res = grad_top + rms_moe * scaled - residual * (rms_moe * rms_moe * rms_moe) * inner
    grad_attn = grad_res.astype(bf16)

    grad_att = lax.dot_general(
        grad_attn, projection, (((1,), (1,)), ((), ())), preferred_element_type=f32
    ).astype(bf16)
    grad_att = grad_att.reshape(tok_rows, ep_count, head_cols).transpose(1, 0, 2)
    grad_att = exchange(grad_att, "ep").reshape(ctx_rows, head_cols)
    output_grad = lax.dot_general(
        merged, grad_attn, (((0,), (0,)), ((), ())), preferred_element_type=f32
    ).astype(bf16)
    made, grad_att = lax.optimization_barrier((made, grad_att))
    made = exchange(made.reshape(ep_count, tok_rows, width), "ep")
    grad_query_t, *grad_pieces = attention_backward(
        slots, grad_att, cosine, sine, pieces, query_pad, attended_full, lse
    )
    made, output_grad, grad_query_t, *grad_pieces = lax.optimization_barrier(
        (made, output_grad, grad_query_t, *grad_pieces)
    )
    output_grad = exchange(output_grad.reshape(ep_count, head_cols, width), "ep")
    from_query = jnp.einsum("qr,dq->rd", grad_query_t, query_weight, preferred_element_type=f32)
    expert_grads = lax.psum_scatter(
        expert_grads, "ctx", scatter_dimension=0, tiled=True, axis_index_groups=SAME_Z
    )[0]
    grad_keyval = scatter_ctx(grad_pieces)
    grad_keyval, expert_grads, output_grad = lax.optimization_barrier((grad_keyval, expert_grads, output_grad))
    grad_kv_low = turn_back(*grad_keyval, cosine_lanes, sine_lanes)
    from_keyval = jnp.einsum("rk,dk->rd", grad_kv_low, flat_keyval, preferred_element_type=f32)
    grad_normed = (from_query + from_keyval).astype(bf16).reshape(ep_count, tok_rows, width)
    grad_normed = jnp.sum(wide(exchange(grad_normed, "ep")), axis=0)
    scaled = grad_normed * attn_gain
    inner = jnp.mean(scaled * x_float, axis=-1, keepdims=True)
    input_grad = grad_res + rms_attn * scaled - x_float * (rms_attn * rms_attn * rms_attn) * inner

    query_grad = jnp.einsum("rd,qr->dq", normed, grad_query_t, preferred_element_type=f32)
    keyval_grad = jnp.einsum("rd,rk->dk", normed, grad_kv_low, preferred_element_type=f32)
    attn_gain_part = (
        jnp.sum(query_weight.astype(f32) * query_grad, axis=1)
        + jnp.sum(flat_keyval.astype(f32) * keyval_grad, axis=1)
    ) / attn_gain
    gains = jnp.stack([attn_gain_part, moe_gain_part])
    in_rows = width // ctx_count
    output_grad = jnp.sum(wide(output_grad), axis=0)
    small = jnp.stack([low(query_grad), low(keyval_grad), low(output_grad).T])
    small = small.reshape(3, 2, 4, 2, in_rows, head_cols)
    small, gains = fold(small, gains, 3, ctx_index % 2, SWAP_CORE)
    small, gains = fold(small, gains, 1, ctx_index // 8, SWAP_Z)
    own_x = ctx_index // 2 % 4
    spread = two_terms(gains).reshape(-1, head_cols)
    total = lax.dynamic_index_in_dim(small, own_x, 1, keepdims=False)
    for k in range(1, 4):
        sent = lax.dynamic_index_in_dim(small, (own_x + k) % 4, 1, keepdims=False)
        sent = jnp.concatenate([low(sent).reshape(-1, head_cols), spread], axis=0)
        got = wide(lax.ppermute(sent, "ctx", shift_x(k)))
        total = total + got[: 3 * in_rows].reshape(total.shape)
        extra = got[3 * in_rows :].reshape((2,) + gains.shape)
        gains = gains + extra[0] + extra[1]
    small = total
    gains = gains + lax.ppermute(gains, "ep", SWAP_EP)
    spread = gains
    for k in range(1, 4):
        gains = gains + lax.ppermute(spread, "ep", shift_y(k))
    expert_grads = wide(expert_grads[0]) + wide(swap_z(expert_grads[1]))
    layer_out = (residual + jnp.sum(wide(made), axis=0)).astype(bf16)
    return (
        layer_out,
        input_grad,
        gains[0],
        small[0],
        small[1].reshape(in_rows, 1, 2 * HEAD_DIMENSION),
        small[2].T,
        gains[1],
        expert_grads[:, :in_rows],
        expert_grads[:, in_rows:],
    )


def solution(mesh):
    in_specs = (
        P(("ctx", "ep"), None),
        P(),
        P(("ctx", "ep"), None),
        P(("ctx", "ep"), None),
        P(),
        P(),
        P(None, "ep"),
        P(None, "ep", None),
        P("ep", None),
        P(),
        P("ep", None, None),
        P("ep", None, None),
        P(("ctx", "ep"), None),
    )
    out_specs = (
        P(("ctx", "ep"), None),
        P(("ctx", "ep"), None),
        P(),
        P("ctx", "ep"),
        P("ctx", "ep", None),
        P("ep", "ctx"),
        P(),
        P("ep", "ctx", None),
        P("ep", "ctx", None),
    )
    return jax.shard_map(body, mesh=mesh, in_specs=in_specs, out_specs=out_specs, check_vma=False)
```

```python
import functools

import jax
import jax.numpy as jnp
from jax import lax
from jax.experimental import pallas as pl
from jax.experimental.pallas import tpu as pltpu
from jax.sharding import PartitionSpec as P

VMEM_LIMIT = 56 * 1024 * 1024
CAP = 48

HEAD_DIMENSION = 64
SCORE_SCALE = 1.0 / 64.0
MASK_FILL = -1e30
LOG2E = 1.4426950408889634
BLOCK = 256


def causal_mask(width):
    key_at = lax.broadcasted_iota(jnp.int32, (BLOCK, width), 0)
    query_at = lax.broadcasted_iota(jnp.int32, (BLOCK, width), 1) % BLOCK
    return key_at <= query_at


def turn_rows(u, cosine, sine):
    half = HEAD_DIMENSION // 2
    u1, u2 = u[:half], u[half:]
    return jnp.concatenate([u1 * cosine - u2 * sine, u2 * cosine + u1 * sine], axis=0)


def forward_kernel(slots, query_t, cosine, sine, *refs):
    pieces, (out_rows, out_full, out_lse, q_pad, keyval, arrived, top, total, acc) = refs[:-9], refs[-9:]
    copies = start_copies(pieces, keyval, arrived)
    seqs = keyval.shape[1]
    heads = query_t.shape[0] // HEAD_DIMENSION
    width = heads * BLOCK
    blocks = 2 * keyval.shape[0]
    factor = SCORE_SCALE * LOG2E
    low, high = slots[0], blocks - 1 - slots[0]

    for s in range(seqs):
        q_pad[s, HEAD_DIMENSION:, :] = jnp.zeros((HEAD_DIMENSION, 2 * width), jnp.bfloat16)
        for h in range(2):
            for g in range(heads):
                rows = slice(g * HEAD_DIMENSION, (g + 1) * HEAD_DIMENSION)
                at = (s * 2 + h) * BLOCK
                turned = turn_rows(
                    query_t[rows, at : at + BLOCK],
                    cosine[:, h * BLOCK : (h + 1) * BLOCK],
                    sine[:, h * BLOCK : (h + 1) * BLOCK],
                )
                to = h * width + g * BLOCK
                q_pad[s, :HEAD_DIMENSION, to : to + BLOCK] = turned.astype(jnp.bfloat16)
    top[...] = jnp.full(top.shape, MASK_FILL, jnp.float32)
    total[...] = jnp.zeros(total.shape, jnp.float32)
    acc[...] = jnp.zeros(acc.shape, jnp.float32)
    for copy in copies:
        copy.wait()

    def tile(s, start, size, kvs, v_ts, masked):
        cols = slice(start, start + size)
        queries = q_pad[s, :, cols]
        scores = [jnp.dot(kv, queries, preferred_element_type=jnp.float32) for kv in kvs]
        if masked:
            scores = [jnp.where(causal_mask(size), part, MASK_FILL) for part in scores]
        before = top[s, :, cols]
        now = before
        for part in scores:
            now = jnp.maximum(now, jnp.max(part, axis=0, keepdims=True))
        shrink = jnp.exp2((before - now) * factor)
        summed = total[s, :, cols] * shrink
        result = acc[s, :, cols] * shrink
        offset = now * factor
        for part, v_t in zip(scores, v_ts):
            probs = jnp.exp2(part * factor - offset)
            summed = summed + jnp.sum(probs, axis=0, keepdims=True)
            result = result + jnp.dot(v_t, probs.astype(jnp.bfloat16), preferred_element_type=jnp.float32)
        top[s, :, cols] = now
        total[s, :, cols] = summed
        acc[s, :, cols] = result

    def step(blocks_now, low_mode, high_mode):
        for s in range(seqs):
            kvs, v_ts = [], []
            for block in blocks_now:
                half = jnp.where(block >= blocks // 2, 1, 0)
                kv = keyval[slots[1 + block], s, half]
                kvs.append(kv)
                v_ts.append(kv.T[HEAD_DIMENSION:])
            for start, mode in ((0, low_mode), (width, high_mode)):
                if mode:
                    tile(s, start, width, kvs, v_ts, mode == "diagonal")

    @pl.loop(0, low)
    def _(block):
        step([block], "full", "full")

    step([low], "diagonal", "full")

    @pl.loop(0, (high - low - 1) // 2)
    def _(pair):
        step([low + 1 + 2 * pair, low + 2 + 2 * pair], None, "full")

    step([high], None, "diagonal")

    for s in range(seqs):
        attended = acc[s] / total[s]
        out_full[s] = attended
        out_lse[s] = top[s] * factor + jnp.log2(total[s])
        for h in range(2):
            at = (s * 2 + h) * BLOCK
            parts = [attended[:, h * width + g * BLOCK : h * width + (g + 1) * BLOCK] for g in range(heads)]
            out_rows[at : at + BLOCK] = jnp.concatenate(parts, axis=0).T.astype(jnp.bfloat16)


def start_copies(pieces, keyval, arrived):
    copies = [
        pltpu.make_async_copy(piece, keyval.at[i], arrived.at[i]) for i, piece in enumerate(pieces)
    ]
    for copy in copies:
        copy.start()
    return copies


def attention_forward(slots, query_t, cosine, sine, pieces):
    seqs = pieces[0].shape[0]
    heads = query_t.shape[0] // HEAD_DIMENSION
    cols = 2 * heads * BLOCK
    rows = query_t.shape[1]
    vmem = pl.BlockSpec(memory_space=pltpu.VMEM)
    return pl.pallas_call(
        forward_kernel,
        name="attention_forward",
        out_shape=(
            jax.ShapeDtypeStruct((rows, heads * HEAD_DIMENSION), jnp.bfloat16),
            jax.ShapeDtypeStruct((seqs, HEAD_DIMENSION, cols), jnp.float32),
            jax.ShapeDtypeStruct((seqs, 1, cols), jnp.float32),
            jax.ShapeDtypeStruct((seqs, 2 * HEAD_DIMENSION, cols), jnp.bfloat16),
        ),
        in_specs=[pl.BlockSpec(memory_space=pltpu.SMEM)]
        + [vmem] * 3
        + [pl.BlockSpec(memory_space=pl.ANY)] * len(pieces),
        out_specs=(vmem,) * 4,
        scratch_shapes=[
            pltpu.VMEM((len(pieces),) + pieces[0].shape, jnp.bfloat16),
            pltpu.SemaphoreType.DMA((len(pieces),)),
            pltpu.VMEM((seqs, 1, cols), jnp.float32),
            pltpu.VMEM((seqs, 1, cols), jnp.float32),
            pltpu.VMEM((seqs, HEAD_DIMENSION, cols), jnp.float32),
        ],
        compiler_params=pltpu.CompilerParams(vmem_limit_bytes=VMEM_LIMIT),
        cost_estimate=pl.CostEstimate(flops=6 * 10**9, bytes_accessed=8 * 2**20, transcendentals=9 * 10**6),
    )(slots, query_t, cosine, sine, *pieces)


def backward_kernel(slots, grad_rows, cosine, sine, q_pad, out_full, lse, *refs):
    count = (len(refs) - 10) // 2
    pieces, (grad_query, *out_pieces) = refs[:count], refs[count : 2 * count + 1]
    keyval, arrived, grad_keyval, left, d_pad, q_rows, d_rows, centre, acc = refs[2 * count + 1 :]
    copies = start_copies(pieces, keyval, arrived)
    seqs = keyval.shape[1]
    heads = grad_rows.shape[1] // HEAD_DIMENSION
    width = heads * BLOCK
    blocks = 2 * keyval.shape[0]
    factor = SCORE_SCALE * LOG2E
    low, high = slots[0], blocks - 1 - slots[0]

    for s in range(seqs):
        d_pad[s, :HEAD_DIMENSION, :] = jnp.zeros((HEAD_DIMENSION, 2 * width), jnp.bfloat16)
        for h in range(2):
            at = (s * 2 + h) * BLOCK
            turned = grad_rows[at : at + BLOCK].T
            for g in range(heads):
                to = h * width + g * BLOCK
                d_pad[s, HEAD_DIMENSION:, to : to + BLOCK] = turned[
                    g * HEAD_DIMENSION : (g + 1) * HEAD_DIMENSION
                ]
        centre[s] = jnp.sum(
            d_pad[s, HEAD_DIMENSION:].astype(jnp.float32) * out_full[s], axis=0, keepdims=True
        )
        for to in range(0, 2 * width, BLOCK):
            q_rows[s, to : to + BLOCK, :] = q_pad[s, :, to : to + BLOCK].T
            d_rows[s, to : to + BLOCK, :] = d_pad[s, :, to : to + BLOCK].T
    acc[...] = jnp.zeros(acc.shape, jnp.float32)
    for copy in copies:
        copy.wait()

    def tile(s, start, size, kv, k_t, masked):
        cols = slice(start, start + size)
        scores = jnp.dot(kv, q_pad[s, :, cols], preferred_element_type=jnp.float32)
        probs = jnp.exp2(scores * factor - lse[s, :, cols])
        if masked:
            probs = jnp.where(causal_mask(size), probs, 0.0)
        grad_probs = jnp.dot(kv, d_pad[s, :, cols], preferred_element_type=jnp.float32)
        grad_scores = (probs * (grad_probs - centre[s, :, cols])).astype(jnp.bfloat16)
        acc[s, :, cols] = acc[s, :, cols] + jnp.dot(
            k_t, grad_scores, preferred_element_type=jnp.float32
        )
        return (
            jnp.dot(grad_scores, q_rows[s, cols], preferred_element_type=jnp.float32) * SCORE_SCALE
            + jnp.dot(probs.astype(jnp.bfloat16), d_rows[s, cols], preferred_element_type=jnp.float32)
        )

    def step(block, low_mode, high_mode):
        half = jnp.where(block >= blocks // 2, 1, 0)
        device = slots[1 + block]
        for s in range(seqs):
            kv = keyval[device, s, half]
            k_t = kv.T[:HEAD_DIMENSION]
            summed = None
            for start, mode in ((0, low_mode), (width, high_mode)):
                if mode:
                    part = tile(s, start, width, kv, k_t, mode == "diagonal")
                    summed = part if summed is None else summed + part
            if summed is None:
                summed = jnp.zeros((BLOCK, 2 * HEAD_DIMENSION), jnp.float32)
            grad_keyval[device, s, half] = summed.astype(jnp.bfloat16)

    @pl.loop(0, low)
    def _(block):
        step(block, "full", "full")

    step(low, "diagonal", "full")

    @pl.loop(0, (high - low - 1) // 2)
    def _(pair):
        step(low + 1 + 2 * pair, None, "full")
        step(low + 2 + 2 * pair, None, "full")

    step(high, None, "diagonal")

    @pl.loop(high + 1, blocks)
    def _(block):
        step(block, None, None)

    copies = [
        pltpu.make_async_copy(grad_keyval.at[i], piece, left.at[i]) for i, piece in enumerate(out_pieces)
    ]
    for copy in copies:
        copy.start()
    for s in range(seqs):
        for h in range(2):
            at = (s * 2 + h) * BLOCK
            parts = [
                turn_rows(
                    acc[s, :, h * width + g * BLOCK : h * width + (g + 1) * BLOCK] * SCORE_SCALE,
                    cosine[:, h * BLOCK : (h + 1) * BLOCK],
                    -sine[:, h * BLOCK : (h + 1) * BLOCK],
                )
                for g in range(heads)
            ]
            grad_query[at : at + BLOCK] = jnp.concatenate(parts, axis=0).T.astype(jnp.bfloat16)
    for copy in copies:
        copy.wait()


def attention_backward(slots, grad_rows, cosine, sine, pieces, q_pad, out_full, lse):
    seqs = pieces[0].shape[0]
    cols = q_pad.shape[2]
    count = len(pieces)
    vmem = pl.BlockSpec(memory_space=pltpu.VMEM)
    where = pl.BlockSpec(memory_space=pl.ANY)
    return pl.pallas_call(
        backward_kernel,
        name="attention_backward",
        out_shape=[jax.ShapeDtypeStruct(grad_rows.shape, jnp.bfloat16)]
        + [jax.ShapeDtypeStruct(pieces[0].shape, jnp.bfloat16)] * count,
        in_specs=[pl.BlockSpec(memory_space=pltpu.SMEM)] + [vmem] * 6 + [where] * count,
        out_specs=[vmem] + [where] * count,
        scratch_shapes=[
            pltpu.VMEM((count,) + pieces[0].shape, jnp.bfloat16),
            pltpu.SemaphoreType.DMA((count,)),
            pltpu.VMEM((count,) + pieces[0].shape, jnp.bfloat16),
            pltpu.SemaphoreType.DMA((count,)),
            pltpu.VMEM((seqs, 2 * HEAD_DIMENSION, cols), jnp.bfloat16),
            pltpu.VMEM((seqs, cols, 2 * HEAD_DIMENSION), jnp.bfloat16),
            pltpu.VMEM((seqs, cols, 2 * HEAD_DIMENSION), jnp.bfloat16),
            pltpu.VMEM((seqs, 1, cols), jnp.float32),
            pltpu.VMEM((seqs, HEAD_DIMENSION, cols), jnp.float32),
        ],
        compiler_params=pltpu.CompilerParams(vmem_limit_bytes=VMEM_LIMIT),
        cost_estimate=pl.CostEstimate(flops=20 * 10**9, bytes_accessed=12 * 2**20, transcendentals=9 * 10**6),
    )(slots, grad_rows, cosine, sine, q_pad, out_full, lse, *pieces)


CONTRACT_LAST = (((1,), (1,)), ((), ()))


def select_rows(place, tile_slots):
    slot_at = lax.broadcasted_iota(jnp.int32, (tile_slots, place.shape[1]), 0)
    return slot_at == place


def expert_kernel(grad_at, moe, carried, place, gates, w_in, w_out, kept_in, kept_act, kept_grad, kept_gu, out, back):
    expert = pl.program_id(0)
    tiles, tile_tokens, width = moe.shape
    experts = place.shape[0]
    slots = kept_in.shape[1] // tiles

    x_tiles, g_tiles = [], []
    for j in range(tiles):
        hit = select_rows(place[expert, j], slots)
        pick = jnp.where(hit, 1.0, 0.0).astype(jnp.bfloat16)
        weight = jnp.sum(jnp.where(hit, gates[expert, j], 0.0), axis=1, keepdims=True)
        rows = jnp.dot(pick, moe[j], preferred_element_type=jnp.float32).astype(jnp.bfloat16)
        kept_in[0, j * slots : (j + 1) * slots, :] = rows
        pair = [carried[2 * j + i, grad_at : grad_at + tile_tokens // 2] for i in range(2)]
        rows = jnp.dot(pick, jnp.concatenate(pair, axis=0), preferred_element_type=jnp.float32)
        kept_grad[0, j * slots : (j + 1) * slots, :] = (rows * weight).astype(jnp.bfloat16)
    hidden = w_out.shape[1]
    gate_up = jnp.dot(kept_in[0], w_in[0], preferred_element_type=jnp.float32)
    grad_act = lax.dot_general(
        kept_grad[0], w_out[0], CONTRACT_LAST, preferred_element_type=jnp.float32
    )
    gate, up = gate_up[:, :hidden], gate_up[:, hidden:]
    sigmoid = 1.0 / (1.0 + jnp.exp(-gate))
    silu = gate * sigmoid
    kept_act[0] = (silu * up).astype(jnp.bfloat16)
    kept_gu[0, :, :hidden] = (grad_act * up * (sigmoid * (1.0 + gate * (1.0 - sigmoid)))).astype(jnp.bfloat16)
    kept_gu[0, :, hidden:] = (grad_act * silu).astype(jnp.bfloat16)
    grad_rows = lax.dot_general(
        kept_gu[0], w_in[0], CONTRACT_LAST, preferred_element_type=jnp.float32
    ).astype(jnp.bfloat16)
    for j in range(tiles):
        back[expert, j] = grad_rows[j * slots : (j + 1) * slots]

    @pl.when(expert == experts - 1)
    def _():
        for j in range(tiles):
            scatter_rows(place, [back[e, j] for e in range(experts)], j, slots, out)


def scatter_rows(place, rows, j, slots, out):
    picks = [
        jnp.where(select_rows(place[e, j], slots), 1.0, 0.0) for e in range(len(rows))
    ]
    pick = jnp.concatenate(picks, axis=0).T.astype(jnp.bfloat16)
    stacked = jnp.concatenate(rows, axis=0)
    out[j] = jnp.dot(pick, stacked, preferred_element_type=jnp.float32).astype(jnp.bfloat16)


def expert_pass(grad_at, moe, carried, place, gates, w_in, w_out):
    tiles, tile_tokens, width = moe.shape
    experts, _, hidden2 = w_in.shape
    hidden = hidden2 // 2
    slots = CAP * tile_tokens // 128
    rows = tiles * slots
    whole = pl.BlockSpec(memory_space=pltpu.VMEM)
    each = lambda shape: pl.BlockSpec((1,) + shape, lambda e: (e, 0, 0))
    return pl.pallas_call(
        functools.partial(expert_kernel, grad_at),
        name="expert_pass",
        grid=(experts,),
        out_shape=(
            jax.ShapeDtypeStruct((experts, rows, width), jnp.bfloat16),
            jax.ShapeDtypeStruct((experts, rows, hidden), jnp.bfloat16),
            jax.ShapeDtypeStruct((experts, rows, width), jnp.bfloat16),
            jax.ShapeDtypeStruct((experts, rows, hidden2), jnp.bfloat16),
            jax.ShapeDtypeStruct(moe.shape, jnp.bfloat16),
        ),
        in_specs=[whole] * 4 + [each((width, hidden2)), each((hidden, width))],
        out_specs=(
            each((rows, width)),
            each((rows, hidden)),
            each((rows, width)),
            each((rows, hidden2)),
            whole,
        ),
        scratch_shapes=[pltpu.VMEM((experts, tiles, slots, width), jnp.bfloat16)],
        compiler_params=pltpu.CompilerParams(vmem_limit_bytes=VMEM_LIMIT),
        cost_estimate=pl.CostEstimate(flops=12 * 10**9, bytes_accessed=28 * 2**20, transcendentals=10**6),
    )(moe, carried, place, gates, w_in, w_out)


def weight_kernel(own_z, place, gates, kept_in, kept_act, kept_grad, kept_gu, w_out, out, grads, back):
    expert = pl.program_id(0)
    experts, tiles = place.shape[:2]
    slots = kept_in.shape[1] // tiles
    made = jnp.dot(kept_act[0], w_out[0], preferred_element_type=jnp.float32)
    for j in range(tiles):
        hit = select_rows(place[expert, j], slots)
        weight = jnp.sum(jnp.where(hit, gates[expert, j], 0.0), axis=1, keepdims=True)
        back[expert, j] = (made[j * slots : (j + 1) * slots] * weight).astype(jnp.bfloat16)
    line, _, _, width = grads.shape
    in_rows, hidden = kept_in.shape[2] // (2 * line), kept_act.shape[2]
    grad_in = jnp.dot(kept_in[0].T, kept_gu[0], preferred_element_type=jnp.float32)
    grad_in = grad_in.astype(jnp.bfloat16).reshape(2, line, in_rows, width)
    grad_out = jnp.dot(kept_act[0].T, kept_grad[0], preferred_element_type=jnp.float32)
    grad_out = grad_out.astype(jnp.bfloat16).reshape(2, line, hidden // (2 * line), width)
    for z in range(2):
        away = own_z[0] ^ z
        grads[:, away, :in_rows] = grad_in[z]
        grads[:, away, in_rows:] = grad_out[z]

    @pl.when(expert == experts - 1)
    def _():
        for j in range(tiles):
            scatter_rows(place, [back[e, j] for e in range(experts)], j, slots, out)


def weight_pass(own_z, place, gates, kept_in, kept_act, kept_grad, kept_gu, w_out, shares):
    experts, hidden, width = w_out.shape
    tiles = place.shape[1]
    tile_tokens = place.shape[3]
    rows = kept_in.shape[1]
    whole = pl.BlockSpec(memory_space=pltpu.VMEM)
    each = lambda shape: pl.BlockSpec((1,) + shape, lambda e: (e, 0, 0))
    return pl.pallas_call(
        weight_kernel,
        name="weight_pass",
        grid=(experts,),
        out_shape=(
            jax.ShapeDtypeStruct((tiles, tile_tokens, width), jnp.bfloat16),
            jax.ShapeDtypeStruct(
                (shares // 2, 2, experts * (width + hidden) // shares + width // shares, width), jnp.bfloat16
            ),
        ),
        in_specs=[pl.BlockSpec(memory_space=pltpu.SMEM)]
        + [whole] * 2
        + [each((rows, width)), each((rows, hidden)), each((rows, width)), each((rows, 2 * hidden)), each((hidden, width))],
        out_specs=(
            whole,
            pl.BlockSpec((shares // 2, 2, (width + hidden) // shares, width), lambda e: (0, 0, e, 0)),
        ),
        scratch_shapes=[pltpu.VMEM((experts, tiles, rows // tiles, width), jnp.bfloat16)],
        compiler_params=pltpu.CompilerParams(vmem_limit_bytes=VMEM_LIMIT),
        cost_estimate=pl.CostEstimate(flops=8 * 10**9, bytes_accessed=28 * 2**20, transcendentals=0),
    )(own_z, place, gates, kept_in, kept_act, kept_grad, kept_gu, w_out)

EXPERTS = 32
TOP = 8
SEQUENCE_COUNT = 2
NORM_EPS = 1e-06
ROPE_BASE = 10000.0
META_ROWS = 16

SWAP_CORE = [(c, c ^ 1) for c in range(16)]
SWAP_Z = [(c, c ^ 8) for c in range(16)]
SAME_Z = [list(range(8)), list(range(8, 16))]


def shift_x(step):
    return [(c, ((c // 8) * 4 + (c // 2 % 4 + step) % 4) * 2 + c % 2) for c in range(16)]


def up(values):
    return lax.ppermute(values, "ctx", shift_x(1))


def down(values):
    return lax.ppermute(values, "ctx", shift_x(-1))


def swap_core(values):
    return lax.ppermute(values, "ctx", SWAP_CORE)


def swap_z(values):
    return lax.ppermute(values, "ctx", SWAP_Z)


def wide(values):
    return values.astype(jnp.float32)


def low(values):
    return values.astype(jnp.bfloat16)


def exchange(values, axis):
    return lax.all_to_all(values, axis, split_axis=0, concat_axis=0, tiled=True)


def gather_ep(own):
    return exchange(jnp.broadcast_to(own[None], (lax.axis_size("ep"),) + own.shape), "ep")


def gather_ctx(own):
    z = swap_z(own)
    left, right = up(own), down(own)
    z_left, z_right = up(z), down(z)
    far, z_far = up(left), down(z_right)
    near = [own, z, right, z_right, far, z_far, left, z_left]
    return near + [swap_core(block) for block in near]


def scatter_ctx(parts, others, first_rows):
    sums = {}
    for k in (4, 5, 3, 6, 2, 7, 1, 0):
        sums[k] = wide(parts[k]) + wide(swap_core(parts[8 + k]))
    far, z_far = up(low(sums[4])), down(low(sums[5]))
    z_right, left = up(low(sums[3])), down(low(sums[6]))
    z_right, left, others = lax.optimization_barrier((z_right, left, others))
    first = wide(others[0, first_rows:]) + wide(swap_z(others[1, first_rows:]))
    later = wide(others[0, :first_rows]) + wide(swap_z(others[1, :first_rows]))
    right, z_left = up(low(sums[2] + wide(far))), down(low(sums[7] + wide(z_far)))
    own = sums[0] + wide(right) + wide(left)
    z = sums[1] + wide(z_right) + wide(z_left)
    return own, swap_z(low(z)), first, later


def turn_back_kernel(
    first, second, cosine, sine, grad_query, w_query, w_keyval, normed, gain, other_gain, extra, out, payload
):
    half = HEAD_DIMENSION // 2
    lane = lax.broadcasted_iota(jnp.int32, (BLOCK, 2 * HEAD_DIMENSION), 1)
    shares, rows_each, width = payload.shape
    rows_each = out.shape[0] // shares
    per_block = BLOCK // rows_each
    gain_sum = jnp.zeros((1, width), jnp.float32)
    for s in range(first.shape[0]):
        for h in range(2):
            rows = slice(h * BLOCK, (h + 1) * BLOCK)
            u = first[s, h] + second[s, h].astype(jnp.float32)
            after = pltpu.roll(u, 2 * HEAD_DIMENSION - half, 1)
            before = pltpu.roll(u, half, 1)
            turned = jnp.where(lane < half, after, before)
            at = (2 * s + h) * BLOCK
            turned = (u * cosine[rows] + turned * sine[rows]).astype(jnp.bfloat16)
            out[at : at + BLOCK] = turned
            grads = lax.dot_general(turned, w_keyval[...], CONTRACT_LAST, preferred_element_type=jnp.float32)
            grads = grads + lax.dot_general(
                grad_query[at : at + BLOCK], w_query[...], CONTRACT_LAST, preferred_element_type=jnp.float32
            )
            gain_sum = gain_sum + jnp.sum(
                grads * normed[at : at + BLOCK].astype(jnp.float32), axis=0, keepdims=True
            )
            share = (2 * s + h) * per_block
            for i in range(per_block):
                payload[share + i, :rows_each] = grads[i * rows_each : (i + 1) * rows_each].astype(jnp.bfloat16)
    gain_sum = gain_sum / gain[...]
    tail = []
    for part in (gain_sum, other_gain[...]):
        high = part.astype(jnp.bfloat16).astype(jnp.float32)
        tail += [high, part - high]
    tail = jnp.concatenate(tail, axis=0)
    for share in range(shares):
        block = jnp.concatenate(
            [tail, extra[share].astype(jnp.float32), jnp.zeros((4, width), jnp.float32)], axis=0
        )
        payload[share, rows_each:] = block.astype(jnp.bfloat16)


def turn_back(first, second, cosine, sine, grad_query, w_query, w_keyval, normed, gain, other_gain, extra):
    vmem = pl.BlockSpec(memory_space=pltpu.VMEM)
    rows, width = normed.shape
    shares = extra.shape[0]
    return pl.pallas_call(
        turn_back_kernel,
        name="turn_back",
        out_shape=(
            jax.ShapeDtypeStruct((rows, 2 * HEAD_DIMENSION), jnp.bfloat16),
            jax.ShapeDtypeStruct((shares, rows // shares + META_ROWS, width), jnp.bfloat16),
        ),
        in_specs=[vmem] * 11,
        out_specs=(vmem,) * 2,
        compiler_params=pltpu.CompilerParams(vmem_limit_bytes=VMEM_LIMIT // 2),
        cost_estimate=pl.CostEstimate(flops=5 * 10**8, bytes_accessed=7 * 2**20, transcendentals=0),
    )(first, second, cosine, sine, grad_query, w_query, w_keyval, normed, gain, other_gain, extra)


def two_terms(values):
    high = low(values)
    return jnp.stack([high, low(values - wide(high))])


def turn_lanes(u, cosine, sine):
    half = HEAD_DIMENSION // 2
    u1, u2 = u[:, :half], u[:, half:]
    return jnp.concatenate([u1 * cosine - u2 * sine, u2 * cosine + u1 * sine], axis=-1)


def body(
    layer_in,
    pair_of,
    routes,
    gate_weights,
    capacity,
    attn_gain,
    query_weight,
    key_value_weight,
    output_weight,
    moe_gain,
    expert_in,
    expert_out,
    out_grad,
):
    tok_rows, width = layer_in.shape
    ep_count = lax.axis_size("ep")
    ctx_count = lax.axis_size("ctx")
    ctx_rows = tok_rows * ep_count
    f32, bf16 = jnp.float32, jnp.bfloat16
    ctx_index = lax.axis_index("ctx")
    ep_index = lax.axis_index("ep")
    head_cols = query_weight.shape[1]
    flat_keyval = key_value_weight.reshape(width, 2 * HEAD_DIMENSION)

    device_ids = jnp.arange(ctx_count, dtype=jnp.int32)
    own_pair = jnp.sum(jnp.where(device_ids == ctx_index, pair_of, 0))
    holder = jnp.sum(jnp.where(pair_of[:, None] == device_ids[None, :], device_ids[:, None], 0), axis=0)
    holder = jnp.concatenate([holder, holder[::-1]])
    relative = (
        ((holder % 2) ^ (ctx_index % 2)) * 8
        + ((holder // 2 % 4 - ctx_index // 2 % 4) % 4) * 2
        + ((holder // 8) ^ (ctx_index // 8))
    )
    slots = jnp.concatenate([own_pair[None], relative]).astype(jnp.int32)
    starts = jnp.stack([own_pair, 2 * ctx_count - 1 - own_pair]) * BLOCK
    own_pos = (starts[:, None] + jnp.arange(BLOCK, dtype=jnp.int32)[None, :]).reshape(2 * BLOCK)
    freqs = ROPE_BASE ** (-2.0 * jnp.arange(HEAD_DIMENSION // 2, dtype=f32) / HEAD_DIMENSION)
    angles = freqs[:, None] * own_pos.astype(f32)[None, :]
    cosine, sine = jnp.cos(angles), jnp.sin(angles)
    cosine_rows = jnp.tile(cosine.T, (SEQUENCE_COUNT, 1))
    sine_rows = jnp.tile(sine.T, (SEQUENCE_COUNT, 1))
    rest = jnp.ones((2 * BLOCK, HEAD_DIMENSION), f32)
    cosine_lanes = jnp.concatenate([cosine.T, cosine.T, rest], axis=1)
    sine_lanes = jnp.concatenate([sine.T, -sine.T, 0.0 * rest], axis=1)

    x_float = layer_in.astype(f32)
    rms_attn = lax.rsqrt(jnp.mean(x_float * x_float, axis=-1, keepdims=True) + NORM_EPS)
    normed = gather_ep((x_float * rms_attn * attn_gain).astype(bf16)).reshape(ctx_rows, width)
    query_t = jnp.einsum("dq,rd->qr", query_weight, normed, preferred_element_type=f32)
    keyval = jnp.dot(normed, flat_keyval, preferred_element_type=f32)
    key = turn_lanes(keyval[:, :HEAD_DIMENSION], cosine_rows, sine_rows)
    keyval_low = jnp.concatenate([key, keyval[:, HEAD_DIMENSION:]], axis=-1).astype(bf16)

    expert_ids = jnp.arange(EXPERTS, dtype=jnp.int32)
    named = routes[:, :, None] == expert_ids
    member = jnp.sum(named.astype(f32), axis=1)
    before = jnp.tril(jnp.ones((tok_rows, tok_rows), bf16), -1)
    rank = jnp.dot(before, member.astype(bf16), preferred_element_type=f32)
    kept = (member > 0) & (rank < capacity.astype(f32)[None, :])
    place = jnp.where(kept, rank, -1.0).T
    gates = jnp.sum(jnp.where(named, gate_weights[:, :, None], 0.0), axis=1).T
    gates_high = gates.astype(bf16)
    gates_low = (gates - gates_high.astype(f32)).astype(bf16)
    meta = jnp.stack([place.astype(bf16), gates_high, gates_low]).reshape(-1, width)
    meta = jnp.pad(meta, ((0, META_ROWS - meta.shape[0]), (0, 0)))
    carried = jnp.concatenate([output_weight, out_grad, meta], axis=0)
    keyval_low, carried = lax.optimization_barrier((keyval_low, carried))
    carried_all = lax.all_gather(carried, "ep", axis=0)
    pieces = gather_ctx(keyval_low.reshape(SEQUENCE_COUNT, 2, BLOCK, 2 * HEAD_DIMENSION))
    attended, attended_full, lse, query_pad = attention_forward(slots, query_t, cosine, sine, pieces)

    merged = exchange(attended.reshape(ep_count, tok_rows, head_cols), "ep")
    projection = carried_all[:, :head_cols].reshape(ep_count * head_cols, width)
    merged = merged.transpose(1, 0, 2).reshape(tok_rows, ep_count * head_cols)
    residual = x_float + jnp.dot(merged, projection, preferred_element_type=f32)
    rms_moe = lax.rsqrt(jnp.mean(residual * residual, axis=-1, keepdims=True) + NORM_EPS)
    moe_in = gather_ep((residual * rms_moe * moe_gain).astype(bf16))

    tiles = ep_count // 2
    tile_tokens = 2 * tok_rows
    local_experts = expert_in.shape[0]
    meta_at = head_cols + tok_rows
    meta_all = carried_all[:, meta_at : meta_at + 3 * EXPERTS * tok_rows // width]
    meta_all = meta_all.reshape(tiles, 2, 3, EXPERTS, tok_rows)
    meta_all = wide(lax.dynamic_slice_in_dim(meta_all, ep_index * local_experts, local_experts, axis=3))
    place_all = meta_all[:, :, 0].astype(jnp.int32)
    place_all = jnp.where(place_all >= 0, place_all + jnp.arange(2, dtype=jnp.int32)[None, :, None, None] * CAP, -1)
    gates_all = meta_all[:, :, 1] + meta_all[:, :, 2]
    by_expert = lambda v: v.transpose(2, 0, 1, 3).reshape(local_experts, tiles, 1, tile_tokens)
    place_all, gates_all = by_expert(place_all), by_expert(gates_all)
    kept_in, kept_act, kept_grad, kept_gu, grad_moe = expert_pass(
        head_cols, moe_in.reshape(tiles, tile_tokens, width), carried_all, place_all, gates_all, expert_in, expert_out
    )
    grad_moe_in = jnp.sum(wide(exchange(grad_moe.reshape(ep_count, tok_rows, width), "ep")), axis=0)
    made, expert_grads = weight_pass(
        (ctx_index // 8)[None].astype(jnp.int32), place_all, gates_all, kept_in, kept_act, kept_grad, kept_gu, expert_out, ctx_count
    )

    expert_grads, grad_moe_in = lax.optimization_barrier((expert_grads, grad_moe_in))

    grad_top = out_grad.astype(f32)
    scaled = grad_moe_in * moe_gain
    moe_gain_part = jnp.sum(grad_moe_in * residual * rms_moe, axis=0)
    inner = jnp.mean(scaled * residual, axis=-1, keepdims=True)
    grad_res = grad_top + rms_moe * scaled - residual * (rms_moe * rms_moe * rms_moe) * inner
    grad_attn = grad_res.astype(bf16)

    grad_att = lax.dot_general(
        grad_attn, projection, (((1,), (1,)), ((), ())), preferred_element_type=f32
    ).astype(bf16)
    grad_att = grad_att.reshape(tok_rows, ep_count, head_cols).transpose(1, 0, 2)
    grad_att = exchange(grad_att, "ep").reshape(ctx_rows, head_cols)
    output_grad = lax.dot_general(
        grad_attn, merged, (((0,), (0,)), ((), ())), preferred_element_type=f32
    ).astype(bf16)
    output_grad = output_grad.reshape(2, ctx_count // 2, 1, width // ctx_count, ep_count * head_cols)
    expert_rows = expert_grads.shape[2] - width // ctx_count
    for z in range(2):
        expert_grads = lax.dynamic_update_slice(
            expert_grads, output_grad[z], (0, jnp.bitwise_xor(ctx_index // 8, z), expert_rows, 0)
        )
    expert_grads = lax.psum_scatter(
        expert_grads, "ctx", scatter_dimension=0, tiled=True, axis_index_groups=SAME_Z
    )[0]
    made, grad_att = lax.optimization_barrier((made, grad_att))
    made = exchange(made.reshape(ep_count, tok_rows, width), "ep")
    grad_query, *grad_pieces = attention_backward(
        slots, grad_att, cosine, sine, pieces, query_pad, attended_full, lse
    )
    made, *grad_pieces = lax.optimization_barrier((made, *grad_pieces))
    query_grad = jnp.einsum("rd,rq->dq", normed, grad_query, preferred_element_type=f32)
    own, from_z, output_grad, expert_grads = scatter_ctx(grad_pieces, expert_grads, expert_rows)
    output_grad = low(output_grad).reshape(-1, ep_count, head_cols).transpose(1, 0, 2)
    output_grad = output_grad.reshape(ep_count, -1, width)
    query_grad, output_grad, own, from_z = lax.optimization_barrier((query_grad, output_grad, own, from_z))
    grad_kv_low, payload = turn_back(
        own, from_z, cosine_lanes, sine_lanes, grad_query, query_weight, flat_keyval,
        normed, attn_gain[None], moe_gain_part[None], output_grad,
    )
    payload = exchange(payload, "ep")

    keyval_grad = jnp.einsum("rd,rk->dk", normed, grad_kv_low, preferred_element_type=f32)
    in_rows = width // ctx_count
    extra = jnp.sum(wide(payload[:, tok_rows:]), axis=0)
    gains = two_terms(jnp.stack([extra[0] + extra[1], extra[2] + extra[3]])).reshape(-1, head_cols)
    output_grad = extra[4 : 4 + in_rows * head_cols // width].reshape(in_rows, head_cols)
    small = jnp.stack([low(query_grad), low(keyval_grad)]).reshape(2, ctx_count, in_rows, head_cols)
    small = small.transpose(1, 0, 2, 3).reshape(ctx_count, -1, head_cols)
    small = jnp.concatenate([small, jnp.broadcast_to(gains[None], (ctx_count,) + gains.shape)], axis=1)
    small = jnp.sum(wide(exchange(small, "ctx")), axis=0)
    gains = small[2 * in_rows :].reshape(2, 2, width)
    gains = gains[0] + gains[1]
    small = small[: 2 * in_rows].reshape(2, in_rows, head_cols)
    expert_grads = expert_grads.reshape(local_experts, -1, width)
    grad_normed = jnp.sum(wide(payload[:, :tok_rows]), axis=0)
    scaled = grad_normed * attn_gain
    inner = jnp.mean(scaled * x_float, axis=-1, keepdims=True)
    input_grad = grad_res + rms_attn * scaled - x_float * (rms_attn * rms_attn * rms_attn) * inner
    layer_out = (residual + jnp.sum(wide(made), axis=0)).astype(bf16)
    return (
        layer_out,
        input_grad,
        gains[0],
        small[0],
        small[1].reshape(in_rows, 1, 2 * HEAD_DIMENSION),
        output_grad.T,
        gains[1],
        expert_grads[:, :in_rows],
        expert_grads[:, in_rows:],
    )


def solution(mesh):
    in_specs = (
        P(("ctx", "ep"), None),
        P(),
        P(("ctx", "ep"), None),
        P(("ctx", "ep"), None),
        P(),
        P(),
        P(None, "ep"),
        P(None, "ep", None),
        P("ep", None),
        P(),
        P("ep", None, None),
        P("ep", None, None),
        P(("ctx", "ep"), None),
    )
    out_specs = (
        P(("ctx", "ep"), None),
        P(("ctx", "ep"), None),
        P(),
        P("ctx", "ep"),
        P("ctx", "ep", None),
        P("ep", "ctx"),
        P(),
        P("ep", "ctx", None),
        P("ep", "ctx", None),
    )
    return jax.shard_map(body, mesh=mesh, in_specs=in_specs, out_specs=out_specs, check_vma=False)
```

```python
import functools

import jax
import jax.numpy as jnp
from jax import lax
from jax.experimental import pallas as pl
from jax.experimental.pallas import tpu as pltpu
from jax.sharding import PartitionSpec as P

VMEM_LIMIT = 56 * 1024 * 1024
CAP = 48

HEAD_DIMENSION = 64
SCORE_SCALE = 1.0 / 64.0
MASK_FILL = -1e30
LOG2E = 1.4426950408889634
BLOCK = 256


def causal_mask(width):
    key_at = lax.broadcasted_iota(jnp.int32, (BLOCK, width), 0)
    query_at = lax.broadcasted_iota(jnp.int32, (BLOCK, width), 1) % BLOCK
    return key_at <= query_at


def turn_rows(u, cosine, sine):
    half = HEAD_DIMENSION // 2
    u1, u2 = u[:half], u[half:]
    return jnp.concatenate([u1 * cosine - u2 * sine, u2 * cosine + u1 * sine], axis=0)


def forward_kernel(slots, query_t, cosine, sine, *refs):
    pieces, (out_rows, out_full, out_lse, q_pad, keyval, arrived, top, total, acc) = refs[:-9], refs[-9:]
    copies = start_copies(pieces, keyval, arrived)
    seqs = keyval.shape[1]
    heads = query_t.shape[0] // HEAD_DIMENSION
    width = heads * BLOCK
    blocks = 2 * keyval.shape[0]
    factor = SCORE_SCALE * LOG2E
    low, high = slots[0], blocks - 1 - slots[0]

    for s in range(seqs):
        q_pad[s, HEAD_DIMENSION:, :] = jnp.zeros((HEAD_DIMENSION, 2 * width), jnp.bfloat16)
        for h in range(2):
            for g in range(heads):
                rows = slice(g * HEAD_DIMENSION, (g + 1) * HEAD_DIMENSION)
                at = (s * 2 + h) * BLOCK
                turned = turn_rows(
                    query_t[rows, at : at + BLOCK],
                    cosine[:, h * BLOCK : (h + 1) * BLOCK],
                    sine[:, h * BLOCK : (h + 1) * BLOCK],
                )
                to = h * width + g * BLOCK
                q_pad[s, :HEAD_DIMENSION, to : to + BLOCK] = turned.astype(jnp.bfloat16)
    top[...] = jnp.full(top.shape, MASK_FILL, jnp.float32)
    total[...] = jnp.zeros(total.shape, jnp.float32)
    acc[...] = jnp.zeros(acc.shape, jnp.float32)
    for copy in copies:
        copy.wait()

    def tile(s, start, size, kvs, v_ts, masked):
        cols = slice(start, start + size)
        queries = q_pad[s, :, cols]
        scores = [jnp.dot(kv, queries, preferred_element_type=jnp.float32) for kv in kvs]
        if masked:
            scores = [jnp.where(causal_mask(size), part, MASK_FILL) for part in scores]
        before = top[s, :, cols]
        now = before
        for part in scores:
            now = jnp.maximum(now, jnp.max(part, axis=0, keepdims=True))
        shrink = jnp.exp2((before - now) * factor)
        summed = total[s, :, cols] * shrink
        result = acc[s, :, cols] * shrink
        offset = now * factor
        for part, v_t in zip(scores, v_ts):
            probs = jnp.exp2(part * factor - offset)
            summed = summed + jnp.sum(probs, axis=0, keepdims=True)
            result = result + jnp.dot(v_t, probs.astype(jnp.bfloat16), preferred_element_type=jnp.float32)
        top[s, :, cols] = now
        total[s, :, cols] = summed
        acc[s, :, cols] = result

    def step(blocks_now, low_mode, high_mode):
        for s in range(seqs):
            kvs, v_ts = [], []
            for block in blocks_now:
                half = jnp.where(block >= blocks // 2, 1, 0)
                kv = keyval[slots[1 + block], s, half]
                kvs.append(kv)
                v_ts.append(kv.T[HEAD_DIMENSION:])
            for start, mode in ((0, low_mode), (width, high_mode)):
                if mode:
                    tile(s, start, width, kvs, v_ts, mode == "diagonal")

    @pl.loop(0, low // 2)
    def _(pair):
        step([2 * pair, 2 * pair + 1], "full", "full")

    @pl.when(low % 2 == 1)
    def _():
        step([low - 1], "full", "full")

    step([low], "diagonal", "full")

    @pl.loop(0, (high - low - 1) // 2)
    def _(pair):
        step([low + 1 + 2 * pair, low + 2 + 2 * pair], None, "full")

    step([high], None, "diagonal")

    for s in range(seqs):
        attended = acc[s] / total[s]
        out_full[s] = attended
        out_lse[s] = top[s] * factor + jnp.log2(total[s])
        for h in range(2):
            at = (s * 2 + h) * BLOCK
            parts = [attended[:, h * width + g * BLOCK : h * width + (g + 1) * BLOCK] for g in range(heads)]
            out_rows[at : at + BLOCK] = jnp.concatenate(parts, axis=0).T.astype(jnp.bfloat16)


def start_copies(pieces, keyval, arrived):
    copies = [
        pltpu.make_async_copy(piece, keyval.at[i], arrived.at[i]) for i, piece in enumerate(pieces)
    ]
    for copy in copies:
        copy.start()
    return copies


def attention_forward(slots, query_t, cosine, sine, pieces):
    seqs = pieces[0].shape[0]
    heads = query_t.shape[0] // HEAD_DIMENSION
    cols = 2 * heads * BLOCK
    rows = query_t.shape[1]
    vmem = pl.BlockSpec(memory_space=pltpu.VMEM)
    return pl.pallas_call(
        forward_kernel,
        name="attention_forward",
        out_shape=(
            jax.ShapeDtypeStruct((rows, heads * HEAD_DIMENSION), jnp.bfloat16),
            jax.ShapeDtypeStruct((seqs, HEAD_DIMENSION, cols), jnp.float32),
            jax.ShapeDtypeStruct((seqs, 1, cols), jnp.float32),
            jax.ShapeDtypeStruct((seqs, 2 * HEAD_DIMENSION, cols), jnp.bfloat16),
        ),
        in_specs=[pl.BlockSpec(memory_space=pltpu.SMEM)]
        + [vmem] * 3
        + [pl.BlockSpec(memory_space=pl.ANY)] * len(pieces),
        out_specs=(vmem,) * 4,
        scratch_shapes=[
            pltpu.VMEM((len(pieces),) + pieces[0].shape, jnp.bfloat16),
            pltpu.SemaphoreType.DMA((len(pieces),)),
            pltpu.VMEM((seqs, 1, cols), jnp.float32),
            pltpu.VMEM((seqs, 1, cols), jnp.float32),
            pltpu.VMEM((seqs, HEAD_DIMENSION, cols), jnp.float32),
        ],
        compiler_params=pltpu.CompilerParams(vmem_limit_bytes=VMEM_LIMIT),
        cost_estimate=pl.CostEstimate(flops=6 * 10**9, bytes_accessed=8 * 2**20, transcendentals=9 * 10**6),
    )(slots, query_t, cosine, sine, *pieces)


def backward_kernel(slots, grad_rows, cosine, sine, q_pad, out_full, lse, *refs):
    count = (len(refs) - 10) // 2
    pieces, (grad_query, *out_pieces) = refs[:count], refs[count : 2 * count + 1]
    keyval, arrived, grad_keyval, left, d_pad, q_rows, d_rows, centre, acc = refs[2 * count + 1 :]
    copies = start_copies(pieces, keyval, arrived)
    seqs = keyval.shape[1]
    heads = grad_rows.shape[1] // HEAD_DIMENSION
    width = heads * BLOCK
    blocks = 2 * keyval.shape[0]
    factor = SCORE_SCALE * LOG2E
    low, high = slots[0], blocks - 1 - slots[0]

    for s in range(seqs):
        d_pad[s, :HEAD_DIMENSION, :] = jnp.zeros((HEAD_DIMENSION, 2 * width), jnp.bfloat16)
        for h in range(2):
            at = (s * 2 + h) * BLOCK
            turned = grad_rows[at : at + BLOCK].T
            for g in range(heads):
                to = h * width + g * BLOCK
                d_pad[s, HEAD_DIMENSION:, to : to + BLOCK] = turned[
                    g * HEAD_DIMENSION : (g + 1) * HEAD_DIMENSION
                ]
        centre[s] = jnp.sum(
            d_pad[s, HEAD_DIMENSION:].astype(jnp.float32) * out_full[s], axis=0, keepdims=True
        )
        for to in range(0, 2 * width, BLOCK):
            q_rows[s, to : to + BLOCK, :] = q_pad[s, :, to : to + BLOCK].T
            d_rows[s, to : to + BLOCK, :] = d_pad[s, :, to : to + BLOCK].T
    acc[...] = jnp.zeros(acc.shape, jnp.float32)
    for copy in copies:
        copy.wait()

    def tile(s, start, size, kv, k_t, masked):
        cols = slice(start, start + size)
        scores = jnp.dot(kv, q_pad[s, :, cols], preferred_element_type=jnp.float32)
        probs = jnp.exp2(scores * factor - lse[s, :, cols])
        if masked:
            probs = jnp.where(causal_mask(size), probs, 0.0)
        grad_probs = jnp.dot(kv, d_pad[s, :, cols], preferred_element_type=jnp.float32)
        grad_scores = (probs * (grad_probs - centre[s, :, cols])).astype(jnp.bfloat16)
        acc[s, :, cols] = acc[s, :, cols] + jnp.dot(
            k_t, grad_scores, preferred_element_type=jnp.float32
        )
        return (
            jnp.dot(grad_scores, q_rows[s, cols], preferred_element_type=jnp.float32) * SCORE_SCALE
            + jnp.dot(probs.astype(jnp.bfloat16), d_rows[s, cols], preferred_element_type=jnp.float32)
        )

    def step(block, low_mode, high_mode):
        half = jnp.where(block >= blocks // 2, 1, 0)
        device = slots[1 + block]
        for s in range(seqs):
            kv = keyval[device, s, half]
            k_t = kv.T[:HEAD_DIMENSION]
            summed = None
            for start, mode in ((0, low_mode), (width, high_mode)):
                if mode:
                    part = tile(s, start, width, kv, k_t, mode == "diagonal")
                    summed = part if summed is None else summed + part
            if summed is None:
                summed = jnp.zeros((BLOCK, 2 * HEAD_DIMENSION), jnp.float32)
            grad_keyval[device, s, half] = summed.astype(jnp.bfloat16)

    @pl.loop(0, low)
    def _(block):
        step(block, "full", "full")

    step(low, "diagonal", "full")

    @pl.loop(0, (high - low - 1) // 2)
    def _(pair):
        step(low + 1 + 2 * pair, None, "full")
        step(low + 2 + 2 * pair, None, "full")

    step(high, None, "diagonal")

    @pl.loop(high + 1, blocks)
    def _(block):
        step(block, None, None)

    copies = [
        pltpu.make_async_copy(grad_keyval.at[i], piece, left.at[i]) for i, piece in enumerate(out_pieces)
    ]
    for copy in copies:
        copy.start()
    for s in range(seqs):
        for h in range(2):
            at = (s * 2 + h) * BLOCK
            parts = [
                turn_rows(
                    acc[s, :, h * width + g * BLOCK : h * width + (g + 1) * BLOCK] * SCORE_SCALE,
                    cosine[:, h * BLOCK : (h + 1) * BLOCK],
                    -sine[:, h * BLOCK : (h + 1) * BLOCK],
                )
                for g in range(heads)
            ]
            grad_query[at : at + BLOCK] = jnp.concatenate(parts, axis=0).T.astype(jnp.bfloat16)
    for copy in copies:
        copy.wait()


def attention_backward(slots, grad_rows, cosine, sine, pieces, q_pad, out_full, lse):
    seqs = pieces[0].shape[0]
    cols = q_pad.shape[2]
    count = len(pieces)
    vmem = pl.BlockSpec(memory_space=pltpu.VMEM)
    where = pl.BlockSpec(memory_space=pl.ANY)
    return pl.pallas_call(
        backward_kernel,
        name="attention_backward",
        out_shape=[jax.ShapeDtypeStruct(grad_rows.shape, jnp.bfloat16)]
        + [jax.ShapeDtypeStruct(pieces[0].shape, jnp.bfloat16)] * count,
        in_specs=[pl.BlockSpec(memory_space=pltpu.SMEM)] + [vmem] * 6 + [where] * count,
        out_specs=[vmem] + [where] * count,
        scratch_shapes=[
            pltpu.VMEM((count,) + pieces[0].shape, jnp.bfloat16),
            pltpu.SemaphoreType.DMA((count,)),
            pltpu.VMEM((count,) + pieces[0].shape, jnp.bfloat16),
            pltpu.SemaphoreType.DMA((count,)),
            pltpu.VMEM((seqs, 2 * HEAD_DIMENSION, cols), jnp.bfloat16),
            pltpu.VMEM((seqs, cols, 2 * HEAD_DIMENSION), jnp.bfloat16),
            pltpu.VMEM((seqs, cols, 2 * HEAD_DIMENSION), jnp.bfloat16),
            pltpu.VMEM((seqs, 1, cols), jnp.float32),
            pltpu.VMEM((seqs, HEAD_DIMENSION, cols), jnp.float32),
        ],
        compiler_params=pltpu.CompilerParams(vmem_limit_bytes=VMEM_LIMIT),
        cost_estimate=pl.CostEstimate(flops=20 * 10**9, bytes_accessed=12 * 2**20, transcendentals=9 * 10**6),
    )(slots, grad_rows, cosine, sine, q_pad, out_full, lse, *pieces)


CONTRACT_LAST = (((1,), (1,)), ((), ()))


def select_rows(place, tile_slots):
    slot_at = lax.broadcasted_iota(jnp.int32, (tile_slots, place.shape[1]), 0)
    return slot_at == place


def expert_kernel(grad_at, moe, carried, place, gates, w_in, w_out, kept_in, kept_act, kept_grad, kept_gu, out, back):
    expert = pl.program_id(0)
    tiles, tile_tokens, width = moe.shape
    experts = place.shape[0]
    slots = kept_in.shape[1] // tiles

    x_tiles, g_tiles = [], []
    for j in range(tiles):
        hit = select_rows(place[expert, j], slots)
        pick = jnp.where(hit, 1.0, 0.0).astype(jnp.bfloat16)
        weight = jnp.sum(jnp.where(hit, gates[expert, j], 0.0), axis=1, keepdims=True)
        rows = jnp.dot(pick, moe[j], preferred_element_type=jnp.float32).astype(jnp.bfloat16)
        kept_in[0, j * slots : (j + 1) * slots, :] = rows
        pair = [carried[2 * j + i, grad_at : grad_at + tile_tokens // 2] for i in range(2)]
        rows = jnp.dot(pick, jnp.concatenate(pair, axis=0), preferred_element_type=jnp.float32)
        kept_grad[0, j * slots : (j + 1) * slots, :] = (rows * weight).astype(jnp.bfloat16)
    hidden = w_out.shape[1]
    gate_up = jnp.dot(kept_in[0], w_in[0], preferred_element_type=jnp.float32)
    grad_act = lax.dot_general(
        kept_grad[0], w_out[0], CONTRACT_LAST, preferred_element_type=jnp.float32
    )
    gate, up = gate_up[:, :hidden], gate_up[:, hidden:]
    sigmoid = 1.0 / (1.0 + jnp.exp(-gate))
    silu = gate * sigmoid
    kept_act[0] = (silu * up).astype(jnp.bfloat16)
    kept_gu[0, :, :hidden] = (grad_act * up * (sigmoid * (1.0 + gate * (1.0 - sigmoid)))).astype(jnp.bfloat16)
    kept_gu[0, :, hidden:] = (grad_act * silu).astype(jnp.bfloat16)
    grad_rows = lax.dot_general(
        kept_gu[0], w_in[0], CONTRACT_LAST, preferred_element_type=jnp.float32
    ).astype(jnp.bfloat16)
    for j in range(tiles):
        back[expert, j] = grad_rows[j * slots : (j + 1) * slots]

    @pl.when(expert == experts - 1)
    def _():
        for j in range(tiles):
            scatter_rows(place, [back[e, j] for e in range(experts)], j, slots, out)


def scatter_rows(place, rows, j, slots, out):
    picks = [
        jnp.where(select_rows(place[e, j], slots), 1.0, 0.0) for e in range(len(rows))
    ]
    pick = jnp.concatenate(picks, axis=0).T.astype(jnp.bfloat16)
    stacked = jnp.concatenate(rows, axis=0)
    out[j] = jnp.dot(pick, stacked, preferred_element_type=jnp.float32).astype(jnp.bfloat16)


def expert_pass(grad_at, moe, carried, place, gates, w_in, w_out):
    tiles, tile_tokens, width = moe.shape
    experts, _, hidden2 = w_in.shape
    hidden = hidden2 // 2
    slots = CAP * tile_tokens // 128
    rows = tiles * slots
    whole = pl.BlockSpec(memory_space=pltpu.VMEM)
    each = lambda shape: pl.BlockSpec((1,) + shape, lambda e: (e, 0, 0))
    return pl.pallas_call(
        functools.partial(expert_kernel, grad_at),
        name="expert_pass",
        grid=(experts,),
        out_shape=(
            jax.ShapeDtypeStruct((experts, rows, width), jnp.bfloat16),
            jax.ShapeDtypeStruct((experts, rows, hidden), jnp.bfloat16),
            jax.ShapeDtypeStruct((experts, rows, width), jnp.bfloat16),
            jax.ShapeDtypeStruct((experts, rows, hidden2), jnp.bfloat16),
            jax.ShapeDtypeStruct(moe.shape, jnp.bfloat16),
        ),
        in_specs=[whole] * 4 + [each((width, hidden2)), each((hidden, width))],
        out_specs=(
            each((rows, width)),
            each((rows, hidden)),
            each((rows, width)),
            each((rows, hidden2)),
            whole,
        ),
        scratch_shapes=[pltpu.VMEM((experts, tiles, slots, width), jnp.bfloat16)],
        compiler_params=pltpu.CompilerParams(vmem_limit_bytes=VMEM_LIMIT),
        cost_estimate=pl.CostEstimate(flops=12 * 10**9, bytes_accessed=28 * 2**20, transcendentals=10**6),
    )(moe, carried, place, gates, w_in, w_out)


def weight_kernel(own_z, place, gates, kept_in, kept_act, kept_grad, kept_gu, w_out, out, grads, back):
    expert = pl.program_id(0)
    experts, tiles = place.shape[:2]
    slots = kept_in.shape[1] // tiles
    made = jnp.dot(kept_act[0], w_out[0], preferred_element_type=jnp.float32)
    for j in range(tiles):
        hit = select_rows(place[expert, j], slots)
        weight = jnp.sum(jnp.where(hit, gates[expert, j], 0.0), axis=1, keepdims=True)
        back[expert, j] = (made[j * slots : (j + 1) * slots] * weight).astype(jnp.bfloat16)
    line, _, _, _, width = grads.shape
    in_rows, hidden = kept_in.shape[2] // (2 * line), kept_act.shape[2]
    grad_in = jnp.dot(kept_in[0].T, kept_gu[0], preferred_element_type=jnp.float32)
    grad_in = grad_in.astype(jnp.bfloat16).reshape(2, line, in_rows, width)
    grad_out = jnp.dot(kept_act[0].T, kept_grad[0], preferred_element_type=jnp.float32)
    grad_out = grad_out.astype(jnp.bfloat16).reshape(2, line, hidden // (2 * line), width)
    for z in range(2):
        away = own_z[0] ^ z
        grads[:, away, 0, :in_rows] = grad_in[z]
        grads[:, away, 0, in_rows:] = grad_out[z]

    @pl.when(expert == experts - 1)
    def _():
        for j in range(tiles):
            scatter_rows(place, [back[e, j] for e in range(experts)], j, slots, out)


def weight_pass(own_z, place, gates, kept_in, kept_act, kept_grad, kept_gu, w_out, shares):
    experts, hidden, width = w_out.shape
    tiles = place.shape[1]
    tile_tokens = place.shape[3]
    rows = kept_in.shape[1]
    whole = pl.BlockSpec(memory_space=pltpu.VMEM)
    each = lambda shape: pl.BlockSpec((1,) + shape, lambda e: (e, 0, 0))
    return pl.pallas_call(
        weight_kernel,
        name="weight_pass",
        grid=(experts,),
        out_shape=(
            jax.ShapeDtypeStruct((tiles, tile_tokens, width), jnp.bfloat16),
            jax.ShapeDtypeStruct((shares // 2, 2, experts, (width + hidden) // shares, width), jnp.bfloat16),
        ),
        in_specs=[pl.BlockSpec(memory_space=pltpu.SMEM)]
        + [whole] * 2
        + [each((rows, width)), each((rows, hidden)), each((rows, width)), each((rows, 2 * hidden)), each((hidden, width))],
        out_specs=(
            whole,
            pl.BlockSpec((shares // 2, 2, 1, (width + hidden) // shares, width), lambda e: (0, 0, e, 0, 0)),
        ),
        scratch_shapes=[pltpu.VMEM((experts, tiles, rows // tiles, width), jnp.bfloat16)],
        compiler_params=pltpu.CompilerParams(vmem_limit_bytes=VMEM_LIMIT),
        cost_estimate=pl.CostEstimate(flops=8 * 10**9, bytes_accessed=28 * 2**20, transcendentals=0),
    )(own_z, place, gates, kept_in, kept_act, kept_grad, kept_gu, w_out)

EXPERTS = 32
TOP = 8
SEQUENCE_COUNT = 2
NORM_EPS = 1e-06
ROPE_BASE = 10000.0
META_ROWS = 16

SWAP_CORE = [(c, c ^ 1) for c in range(16)]
SWAP_Z = [(c, c ^ 8) for c in range(16)]
SAME_Z = [list(range(8)), list(range(8, 16))]


def shift_x(step):
    return [(c, ((c // 8) * 4 + (c // 2 % 4 + step) % 4) * 2 + c % 2) for c in range(16)]


def up(values):
    return lax.ppermute(values, "ctx", shift_x(1))


def down(values):
    return lax.ppermute(values, "ctx", shift_x(-1))


def swap_core(values):
    return lax.ppermute(values, "ctx", SWAP_CORE)


def swap_z(values):
    return lax.ppermute(values, "ctx", SWAP_Z)


def wide(values):
    return values.astype(jnp.float32)


def low(values):
    return values.astype(jnp.bfloat16)


def exchange(values, axis):
    return lax.all_to_all(values, axis, split_axis=0, concat_axis=0, tiled=True)


def gather_ep(own):
    return exchange(jnp.broadcast_to(own[None], (lax.axis_size("ep"),) + own.shape), "ep")


def gather_ctx(own):
    z = swap_z(own)
    left, right = up(own), down(own)
    z_left, z_right = up(z), down(z)
    far, z_far = up(left), down(z_right)
    near = [own, z, right, z_right, far, z_far, left, z_left]
    return near + [swap_core(block) for block in near]


def scatter_ctx(parts, others):
    sums = {}
    for k in (4, 5, 3, 6, 2, 7, 1, 0):
        sums[k] = wide(parts[k]) + wide(swap_core(parts[8 + k]))
    far, z_far = up(low(sums[4])), down(low(sums[5]))
    z_right, left = up(low(sums[3])), down(low(sums[6]))
    z_right, left, others = lax.optimization_barrier((z_right, left, others))
    others_z = swap_z(others[1])
    right, z_left = up(low(sums[2] + wide(far))), down(low(sums[7] + wide(z_far)))
    own = sums[0] + wide(right) + wide(left)
    z = sums[1] + wide(z_right) + wide(z_left)
    return own, swap_z(low(z)), others_z, others[0]


def turn_back_kernel(
    first, second, cosine, sine, grad_query, w_query, w_keyval, normed, gain, other_gain, out, payload
):
    half = HEAD_DIMENSION // 2
    lane = lax.broadcasted_iota(jnp.int32, (BLOCK, 2 * HEAD_DIMENSION), 1)
    shares, rows_each, width = payload.shape
    rows_each = out.shape[0] // shares
    per_block = BLOCK // rows_each
    gain_sum = jnp.zeros((1, width), jnp.float32)
    for s in range(first.shape[0]):
        for h in range(2):
            rows = slice(h * BLOCK, (h + 1) * BLOCK)
            u = first[s, h] + second[s, h].astype(jnp.float32)
            after = pltpu.roll(u, 2 * HEAD_DIMENSION - half, 1)
            before = pltpu.roll(u, half, 1)
            turned = jnp.where(lane < half, after, before)
            at = (2 * s + h) * BLOCK
            turned = (u * cosine[rows] + turned * sine[rows]).astype(jnp.bfloat16)
            out[at : at + BLOCK] = turned
            grads = lax.dot_general(turned, w_keyval[...], CONTRACT_LAST, preferred_element_type=jnp.float32)
            grads = grads + lax.dot_general(
                grad_query[at : at + BLOCK], w_query[...], CONTRACT_LAST, preferred_element_type=jnp.float32
            )
            gain_sum = gain_sum + jnp.sum(
                grads * normed[at : at + BLOCK].astype(jnp.float32), axis=0, keepdims=True
            )
            share = (2 * s + h) * per_block
            for i in range(per_block):
                payload[share + i, :rows_each] = grads[i * rows_each : (i + 1) * rows_each].astype(jnp.bfloat16)
    gain_sum = gain_sum / gain[...]
    tail = []
    for part in (gain_sum, other_gain[...]):
        high = part.astype(jnp.bfloat16).astype(jnp.float32)
        tail += [high, part - high]
    tail = jnp.concatenate(tail + [jnp.zeros((META_ROWS - 4, width), jnp.float32)], axis=0)
    for share in range(shares):
        payload[share, rows_each:] = tail.astype(jnp.bfloat16)


def turn_back(first, second, cosine, sine, grad_query, w_query, w_keyval, normed, gain, other_gain):
    vmem = pl.BlockSpec(memory_space=pltpu.VMEM)
    rows, width = normed.shape
    shares = lax.axis_size("ep")
    return pl.pallas_call(
        turn_back_kernel,
        name="turn_back",
        out_shape=(
            jax.ShapeDtypeStruct((rows, 2 * HEAD_DIMENSION), jnp.bfloat16),
            jax.ShapeDtypeStruct((shares, rows // shares + META_ROWS, width), jnp.bfloat16),
        ),
        in_specs=[vmem] * 10,
        out_specs=(vmem,) * 2,
        compiler_params=pltpu.CompilerParams(vmem_limit_bytes=VMEM_LIMIT // 2),
        cost_estimate=pl.CostEstimate(flops=5 * 10**8, bytes_accessed=7 * 2**20, transcendentals=0),
    )(first, second, cosine, sine, grad_query, w_query, w_keyval, normed, gain, other_gain)


def two_terms(values):
    high = low(values)
    return jnp.stack([high, low(values - wide(high))])


def turn_lanes(u, cosine, sine):
    half = HEAD_DIMENSION // 2
    u1, u2 = u[:, :half], u[:, half:]
    return jnp.concatenate([u1 * cosine - u2 * sine, u2 * cosine + u1 * sine], axis=-1)


def body(
    layer_in,
    pair_of,
    routes,
    gate_weights,
    capacity,
    attn_gain,
    query_weight,
    key_value_weight,
    output_weight,
    moe_gain,
    expert_in,
    expert_out,
    out_grad,
):
    tok_rows, width = layer_in.shape
    ep_count = lax.axis_size("ep")
    ctx_count = lax.axis_size("ctx")
    ctx_rows = tok_rows * ep_count
    f32, bf16 = jnp.float32, jnp.bfloat16
    ctx_index = lax.axis_index("ctx")
    ep_index = lax.axis_index("ep")
    head_cols = query_weight.shape[1]
    flat_keyval = key_value_weight.reshape(width, 2 * HEAD_DIMENSION)

    device_ids = jnp.arange(ctx_count, dtype=jnp.int32)
    own_pair = jnp.sum(jnp.where(device_ids == ctx_index, pair_of, 0))
    holder = jnp.sum(jnp.where(pair_of[:, None] == device_ids[None, :], device_ids[:, None], 0), axis=0)
    holder = jnp.concatenate([holder, holder[::-1]])
    relative = (
        ((holder % 2) ^ (ctx_index % 2)) * 8
        + ((holder // 2 % 4 - ctx_index // 2 % 4) % 4) * 2
        + ((holder // 8) ^ (ctx_index // 8))
    )
    slots = jnp.concatenate([own_pair[None], relative]).astype(jnp.int32)
    starts = jnp.stack([own_pair, 2 * ctx_count - 1 - own_pair]) * BLOCK
    own_pos = (starts[:, None] + jnp.arange(BLOCK, dtype=jnp.int32)[None, :]).reshape(2 * BLOCK)
    freqs = ROPE_BASE ** (-2.0 * jnp.arange(HEAD_DIMENSION // 2, dtype=f32) / HEAD_DIMENSION)
    angles = freqs[:, None] * own_pos.astype(f32)[None, :]
    cosine, sine = jnp.cos(angles), jnp.sin(angles)
    cosine_rows = jnp.tile(cosine.T, (SEQUENCE_COUNT, 1))
    sine_rows = jnp.tile(sine.T, (SEQUENCE_COUNT, 1))
    rest = jnp.ones((2 * BLOCK, HEAD_DIMENSION), f32)
    cosine_lanes = jnp.concatenate([cosine.T, cosine.T, rest], axis=1)
    sine_lanes = jnp.concatenate([sine.T, -sine.T, 0.0 * rest], axis=1)

    x_float = layer_in.astype(f32)
    rms_attn = lax.rsqrt(jnp.mean(x_float * x_float, axis=-1, keepdims=True) + NORM_EPS)
    normed = gather_ep((x_float * rms_attn * attn_gain).astype(bf16)).reshape(ctx_rows, width)
    query_t = jnp.einsum("dq,rd->qr", query_weight, normed, preferred_element_type=f32)
    keyval = jnp.dot(normed, flat_keyval, preferred_element_type=f32)
    key = turn_lanes(keyval[:, :HEAD_DIMENSION], cosine_rows, sine_rows)
    keyval_low = jnp.concatenate([key, keyval[:, HEAD_DIMENSION:]], axis=-1).astype(bf16)

    expert_ids = jnp.arange(EXPERTS, dtype=jnp.int32)
    named = routes[:, :, None] == expert_ids
    member = jnp.sum(named.astype(f32), axis=1)
    before = jnp.tril(jnp.ones((tok_rows, tok_rows), bf16), -1)
    rank = jnp.dot(before, member.astype(bf16), preferred_element_type=f32)
    kept = (member > 0) & (rank < capacity.astype(f32)[None, :])
    place = jnp.where(kept, rank, -1.0).T
    gates = jnp.sum(jnp.where(named, gate_weights[:, :, None], 0.0), axis=1).T
    gates_high = gates.astype(bf16)
    gates_low = (gates - gates_high.astype(f32)).astype(bf16)
    meta = jnp.stack([place.astype(bf16), gates_high, gates_low]).reshape(-1, width)
    meta = jnp.pad(meta, ((0, META_ROWS - meta.shape[0]), (0, 0)))
    carried = jnp.concatenate([output_weight, out_grad, meta], axis=0)
    keyval_low, carried = lax.optimization_barrier((keyval_low, carried))
    carried_all = lax.all_gather(carried, "ep", axis=0)
    pieces = gather_ctx(keyval_low.reshape(SEQUENCE_COUNT, 2, BLOCK, 2 * HEAD_DIMENSION))
    attended, attended_full, lse, query_pad = attention_forward(slots, query_t, cosine, sine, pieces)

    merged = exchange(attended.reshape(ep_count, tok_rows, head_cols), "ep")
    projection = carried_all[:, :head_cols].reshape(ep_count * head_cols, width)
    merged = merged.transpose(1, 0, 2).reshape(tok_rows, ep_count * head_cols)
    residual = x_float + jnp.dot(merged, projection, preferred_element_type=f32)
    rms_moe = lax.rsqrt(jnp.mean(residual * residual, axis=-1, keepdims=True) + NORM_EPS)
    moe_in = gather_ep((residual * rms_moe * moe_gain).astype(bf16))

    tiles = ep_count // 2
    tile_tokens = 2 * tok_rows
    local_experts = expert_in.shape[0]
    meta_at = head_cols + tok_rows
    meta_all = carried_all[:, meta_at : meta_at + 3 * EXPERTS * tok_rows // width]
    meta_all = meta_all.reshape(tiles, 2, 3, EXPERTS, tok_rows)
    meta_all = wide(lax.dynamic_slice_in_dim(meta_all, ep_index * local_experts, local_experts, axis=3))
    place_all = meta_all[:, :, 0].astype(jnp.int32)
    place_all = jnp.where(place_all >= 0, place_all + jnp.arange(2, dtype=jnp.int32)[None, :, None, None] * CAP, -1)
    gates_all = meta_all[:, :, 1] + meta_all[:, :, 2]
    by_expert = lambda v: v.transpose(2, 0, 1, 3).reshape(local_experts, tiles, 1, tile_tokens)
    place_all, gates_all = by_expert(place_all), by_expert(gates_all)
    kept_in, kept_act, kept_grad, kept_gu, grad_moe = expert_pass(
        head_cols, moe_in.reshape(tiles, tile_tokens, width), carried_all, place_all, gates_all, expert_in, expert_out
    )
    grad_moe_in = jnp.sum(wide(exchange(grad_moe.reshape(ep_count, tok_rows, width), "ep")), axis=0)
    made, expert_grads = weight_pass(
        (ctx_index // 8)[None].astype(jnp.int32), place_all, gates_all, kept_in, kept_act, kept_grad, kept_gu, expert_out, ctx_count
    )

    expert_grads, grad_moe_in = lax.optimization_barrier((expert_grads, grad_moe_in))

    grad_top = out_grad.astype(f32)
    scaled = grad_moe_in * moe_gain
    moe_gain_part = jnp.sum(grad_moe_in * residual * rms_moe, axis=0)
    inner = jnp.mean(scaled * residual, axis=-1, keepdims=True)
    grad_res = grad_top + rms_moe * scaled - residual * (rms_moe * rms_moe * rms_moe) * inner
    grad_attn = grad_res.astype(bf16)

    grad_att = lax.dot_general(
        grad_attn, projection, (((1,), (1,)), ((), ())), preferred_element_type=f32
    ).astype(bf16)
    grad_att = grad_att.reshape(tok_rows, ep_count, head_cols).transpose(1, 0, 2)
    grad_att = exchange(grad_att, "ep").reshape(ctx_rows, head_cols)
    output_grad = lax.dot_general(
        merged, grad_attn, (((0,), (0,)), ((), ())), preferred_element_type=f32
    ).astype(bf16)
    expert_grads = lax.psum_scatter(
        expert_grads, "ctx", scatter_dimension=0, tiled=True, axis_index_groups=SAME_Z
    )[0]
    made, grad_att = lax.optimization_barrier((made, grad_att))
    made = exchange(made.reshape(ep_count, tok_rows, width), "ep")
    grad_query, *grad_pieces = attention_backward(
        slots, grad_att, cosine, sine, pieces, query_pad, attended_full, lse
    )
    made, output_grad, *grad_pieces = lax.optimization_barrier((made, output_grad, *grad_pieces))
    output_grad = exchange(output_grad.reshape(ep_count, head_cols, width), "ep")
    query_grad = jnp.einsum("rd,rq->dq", normed, grad_query, preferred_element_type=f32)
    own, from_z, others_z, expert_grads = scatter_ctx(grad_pieces, expert_grads)
    query_grad, output_grad, others_z, own, from_z = lax.optimization_barrier(
        (query_grad, output_grad, others_z, own, from_z)
    )
    grad_kv_low, payload = turn_back(
        own, from_z, cosine_lanes, sine_lanes, grad_query, query_weight, flat_keyval,
        normed, attn_gain[None], moe_gain_part[None],
    )
    payload = exchange(payload, "ep")

    keyval_grad = jnp.einsum("rd,rk->dk", normed, grad_kv_low, preferred_element_type=f32)
    in_rows = width // ctx_count
    extra = jnp.sum(wide(payload[:, tok_rows:]), axis=0)
    gains = two_terms(jnp.stack([extra[0] + extra[1], extra[2] + extra[3]])).reshape(-1, head_cols)
    output_grad = low(jnp.sum(wide(output_grad), axis=0)).T
    small = jnp.stack([low(query_grad), low(keyval_grad), output_grad]).reshape(3, ctx_count, in_rows, head_cols)
    small = small.transpose(1, 0, 2, 3).reshape(ctx_count, -1, head_cols)
    small = jnp.concatenate([small, jnp.broadcast_to(gains[None], (ctx_count,) + gains.shape)], axis=1)
    small = jnp.sum(wide(exchange(small, "ctx")), axis=0)
    gains = small[3 * in_rows :].reshape(2, 2, width)
    gains = gains[0] + gains[1]
    small = small[: 3 * in_rows].reshape(3, in_rows, head_cols)
    expert_grads = wide(expert_grads) + wide(others_z)
    grad_normed = jnp.sum(wide(payload[:, :tok_rows]), axis=0)
    scaled = grad_normed * attn_gain
    inner = jnp.mean(scaled * x_float, axis=-1, keepdims=True)
    input_grad = grad_res + rms_attn * scaled - x_float * (rms_attn * rms_attn * rms_attn) * inner
    layer_out = (residual + jnp.sum(wide(made), axis=0)).astype(bf16)
    return (
        layer_out,
        input_grad,
        gains[0],
        small[0],
        small[1].reshape(in_rows, 1, 2 * HEAD_DIMENSION),
        small[2].T,
        gains[1],
        expert_grads[:, :in_rows],
        expert_grads[:, in_rows:],
    )


def solution(mesh):
    in_specs = (
        P(("ctx", "ep"), None),
        P(),
        P(("ctx", "ep"), None),
        P(("ctx", "ep"), None),
        P(),
        P(),
        P(None, "ep"),
        P(None, "ep", None),
        P("ep", None),
        P(),
        P("ep", None, None),
        P("ep", None, None),
        P(("ctx", "ep"), None),
    )
    out_specs = (
        P(("ctx", "ep"), None),
        P(("ctx", "ep"), None),
        P(),
        P("ctx", "ep"),
        P("ctx", "ep", None),
        P("ep", "ctx"),
        P(),
        P("ep", "ctx", None),
        P("ep", "ctx", None),
    )
    return jax.shard_map(body, mesh=mesh, in_specs=in_specs, out_specs=out_specs, check_vma=False)
```

```python
import functools

import jax
import jax.numpy as jnp
from jax import lax
from jax.experimental import pallas as pl
from jax.experimental.pallas import tpu as pltpu
from jax.sharding import PartitionSpec as P

VMEM_LIMIT = 56 * 1024 * 1024
CAP = 48

HEAD_DIMENSION = 64
SCORE_SCALE = 1.0 / 64.0
MASK_FILL = -1e30
LOG2E = 1.4426950408889634
BLOCK = 256


def causal_mask(width):
    key_at = lax.broadcasted_iota(jnp.int32, (BLOCK, width), 0)
    query_at = lax.broadcasted_iota(jnp.int32, (BLOCK, width), 1) % BLOCK
    return key_at <= query_at


def turn_rows(u, cosine, sine):
    half = HEAD_DIMENSION // 2
    u1, u2 = u[:half], u[half:]
    return jnp.concatenate([u1 * cosine - u2 * sine, u2 * cosine + u1 * sine], axis=0)


def forward_kernel(slots, query_t, cosine, sine, *refs):
    pieces, (out_rows, out_full, out_lse, q_pad, keyval, arrived, top, total, acc) = refs[:-9], refs[-9:]
    copies = start_copies(pieces, keyval, arrived)
    seqs = keyval.shape[1]
    heads = query_t.shape[0] // HEAD_DIMENSION
    width = heads * BLOCK
    blocks = 2 * keyval.shape[0]
    factor = SCORE_SCALE * LOG2E
    low, high = slots[0], blocks - 1 - slots[0]

    for s in range(seqs):
        q_pad[s, HEAD_DIMENSION:, :] = jnp.zeros((HEAD_DIMENSION, 2 * width), jnp.bfloat16)
        for h in range(2):
            for g in range(heads):
                rows = slice(g * HEAD_DIMENSION, (g + 1) * HEAD_DIMENSION)
                at = (s * 2 + h) * BLOCK
                turned = turn_rows(
                    query_t[rows, at : at + BLOCK],
                    cosine[:, h * BLOCK : (h + 1) * BLOCK],
                    sine[:, h * BLOCK : (h + 1) * BLOCK],
                )
                to = h * width + g * BLOCK
                q_pad[s, :HEAD_DIMENSION, to : to + BLOCK] = turned.astype(jnp.bfloat16)
    top[...] = jnp.full(top.shape, MASK_FILL, jnp.float32)
    total[...] = jnp.zeros(total.shape, jnp.float32)
    acc[...] = jnp.zeros(acc.shape, jnp.float32)
    for copy in copies:
        copy.wait()

    def tile(s, start, size, kvs, v_ts, masked):
        cols = slice(start, start + size)
        queries = q_pad[s, :, cols]
        scores = [jnp.dot(kv, queries, preferred_element_type=jnp.float32) for kv in kvs]
        if masked:
            scores = [jnp.where(causal_mask(size), part, MASK_FILL) for part in scores]
        before = top[s, :, cols]
        now = before
        for part in scores:
            now = jnp.maximum(now, jnp.max(part, axis=0, keepdims=True))
        shrink = jnp.exp2((before - now) * factor)
        summed = total[s, :, cols] * shrink
        result = acc[s, :, cols] * shrink
        offset = now * factor
        for part, v_t in zip(scores, v_ts):
            probs = jnp.exp2(part * factor - offset)
            summed = summed + jnp.sum(probs, axis=0, keepdims=True)
            result = result + jnp.dot(v_t, probs.astype(jnp.bfloat16), preferred_element_type=jnp.float32)
        top[s, :, cols] = now
        total[s, :, cols] = summed
        acc[s, :, cols] = result

    def step(blocks_now, low_mode, high_mode):
        for s in range(seqs):
            kvs, v_ts = [], []
            for block in blocks_now:
                half = jnp.where(block >= blocks // 2, 1, 0)
                kv = keyval[slots[1 + block], s, half]
                kvs.append(kv)
                v_ts.append(kv.T[HEAD_DIMENSION:])
            for start, mode in ((0, low_mode), (width, high_mode)):
                if mode:
                    tile(s, start, width, kvs, v_ts, mode == "diagonal")

    @pl.loop(0, low // 2)
    def _(pair):
        step([2 * pair, 2 * pair + 1], "full", "full")

    @pl.when(low % 2 == 1)
    def _():
        step([low - 1], "full", "full")

    step([low], "diagonal", "full")

    @pl.loop(0, (high - low - 1) // 2)
    def _(pair):
        step([low + 1 + 2 * pair, low + 2 + 2 * pair], None, "full")

    step([high], None, "diagonal")

    for s in range(seqs):
        attended = acc[s] / total[s]
        out_full[s] = attended
        out_lse[s] = top[s] * factor + jnp.log2(total[s])
        for h in range(2):
            at = (s * 2 + h) * BLOCK
            parts = [attended[:, h * width + g * BLOCK : h * width + (g + 1) * BLOCK] for g in range(heads)]
            out_rows[at : at + BLOCK] = jnp.concatenate(parts, axis=0).T.astype(jnp.bfloat16)


def start_copies(pieces, keyval, arrived):
    copies = [
        pltpu.make_async_copy(piece, keyval.at[i], arrived.at[i]) for i, piece in enumerate(pieces)
    ]
    for copy in copies:
        copy.start()
    return copies


def attention_forward(slots, query_t, cosine, sine, pieces):
    seqs = pieces[0].shape[0]
    heads = query_t.shape[0] // HEAD_DIMENSION
    cols = 2 * heads * BLOCK
    rows = query_t.shape[1]
    vmem = pl.BlockSpec(memory_space=pltpu.VMEM)
    return pl.pallas_call(
        forward_kernel,
        name="attention_forward",
        out_shape=(
            jax.ShapeDtypeStruct((rows, heads * HEAD_DIMENSION), jnp.bfloat16),
            jax.ShapeDtypeStruct((seqs, HEAD_DIMENSION, cols), jnp.float32),
            jax.ShapeDtypeStruct((seqs, 1, cols), jnp.float32),
            jax.ShapeDtypeStruct((seqs, 2 * HEAD_DIMENSION, cols), jnp.bfloat16),
        ),
        in_specs=[pl.BlockSpec(memory_space=pltpu.SMEM)]
        + [vmem] * 3
        + [pl.BlockSpec(memory_space=pl.ANY)] * len(pieces),
        out_specs=(vmem,) * 4,
        scratch_shapes=[
            pltpu.VMEM((len(pieces),) + pieces[0].shape, jnp.bfloat16),
            pltpu.SemaphoreType.DMA((len(pieces),)),
            pltpu.VMEM((seqs, 1, cols), jnp.float32),
            pltpu.VMEM((seqs, 1, cols), jnp.float32),
            pltpu.VMEM((seqs, HEAD_DIMENSION, cols), jnp.float32),
        ],
        compiler_params=pltpu.CompilerParams(vmem_limit_bytes=VMEM_LIMIT),
        cost_estimate=pl.CostEstimate(flops=6 * 10**9, bytes_accessed=8 * 2**20, transcendentals=9 * 10**6),
    )(slots, query_t, cosine, sine, *pieces)


def backward_kernel(slots, grad_rows, cosine, sine, q_pad, out_full, lse, *refs):
    count = (len(refs) - 10) // 2
    pieces, (grad_query, *out_pieces) = refs[:count], refs[count : 2 * count + 1]
    keyval, arrived, grad_keyval, left, d_pad, q_rows, d_rows, centre, acc = refs[2 * count + 1 :]
    copies = start_copies(pieces, keyval, arrived)
    seqs = keyval.shape[1]
    heads = grad_rows.shape[1] // HEAD_DIMENSION
    width = heads * BLOCK
    blocks = 2 * keyval.shape[0]
    factor = SCORE_SCALE * LOG2E
    low, high = slots[0], blocks - 1 - slots[0]

    for s in range(seqs):
        d_pad[s, :HEAD_DIMENSION, :] = jnp.zeros((HEAD_DIMENSION, 2 * width), jnp.bfloat16)
        for h in range(2):
            at = (s * 2 + h) * BLOCK
            turned = grad_rows[at : at + BLOCK].T
            for g in range(heads):
                to = h * width + g * BLOCK
                d_pad[s, HEAD_DIMENSION:, to : to + BLOCK] = turned[
                    g * HEAD_DIMENSION : (g + 1) * HEAD_DIMENSION
                ]
        centre[s] = jnp.sum(
            d_pad[s, HEAD_DIMENSION:].astype(jnp.float32) * out_full[s], axis=0, keepdims=True
        )
        for to in range(0, 2 * width, BLOCK):
            q_rows[s, to : to + BLOCK, :] = q_pad[s, :, to : to + BLOCK].T
            d_rows[s, to : to + BLOCK, :] = d_pad[s, :, to : to + BLOCK].T
    acc[...] = jnp.zeros(acc.shape, jnp.float32)
    for copy in copies:
        copy.wait()

    def tile(s, start, size, kv, k_t, masked):
        cols = slice(start, start + size)
        scores = jnp.dot(kv, q_pad[s, :, cols], preferred_element_type=jnp.float32)
        probs = jnp.exp2(scores * factor - lse[s, :, cols])
        if masked:
            probs = jnp.where(causal_mask(size), probs, 0.0)
        grad_probs = jnp.dot(kv, d_pad[s, :, cols], preferred_element_type=jnp.float32)
        grad_scores = (probs * (grad_probs - centre[s, :, cols])).astype(jnp.bfloat16)
        acc[s, :, cols] = acc[s, :, cols] + jnp.dot(
            k_t, grad_scores, preferred_element_type=jnp.float32
        )
        return (
            jnp.dot(grad_scores, q_rows[s, cols], preferred_element_type=jnp.float32) * SCORE_SCALE
            + jnp.dot(probs.astype(jnp.bfloat16), d_rows[s, cols], preferred_element_type=jnp.float32)
        )

    def step(block, low_mode, high_mode):
        half = jnp.where(block >= blocks // 2, 1, 0)
        device = slots[1 + block]
        for s in range(seqs):
            kv = keyval[device, s, half]
            k_t = kv.T[:HEAD_DIMENSION]
            summed = None
            for start, mode in ((0, low_mode), (width, high_mode)):
                if mode:
                    part = tile(s, start, width, kv, k_t, mode == "diagonal")
                    summed = part if summed is None else summed + part
            if summed is None:
                summed = jnp.zeros((BLOCK, 2 * HEAD_DIMENSION), jnp.float32)
            grad_keyval[device, s, half] = summed.astype(jnp.bfloat16)

    @pl.loop(0, low)
    def _(block):
        step(block, "full", "full")

    step(low, "diagonal", "full")

    @pl.loop(0, (high - low - 1) // 2)
    def _(pair):
        step(low + 1 + 2 * pair, None, "full")
        step(low + 2 + 2 * pair, None, "full")

    step(high, None, "diagonal")

    @pl.loop(high + 1, blocks)
    def _(block):
        step(block, None, None)

    copies = [
        pltpu.make_async_copy(grad_keyval.at[i], piece, left.at[i]) for i, piece in enumerate(out_pieces)
    ]
    for copy in copies:
        copy.start()
    for s in range(seqs):
        for h in range(2):
            at = (s * 2 + h) * BLOCK
            parts = [
                turn_rows(
                    acc[s, :, h * width + g * BLOCK : h * width + (g + 1) * BLOCK] * SCORE_SCALE,
                    cosine[:, h * BLOCK : (h + 1) * BLOCK],
                    -sine[:, h * BLOCK : (h + 1) * BLOCK],
                )
                for g in range(heads)
            ]
            grad_query[at : at + BLOCK] = jnp.concatenate(parts, axis=0).T.astype(jnp.bfloat16)
    for copy in copies:
        copy.wait()


def attention_backward(slots, grad_rows, cosine, sine, pieces, q_pad, out_full, lse):
    seqs = pieces[0].shape[0]
    cols = q_pad.shape[2]
    count = len(pieces)
    vmem = pl.BlockSpec(memory_space=pltpu.VMEM)
    where = pl.BlockSpec(memory_space=pl.ANY)
    return pl.pallas_call(
        backward_kernel,
        name="attention_backward",
        out_shape=[jax.ShapeDtypeStruct(grad_rows.shape, jnp.bfloat16)]
        + [jax.ShapeDtypeStruct(pieces[0].shape, jnp.bfloat16)] * count,
        in_specs=[pl.BlockSpec(memory_space=pltpu.SMEM)] + [vmem] * 6 + [where] * count,
        out_specs=[vmem] + [where] * count,
        scratch_shapes=[
            pltpu.VMEM((count,) + pieces[0].shape, jnp.bfloat16),
            pltpu.SemaphoreType.DMA((count,)),
            pltpu.VMEM((count,) + pieces[0].shape, jnp.bfloat16),
            pltpu.SemaphoreType.DMA((count,)),
            pltpu.VMEM((seqs, 2 * HEAD_DIMENSION, cols), jnp.bfloat16),
            pltpu.VMEM((seqs, cols, 2 * HEAD_DIMENSION), jnp.bfloat16),
            pltpu.VMEM((seqs, cols, 2 * HEAD_DIMENSION), jnp.bfloat16),
            pltpu.VMEM((seqs, 1, cols), jnp.float32),
            pltpu.VMEM((seqs, HEAD_DIMENSION, cols), jnp.float32),
        ],
        compiler_params=pltpu.CompilerParams(vmem_limit_bytes=VMEM_LIMIT),
        cost_estimate=pl.CostEstimate(flops=20 * 10**9, bytes_accessed=12 * 2**20, transcendentals=9 * 10**6),
    )(slots, grad_rows, cosine, sine, q_pad, out_full, lse, *pieces)


CONTRACT_LAST = (((1,), (1,)), ((), ()))


def select_rows(place, tile_slots):
    slot_at = lax.broadcasted_iota(jnp.int32, (tile_slots, place.shape[1]), 0)
    return slot_at == place


def expert_kernel(grad_at, moe, carried, place, gates, w_in, w_out, kept_in, kept_act, kept_grad, kept_gu, out, back):
    expert = pl.program_id(0)
    tiles, tile_tokens, width = moe.shape
    experts = place.shape[0]
    slots = kept_in.shape[1] // tiles

    x_tiles, g_tiles = [], []
    for j in range(tiles):
        hit = select_rows(place[expert, j], slots)
        pick = jnp.where(hit, 1.0, 0.0).astype(jnp.bfloat16)
        weight = jnp.sum(jnp.where(hit, gates[expert, j], 0.0), axis=1, keepdims=True)
        rows = jnp.dot(pick, moe[j], preferred_element_type=jnp.float32).astype(jnp.bfloat16)
        kept_in[0, j * slots : (j + 1) * slots, :] = rows
        pair = [carried[2 * j + i, grad_at : grad_at + tile_tokens // 2] for i in range(2)]
        rows = jnp.dot(pick, jnp.concatenate(pair, axis=0), preferred_element_type=jnp.float32)
        kept_grad[0, j * slots : (j + 1) * slots, :] = (rows * weight).astype(jnp.bfloat16)
    hidden = w_out.shape[1]
    gate_up = jnp.dot(kept_in[0], w_in[0], preferred_element_type=jnp.float32)
    grad_act = lax.dot_general(
        kept_grad[0], w_out[0], CONTRACT_LAST, preferred_element_type=jnp.float32
    )
    gate, up = gate_up[:, :hidden], gate_up[:, hidden:]
    sigmoid = 1.0 / (1.0 + jnp.exp(-gate))
    silu = gate * sigmoid
    kept_act[0] = (silu * up).astype(jnp.bfloat16)
    kept_gu[0, :, :hidden] = (grad_act * up * (sigmoid * (1.0 + gate * (1.0 - sigmoid)))).astype(jnp.bfloat16)
    kept_gu[0, :, hidden:] = (grad_act * silu).astype(jnp.bfloat16)
    grad_rows = lax.dot_general(
        kept_gu[0], w_in[0], CONTRACT_LAST, preferred_element_type=jnp.float32
    ).astype(jnp.bfloat16)
    for j in range(tiles):
        back[expert, j] = grad_rows[j * slots : (j + 1) * slots]

    @pl.when(expert == experts - 1)
    def _():
        for j in range(tiles):
            scatter_rows(place, [back[e, j] for e in range(experts)], j, slots, out)


def scatter_rows(place, rows, j, slots, out):
    picks = [
        jnp.where(select_rows(place[e, j], slots), 1.0, 0.0) for e in range(len(rows))
    ]
    pick = jnp.concatenate(picks, axis=0).T.astype(jnp.bfloat16)
    stacked = jnp.concatenate(rows, axis=0)
    out[j] = jnp.dot(pick, stacked, preferred_element_type=jnp.float32).astype(jnp.bfloat16)


def expert_pass(grad_at, moe, carried, place, gates, w_in, w_out):
    tiles, tile_tokens, width = moe.shape
    experts, _, hidden2 = w_in.shape
    hidden = hidden2 // 2
    slots = CAP * tile_tokens // 128
    rows = tiles * slots
    whole = pl.BlockSpec(memory_space=pltpu.VMEM)
    each = lambda shape: pl.BlockSpec((1,) + shape, lambda e: (e, 0, 0))
    return pl.pallas_call(
        functools.partial(expert_kernel, grad_at),
        name="expert_pass",
        grid=(experts,),
        out_shape=(
            jax.ShapeDtypeStruct((experts, rows, width), jnp.bfloat16),
            jax.ShapeDtypeStruct((experts, rows, hidden), jnp.bfloat16),
            jax.ShapeDtypeStruct((experts, rows, width), jnp.bfloat16),
            jax.ShapeDtypeStruct((experts, rows, hidden2), jnp.bfloat16),
            jax.ShapeDtypeStruct(moe.shape, jnp.bfloat16),
        ),
        in_specs=[whole] * 4 + [each((width, hidden2)), each((hidden, width))],
        out_specs=(
            each((rows, width)),
            each((rows, hidden)),
            each((rows, width)),
            each((rows, hidden2)),
            whole,
        ),
        scratch_shapes=[pltpu.VMEM((experts, tiles, slots, width), jnp.bfloat16)],
        compiler_params=pltpu.CompilerParams(vmem_limit_bytes=VMEM_LIMIT),
        cost_estimate=pl.CostEstimate(flops=12 * 10**9, bytes_accessed=28 * 2**20, transcendentals=10**6),
    )(moe, carried, place, gates, w_in, w_out)


def weight_kernel(own_z, place, gates, kept_in, kept_act, kept_grad, kept_gu, w_out, out, grads, back):
    expert = pl.program_id(0)
    experts, tiles = place.shape[:2]
    slots = kept_in.shape[1] // tiles
    made = jnp.dot(kept_act[0], w_out[0], preferred_element_type=jnp.float32)
    for j in range(tiles):
        hit = select_rows(place[expert, j], slots)
        weight = jnp.sum(jnp.where(hit, gates[expert, j], 0.0), axis=1, keepdims=True)
        back[expert, j] = (made[j * slots : (j + 1) * slots] * weight).astype(jnp.bfloat16)
    line, _, _, _, width = grads.shape
    in_rows, hidden = kept_in.shape[2] // (2 * line), kept_act.shape[2]
    grad_in = jnp.dot(kept_in[0].T, kept_gu[0], preferred_element_type=jnp.float32)
    grad_in = grad_in.astype(jnp.bfloat16).reshape(2, line, in_rows, width)
    grad_out = jnp.dot(kept_act[0].T, kept_grad[0], preferred_element_type=jnp.float32)
    grad_out = grad_out.astype(jnp.bfloat16).reshape(2, line, hidden // (2 * line), width)
    for z in range(2):
        away = own_z[0] ^ z
        grads[:, away, 0, :in_rows] = grad_in[z]
        grads[:, away, 0, in_rows:] = grad_out[z]

    @pl.when(expert == experts - 1)
    def _():
        for j in range(tiles):
            scatter_rows(place, [back[e, j] for e in range(experts)], j, slots, out)


def weight_pass(own_z, place, gates, kept_in, kept_act, kept_grad, kept_gu, w_out, shares):
    experts, hidden, width = w_out.shape
    tiles = place.shape[1]
    tile_tokens = place.shape[3]
    rows = kept_in.shape[1]
    whole = pl.BlockSpec(memory_space=pltpu.VMEM)
    each = lambda shape: pl.BlockSpec((1,) + shape, lambda e: (e, 0, 0))
    return pl.pallas_call(
        weight_kernel,
        name="weight_pass",
        grid=(experts,),
        out_shape=(
            jax.ShapeDtypeStruct((tiles, tile_tokens, width), jnp.bfloat16),
            jax.ShapeDtypeStruct((shares // 2, 2, experts, (width + hidden) // shares, width), jnp.bfloat16),
        ),
        in_specs=[pl.BlockSpec(memory_space=pltpu.SMEM)]
        + [whole] * 2
        + [each((rows, width)), each((rows, hidden)), each((rows, width)), each((rows, 2 * hidden)), each((hidden, width))],
        out_specs=(
            whole,
            pl.BlockSpec((shares // 2, 2, 1, (width + hidden) // shares, width), lambda e: (0, 0, e, 0, 0)),
        ),
        scratch_shapes=[pltpu.VMEM((experts, tiles, rows // tiles, width), jnp.bfloat16)],
        compiler_params=pltpu.CompilerParams(vmem_limit_bytes=VMEM_LIMIT),
        cost_estimate=pl.CostEstimate(flops=8 * 10**9, bytes_accessed=28 * 2**20, transcendentals=0),
    )(own_z, place, gates, kept_in, kept_act, kept_grad, kept_gu, w_out)

EXPERTS = 32
TOP = 8
SEQUENCE_COUNT = 2
NORM_EPS = 1e-06
ROPE_BASE = 10000.0
META_ROWS = 16

SWAP_CORE = [(c, c ^ 1) for c in range(16)]
SWAP_Z = [(c, c ^ 8) for c in range(16)]
SAME_Z = [list(range(8)), list(range(8, 16))]


def shift_x(step):
    return [(c, ((c // 8) * 4 + (c // 2 % 4 + step) % 4) * 2 + c % 2) for c in range(16)]


def up(values):
    return lax.ppermute(values, "ctx", shift_x(1))


def down(values):
    return lax.ppermute(values, "ctx", shift_x(-1))


def swap_core(values):
    return lax.ppermute(values, "ctx", SWAP_CORE)


def swap_z(values):
    return lax.ppermute(values, "ctx", SWAP_Z)


def wide(values):
    return values.astype(jnp.float32)


def low(values):
    return values.astype(jnp.bfloat16)


def exchange(values, axis):
    return lax.all_to_all(values, axis, split_axis=0, concat_axis=0, tiled=True)


def gather_ep(own):
    return exchange(jnp.broadcast_to(own[None], (lax.axis_size("ep"),) + own.shape), "ep")


def gather_ctx(own):
    z = swap_z(own)
    left, right = up(own), down(own)
    z_left, z_right = up(z), down(z)
    far, z_far = up(left), down(z_right)
    near = [own, z, right, z_right, far, z_far, left, z_left]
    return near + [swap_core(block) for block in near]


def scatter_ctx(parts, others):
    sums = {}
    for k in (4, 5, 3, 6, 2, 7, 1, 0):
        sums[k] = wide(parts[k]) + wide(swap_core(parts[8 + k]))
    far, z_far = up(low(sums[4])), down(low(sums[5]))
    z_right, left = up(low(sums[3])), down(low(sums[6]))
    sums[2], sums[7], others = lax.optimization_barrier((sums[2], sums[7], others))
    others_z = swap_z(others[1])
    right, z_left = up(low(sums[2] + wide(far))), down(low(sums[7] + wide(z_far)))
    own = sums[0] + wide(right) + wide(left)
    z = sums[1] + wide(z_right) + wide(z_left)
    return own, swap_z(low(z)), others_z, others[0]


def turn_back_kernel(
    first, second, cosine, sine, grad_query, w_query, w_keyval, normed, gain, other_gain, out, payload
):
    half = HEAD_DIMENSION // 2
    lane = lax.broadcasted_iota(jnp.int32, (BLOCK, 2 * HEAD_DIMENSION), 1)
    shares, rows_each, width = payload.shape
    rows_each = out.shape[0] // shares
    per_block = BLOCK // rows_each
    gain_sum = jnp.zeros((1, width), jnp.float32)
    for s in range(first.shape[0]):
        for h in range(2):
            rows = slice(h * BLOCK, (h + 1) * BLOCK)
            u = first[s, h] + second[s, h].astype(jnp.float32)
            after = pltpu.roll(u, 2 * HEAD_DIMENSION - half, 1)
            before = pltpu.roll(u, half, 1)
            turned = jnp.where(lane < half, after, before)
            at = (2 * s + h) * BLOCK
            turned = (u * cosine[rows] + turned * sine[rows]).astype(jnp.bfloat16)
            out[at : at + BLOCK] = turned
            grads = lax.dot_general(turned, w_keyval[...], CONTRACT_LAST, preferred_element_type=jnp.float32)
            grads = grads + lax.dot_general(
                grad_query[at : at + BLOCK], w_query[...], CONTRACT_LAST, preferred_element_type=jnp.float32
            )
            gain_sum = gain_sum + jnp.sum(
                grads * normed[at : at + BLOCK].astype(jnp.float32), axis=0, keepdims=True
            )
            share = (2 * s + h) * per_block
            for i in range(per_block):
                payload[share + i, :rows_each] = grads[i * rows_each : (i + 1) * rows_each].astype(jnp.bfloat16)
    gain_sum = gain_sum / gain[...]
    tail = []
    for part in (gain_sum, other_gain[...]):
        high = part.astype(jnp.bfloat16).astype(jnp.float32)
        tail += [high, part - high]
    tail = jnp.concatenate(tail + [jnp.zeros((META_ROWS - 4, width), jnp.float32)], axis=0)
    for share in range(shares):
        payload[share, rows_each:] = tail.astype(jnp.bfloat16)


def turn_back(first, second, cosine, sine, grad_query, w_query, w_keyval, normed, gain, other_gain):
    vmem = pl.BlockSpec(memory_space=pltpu.VMEM)
    rows, width = normed.shape
    shares = lax.axis_size("ep")
    return pl.pallas_call(
        turn_back_kernel,
        name="turn_back",
        out_shape=(
            jax.ShapeDtypeStruct((rows, 2 * HEAD_DIMENSION), jnp.bfloat16),
            jax.ShapeDtypeStruct((shares, rows // shares + META_ROWS, width), jnp.bfloat16),
        ),
        in_specs=[vmem] * 10,
        out_specs=(vmem,) * 2,
        compiler_params=pltpu.CompilerParams(vmem_limit_bytes=VMEM_LIMIT // 2),
        cost_estimate=pl.CostEstimate(flops=5 * 10**8, bytes_accessed=7 * 2**20, transcendentals=0),
    )(first, second, cosine, sine, grad_query, w_query, w_keyval, normed, gain, other_gain)


def two_terms(values):
    high = low(values)
    return jnp.stack([high, low(values - wide(high))])


def turn_lanes(u, cosine, sine):
    half = HEAD_DIMENSION // 2
    u1, u2 = u[:, :half], u[:, half:]
    return jnp.concatenate([u1 * cosine - u2 * sine, u2 * cosine + u1 * sine], axis=-1)


def body(
    layer_in,
    pair_of,
    routes,
    gate_weights,
    capacity,
    attn_gain,
    query_weight,
    key_value_weight,
    output_weight,
    moe_gain,
    expert_in,
    expert_out,
    out_grad,
):
    tok_rows, width = layer_in.shape
    ep_count = lax.axis_size("ep")
    ctx_count = lax.axis_size("ctx")
    ctx_rows = tok_rows * ep_count
    f32, bf16 = jnp.float32, jnp.bfloat16
    ctx_index = lax.axis_index("ctx")
    ep_index = lax.axis_index("ep")
    head_cols = query_weight.shape[1]
    flat_keyval = key_value_weight.reshape(width, 2 * HEAD_DIMENSION)

    device_ids = jnp.arange(ctx_count, dtype=jnp.int32)
    own_pair = jnp.sum(jnp.where(device_ids == ctx_index, pair_of, 0))
    holder = jnp.sum(jnp.where(pair_of[:, None] == device_ids[None, :], device_ids[:, None], 0), axis=0)
    holder = jnp.concatenate([holder, holder[::-1]])
    relative = (
        ((holder % 2) ^ (ctx_index % 2)) * 8
        + ((holder // 2 % 4 - ctx_index // 2 % 4) % 4) * 2
        + ((holder // 8) ^ (ctx_index // 8))
    )
    slots = jnp.concatenate([own_pair[None], relative]).astype(jnp.int32)
    starts = jnp.stack([own_pair, 2 * ctx_count - 1 - own_pair]) * BLOCK
    own_pos = (starts[:, None] + jnp.arange(BLOCK, dtype=jnp.int32)[None, :]).reshape(2 * BLOCK)
    freqs = ROPE_BASE ** (-2.0 * jnp.arange(HEAD_DIMENSION // 2, dtype=f32) / HEAD_DIMENSION)
    angles = freqs[:, None] * own_pos.astype(f32)[None, :]
    cosine, sine = jnp.cos(angles), jnp.sin(angles)
    cosine_rows = jnp.tile(cosine.T, (SEQUENCE_COUNT, 1))
    sine_rows = jnp.tile(sine.T, (SEQUENCE_COUNT, 1))
    rest = jnp.ones((2 * BLOCK, HEAD_DIMENSION), f32)
    cosine_lanes = jnp.concatenate([cosine.T, cosine.T, rest], axis=1)
    sine_lanes = jnp.concatenate([sine.T, -sine.T, 0.0 * rest], axis=1)

    x_float = layer_in.astype(f32)
    rms_attn = lax.rsqrt(jnp.mean(x_float * x_float, axis=-1, keepdims=True) + NORM_EPS)
    normed = gather_ep((x_float * rms_attn * attn_gain).astype(bf16)).reshape(ctx_rows, width)
    query_t = jnp.einsum("dq,rd->qr", query_weight, normed, preferred_element_type=f32)
    keyval = jnp.dot(normed, flat_keyval, preferred_element_type=f32)
    key = turn_lanes(keyval[:, :HEAD_DIMENSION], cosine_rows, sine_rows)
    keyval_low = jnp.concatenate([key, keyval[:, HEAD_DIMENSION:]], axis=-1).astype(bf16)

    expert_ids = jnp.arange(EXPERTS, dtype=jnp.int32)
    named = routes[:, :, None] == expert_ids
    member = jnp.sum(named.astype(f32), axis=1)
    before = jnp.tril(jnp.ones((tok_rows, tok_rows), bf16), -1)
    rank = jnp.dot(before, member.astype(bf16), preferred_element_type=f32)
    kept = (member > 0) & (rank < capacity.astype(f32)[None, :])
    place = jnp.where(kept, rank, -1.0).T
    gates = jnp.sum(jnp.where(named, gate_weights[:, :, None], 0.0), axis=1).T
    gates_high = gates.astype(bf16)
    gates_low = (gates - gates_high.astype(f32)).astype(bf16)
    meta = jnp.stack([place.astype(bf16), gates_high, gates_low]).reshape(-1, width)
    meta = jnp.pad(meta, ((0, META_ROWS - meta.shape[0]), (0, 0)))
    carried = jnp.concatenate([output_weight, out_grad, meta], axis=0)
    keyval_low, carried = lax.optimization_barrier((keyval_low, carried))
    carried_all = lax.all_gather(carried, "ep", axis=0)
    pieces = gather_ctx(keyval_low.reshape(SEQUENCE_COUNT, 2, BLOCK, 2 * HEAD_DIMENSION))
    attended, attended_full, lse, query_pad = attention_forward(slots, query_t, cosine, sine, pieces)

    merged = exchange(attended.reshape(ep_count, tok_rows, head_cols), "ep")
    projection = carried_all[:, :head_cols].reshape(ep_count * head_cols, width)
    merged = merged.transpose(1, 0, 2).reshape(tok_rows, ep_count * head_cols)
    residual = x_float + jnp.dot(merged, projection, preferred_element_type=f32)
    rms_moe = lax.rsqrt(jnp.mean(residual * residual, axis=-1, keepdims=True) + NORM_EPS)
    moe_in = gather_ep((residual * rms_moe * moe_gain).astype(bf16))

    tiles = ep_count // 2
    tile_tokens = 2 * tok_rows
    local_experts = expert_in.shape[0]
    meta_at = head_cols + tok_rows
    meta_all = carried_all[:, meta_at : meta_at + 3 * EXPERTS * tok_rows // width]
    meta_all = meta_all.reshape(tiles, 2, 3, EXPERTS, tok_rows)
    meta_all = wide(lax.dynamic_slice_in_dim(meta_all, ep_index * local_experts, local_experts, axis=3))
    place_all = meta_all[:, :, 0].astype(jnp.int32)
    place_all = jnp.where(place_all >= 0, place_all + jnp.arange(2, dtype=jnp.int32)[None, :, None, None] * CAP, -1)
    gates_all = meta_all[:, :, 1] + meta_all[:, :, 2]
    by_expert = lambda v: v.transpose(2, 0, 1, 3).reshape(local_experts, tiles, 1, tile_tokens)
    place_all, gates_all = by_expert(place_all), by_expert(gates_all)
    kept_in, kept_act, kept_grad, kept_gu, grad_moe = expert_pass(
        head_cols, moe_in.reshape(tiles, tile_tokens, width), carried_all, place_all, gates_all, expert_in, expert_out
    )
    grad_moe_in = jnp.sum(wide(exchange(grad_moe.reshape(ep_count, tok_rows, width), "ep")), axis=0)
    made, expert_grads = weight_pass(
        (ctx_index // 8)[None].astype(jnp.int32), place_all, gates_all, kept_in, kept_act, kept_grad, kept_gu, expert_out, ctx_count
    )

    expert_grads, grad_moe_in = lax.optimization_barrier((expert_grads, grad_moe_in))

    grad_top = out_grad.astype(f32)
    scaled = grad_moe_in * moe_gain
    moe_gain_part = jnp.sum(grad_moe_in * residual * rms_moe, axis=0)
    inner = jnp.mean(scaled * residual, axis=-1, keepdims=True)
    grad_res = grad_top + rms_moe * scaled - residual * (rms_moe * rms_moe * rms_moe) * inner
    grad_attn = grad_res.astype(bf16)

    grad_att = lax.dot_general(
        grad_attn, projection, (((1,), (1,)), ((), ())), preferred_element_type=f32
    ).astype(bf16)
    grad_att = grad_att.reshape(tok_rows, ep_count, head_cols).transpose(1, 0, 2)
    grad_att = exchange(grad_att, "ep").reshape(ctx_rows, head_cols)
    output_grad = lax.dot_general(
        merged, grad_attn, (((0,), (0,)), ((), ())), preferred_element_type=f32
    ).astype(bf16)
    expert_grads = lax.psum_scatter(
        expert_grads, "ctx", scatter_dimension=0, tiled=True, axis_index_groups=SAME_Z
    )[0]
    made, grad_att = lax.optimization_barrier((made, grad_att))
    made = exchange(made.reshape(ep_count, tok_rows, width), "ep")
    grad_query, *grad_pieces = attention_backward(
        slots, grad_att, cosine, sine, pieces, query_pad, attended_full, lse
    )
    made, output_grad, *grad_pieces = lax.optimization_barrier((made, output_grad, *grad_pieces))
    output_grad = exchange(output_grad.reshape(ep_count, head_cols, width), "ep")
    query_grad = jnp.einsum("rd,rq->dq", normed, grad_query, preferred_element_type=f32)
    own, from_z, others_z, expert_grads = scatter_ctx(grad_pieces, expert_grads)
    query_grad, output_grad, others_z, own, from_z = lax.optimization_barrier(
        (query_grad, output_grad, others_z, own, from_z)
    )
    grad_kv_low, payload = turn_back(
        own, from_z, cosine_lanes, sine_lanes, grad_query, query_weight, flat_keyval,
        normed, attn_gain[None], moe_gain_part[None],
    )
    payload = exchange(payload, "ep")

    keyval_grad = jnp.einsum("rd,rk->dk", normed, grad_kv_low, preferred_element_type=f32)
    in_rows = width // ctx_count
    extra = jnp.sum(wide(payload[:, tok_rows:]), axis=0)
    gains = two_terms(jnp.stack([extra[0] + extra[1], extra[2] + extra[3]])).reshape(-1, head_cols)
    output_grad = low(jnp.sum(wide(output_grad), axis=0)).T
    small = jnp.stack([low(query_grad), low(keyval_grad), output_grad]).reshape(3, ctx_count, in_rows, head_cols)
    small = small.transpose(1, 0, 2, 3).reshape(ctx_count, -1, head_cols)
    small = jnp.concatenate([small, jnp.broadcast_to(gains[None], (ctx_count,) + gains.shape)], axis=1)
    small = jnp.sum(wide(exchange(small, "ctx")), axis=0)
    gains = small[3 * in_rows :].reshape(2, 2, width)
    gains = gains[0] + gains[1]
    small = small[: 3 * in_rows].reshape(3, in_rows, head_cols)
    expert_grads = wide(expert_grads) + wide(others_z)
    grad_normed = jnp.sum(wide(payload[:, :tok_rows]), axis=0)
    scaled = grad_normed * attn_gain
    inner = jnp.mean(scaled * x_float, axis=-1, keepdims=True)
    input_grad = grad_res + rms_attn * scaled - x_float * (rms_attn * rms_attn * rms_attn) * inner
    layer_out = (residual + jnp.sum(wide(made), axis=0)).astype(bf16)
    return (
        layer_out,
        input_grad,
        gains[0],
        small[0],
        small[1].reshape(in_rows, 1, 2 * HEAD_DIMENSION),
        small[2].T,
        gains[1],
        expert_grads[:, :in_rows],
        expert_grads[:, in_rows:],
    )


def solution(mesh):
    in_specs = (
        P(("ctx", "ep"), None),
        P(),
        P(("ctx", "ep"), None),
        P(("ctx", "ep"), None),
        P(),
        P(),
        P(None, "ep"),
        P(None, "ep", None),
        P("ep", None),
        P(),
        P("ep", None, None),
        P("ep", None, None),
        P(("ctx", "ep"), None),
    )
    out_specs = (
        P(("ctx", "ep"), None),
        P(("ctx", "ep"), None),
        P(),
        P("ctx", "ep"),
        P("ctx", "ep", None),
        P("ep", "ctx"),
        P(),
        P("ep", "ctx", None),
        P("ep", "ctx", None),
    )
    return jax.shard_map(body, mesh=mesh, in_specs=in_specs, out_specs=out_specs, check_vma=False)
```

```python
import functools

import jax
import jax.numpy as jnp
from jax import lax
from jax.experimental import pallas as pl
from jax.experimental.pallas import tpu as pltpu
from jax.sharding import PartitionSpec as P

VMEM_LIMIT = 56 * 1024 * 1024
CAP = 48

HEAD_DIMENSION = 64
SCORE_SCALE = 1.0 / 64.0
MASK_FILL = -1e30
LOG2E = 1.4426950408889634
BLOCK = 256


def causal_mask(width):
    key_at = lax.broadcasted_iota(jnp.int32, (BLOCK, width), 0)
    query_at = lax.broadcasted_iota(jnp.int32, (BLOCK, width), 1) % BLOCK
    return key_at <= query_at


def turn_rows(u, cosine, sine):
    half = HEAD_DIMENSION // 2
    u1, u2 = u[:half], u[half:]
    return jnp.concatenate([u1 * cosine - u2 * sine, u2 * cosine + u1 * sine], axis=0)


def forward_kernel(slots, query_t, cosine, sine, *refs):
    pieces, (out_rows, out_full, out_lse, q_pad, keyval, arrived, top, total, acc) = refs[:-9], refs[-9:]
    copies = start_copies(pieces, keyval, arrived)
    seqs = keyval.shape[1]
    heads = query_t.shape[0] // HEAD_DIMENSION
    width = heads * BLOCK
    blocks = 2 * keyval.shape[0]
    factor = SCORE_SCALE * LOG2E
    low, high = slots[0], blocks - 1 - slots[0]

    for s in range(seqs):
        q_pad[s, HEAD_DIMENSION:, :] = jnp.zeros((HEAD_DIMENSION, 2 * width), jnp.bfloat16)
        for h in range(2):
            for g in range(heads):
                rows = slice(g * HEAD_DIMENSION, (g + 1) * HEAD_DIMENSION)
                at = (s * 2 + h) * BLOCK
                turned = turn_rows(
                    query_t[rows, at : at + BLOCK],
                    cosine[:, h * BLOCK : (h + 1) * BLOCK],
                    sine[:, h * BLOCK : (h + 1) * BLOCK],
                )
                to = h * width + g * BLOCK
                q_pad[s, :HEAD_DIMENSION, to : to + BLOCK] = turned.astype(jnp.bfloat16)
    top[...] = jnp.full(top.shape, MASK_FILL, jnp.float32)
    total[...] = jnp.zeros(total.shape, jnp.float32)
    acc[...] = jnp.zeros(acc.shape, jnp.float32)
    for copy in copies:
        copy.wait()

    def tile(s, start, size, kvs, v_ts, masked):
        cols = slice(start, start + size)
        queries = q_pad[s, :, cols]
        scores = [jnp.dot(kv, queries, preferred_element_type=jnp.float32) for kv in kvs]
        if masked:
            scores = [jnp.where(causal_mask(size), part, MASK_FILL) for part in scores]
        before = top[s, :, cols]
        now = before
        for part in scores:
            now = jnp.maximum(now, jnp.max(part, axis=0, keepdims=True))
        shrink = jnp.exp2((before - now) * factor)
        summed = total[s, :, cols] * shrink
        result = acc[s, :, cols] * shrink
        offset = now * factor
        for part, v_t in zip(scores, v_ts):
            probs = jnp.exp2(part * factor - offset)
            summed = summed + jnp.sum(probs, axis=0, keepdims=True)
            result = result + jnp.dot(v_t, probs.astype(jnp.bfloat16), preferred_element_type=jnp.float32)
        top[s, :, cols] = now
        total[s, :, cols] = summed
        acc[s, :, cols] = result

    def step(blocks_now, low_mode, high_mode):
        for s in range(seqs):
            kvs, v_ts = [], []
            for block in blocks_now:
                half = jnp.where(block >= blocks // 2, 1, 0)
                kv = keyval[slots[1 + block], s, half]
                kvs.append(kv)
                v_ts.append(kv.T[HEAD_DIMENSION:])
            for start, mode in ((0, low_mode), (width, high_mode)):
                if mode:
                    tile(s, start, width, kvs, v_ts, mode == "diagonal")

    @pl.loop(0, low // 2)
    def _(pair):
        step([2 * pair, 2 * pair + 1], "full", "full")

    @pl.when(low % 2 == 1)
    def _():
        step([low - 1], "full", "full")

    step([low], "diagonal", "full")

    @pl.loop(0, (high - low - 1) // 2)
    def _(pair):
        step([low + 1 + 2 * pair, low + 2 + 2 * pair], None, "full")

    step([high], None, "diagonal")

    for s in range(seqs):
        attended = acc[s] / total[s]
        out_full[s] = attended
        out_lse[s] = top[s] * factor + jnp.log2(total[s])
        for h in range(2):
            at = (s * 2 + h) * BLOCK
            parts = [attended[:, h * width + g * BLOCK : h * width + (g + 1) * BLOCK] for g in range(heads)]
            out_rows[at : at + BLOCK] = jnp.concatenate(parts, axis=0).T.astype(jnp.bfloat16)


def start_copies(pieces, keyval, arrived):
    copies = [
        pltpu.make_async_copy(piece, keyval.at[i], arrived.at[i]) for i, piece in enumerate(pieces)
    ]
    for copy in copies:
        copy.start()
    return copies


def attention_forward(slots, query_t, cosine, sine, pieces):
    seqs = pieces[0].shape[0]
    heads = query_t.shape[0] // HEAD_DIMENSION
    cols = 2 * heads * BLOCK
    rows = query_t.shape[1]
    vmem = pl.BlockSpec(memory_space=pltpu.VMEM)
    return pl.pallas_call(
        forward_kernel,
        name="attention_forward",
        out_shape=(
            jax.ShapeDtypeStruct((rows, heads * HEAD_DIMENSION), jnp.bfloat16),
            jax.ShapeDtypeStruct((seqs, HEAD_DIMENSION, cols), jnp.float32),
            jax.ShapeDtypeStruct((seqs, 1, cols), jnp.float32),
            jax.ShapeDtypeStruct((seqs, 2 * HEAD_DIMENSION, cols), jnp.bfloat16),
        ),
        in_specs=[pl.BlockSpec(memory_space=pltpu.SMEM)]
        + [vmem] * 3
        + [pl.BlockSpec(memory_space=pl.ANY)] * len(pieces),
        out_specs=(vmem,) * 4,
        scratch_shapes=[
            pltpu.VMEM((len(pieces),) + pieces[0].shape, jnp.bfloat16),
            pltpu.SemaphoreType.DMA((len(pieces),)),
            pltpu.VMEM((seqs, 1, cols), jnp.float32),
            pltpu.VMEM((seqs, 1, cols), jnp.float32),
            pltpu.VMEM((seqs, HEAD_DIMENSION, cols), jnp.float32),
        ],
        compiler_params=pltpu.CompilerParams(vmem_limit_bytes=VMEM_LIMIT),
        cost_estimate=pl.CostEstimate(flops=6 * 10**9, bytes_accessed=8 * 2**20, transcendentals=9 * 10**6),
    )(slots, query_t, cosine, sine, *pieces)


def backward_kernel(slots, grad_rows, cosine, sine, q_pad, out_full, lse, *refs):
    count = (len(refs) - 10) // 2
    pieces, (grad_query, *out_pieces) = refs[:count], refs[count : 2 * count + 1]
    keyval, arrived, grad_keyval, left, d_pad, q_rows, d_rows, centre, acc = refs[2 * count + 1 :]
    copies = start_copies(pieces, keyval, arrived)
    seqs = keyval.shape[1]
    heads = grad_rows.shape[1] // HEAD_DIMENSION
    width = heads * BLOCK
    blocks = 2 * keyval.shape[0]
    factor = SCORE_SCALE * LOG2E
    low, high = slots[0], blocks - 1 - slots[0]

    for s in range(seqs):
        d_pad[s, :HEAD_DIMENSION, :] = jnp.zeros((HEAD_DIMENSION, 2 * width), jnp.bfloat16)
        for h in range(2):
            at = (s * 2 + h) * BLOCK
            turned = grad_rows[at : at + BLOCK].T
            for g in range(heads):
                to = h * width + g * BLOCK
                d_pad[s, HEAD_DIMENSION:, to : to + BLOCK] = turned[
                    g * HEAD_DIMENSION : (g + 1) * HEAD_DIMENSION
                ]
        centre[s] = jnp.sum(
            d_pad[s, HEAD_DIMENSION:].astype(jnp.float32) * out_full[s], axis=0, keepdims=True
        )
        for to in range(0, 2 * width, BLOCK):
            q_rows[s, to : to + BLOCK, :] = q_pad[s, :, to : to + BLOCK].T
            d_rows[s, to : to + BLOCK, :] = d_pad[s, :, to : to + BLOCK].T
    acc[...] = jnp.zeros(acc.shape, jnp.float32)
    for copy in copies:
        copy.wait()

    def tile(s, start, size, kv, k_t, masked):
        cols = slice(start, start + size)
        scores = jnp.dot(kv, q_pad[s, :, cols], preferred_element_type=jnp.float32)
        probs = jnp.exp2(scores * factor - lse[s, :, cols])
        if masked:
            probs = jnp.where(causal_mask(size), probs, 0.0)
        grad_probs = jnp.dot(kv, d_pad[s, :, cols], preferred_element_type=jnp.float32)
        grad_scores = (probs * (grad_probs - centre[s, :, cols])).astype(jnp.bfloat16)
        acc[s, :, cols] = acc[s, :, cols] + jnp.dot(
            k_t, grad_scores, preferred_element_type=jnp.float32
        )
        return (
            jnp.dot(grad_scores, q_rows[s, cols], preferred_element_type=jnp.float32) * SCORE_SCALE
            + jnp.dot(probs.astype(jnp.bfloat16), d_rows[s, cols], preferred_element_type=jnp.float32)
        )

    def step(block, low_mode, high_mode):
        half = jnp.where(block >= blocks // 2, 1, 0)
        device = slots[1 + block]
        for s in range(seqs):
            kv = keyval[device, s, half]
            k_t = kv.T[:HEAD_DIMENSION]
            summed = None
            for start, mode in ((0, low_mode), (width, high_mode)):
                if mode:
                    part = tile(s, start, width, kv, k_t, mode == "diagonal")
                    summed = part if summed is None else summed + part
            if summed is None:
                summed = jnp.zeros((BLOCK, 2 * HEAD_DIMENSION), jnp.float32)
            grad_keyval[device, s, half] = summed.astype(jnp.bfloat16)

    @pl.loop(0, low)
    def _(block):
        step(block, "full", "full")

    step(low, "diagonal", "full")

    @pl.loop(0, (high - low - 1) // 2)
    def _(pair):
        step(low + 1 + 2 * pair, None, "full")
        step(low + 2 + 2 * pair, None, "full")

    step(high, None, "diagonal")

    @pl.loop(high + 1, blocks)
    def _(block):
        step(block, None, None)

    copies = [
        pltpu.make_async_copy(grad_keyval.at[i], piece, left.at[i]) for i, piece in enumerate(out_pieces)
    ]
    for copy in copies:
        copy.start()
    for s in range(seqs):
        for h in range(2):
            at = (s * 2 + h) * BLOCK
            parts = [
                turn_rows(
                    acc[s, :, h * width + g * BLOCK : h * width + (g + 1) * BLOCK] * SCORE_SCALE,
                    cosine[:, h * BLOCK : (h + 1) * BLOCK],
                    -sine[:, h * BLOCK : (h + 1) * BLOCK],
                )
                for g in range(heads)
            ]
            grad_query[at : at + BLOCK] = jnp.concatenate(parts, axis=0).T.astype(jnp.bfloat16)
    for copy in copies:
        copy.wait()


def attention_backward(slots, grad_rows, cosine, sine, pieces, q_pad, out_full, lse):
    seqs = pieces[0].shape[0]
    cols = q_pad.shape[2]
    count = len(pieces)
    vmem = pl.BlockSpec(memory_space=pltpu.VMEM)
    where = pl.BlockSpec(memory_space=pl.ANY)
    return pl.pallas_call(
        backward_kernel,
        name="attention_backward",
        out_shape=[jax.ShapeDtypeStruct(grad_rows.shape, jnp.bfloat16)]
        + [jax.ShapeDtypeStruct(pieces[0].shape, jnp.bfloat16)] * count,
        in_specs=[pl.BlockSpec(memory_space=pltpu.SMEM)] + [vmem] * 6 + [where] * count,
        out_specs=[vmem] + [where] * count,
        scratch_shapes=[
            pltpu.VMEM((count,) + pieces[0].shape, jnp.bfloat16),
            pltpu.SemaphoreType.DMA((count,)),
            pltpu.VMEM((count,) + pieces[0].shape, jnp.bfloat16),
            pltpu.SemaphoreType.DMA((count,)),
            pltpu.VMEM((seqs, 2 * HEAD_DIMENSION, cols), jnp.bfloat16),
            pltpu.VMEM((seqs, cols, 2 * HEAD_DIMENSION), jnp.bfloat16),
            pltpu.VMEM((seqs, cols, 2 * HEAD_DIMENSION), jnp.bfloat16),
            pltpu.VMEM((seqs, 1, cols), jnp.float32),
            pltpu.VMEM((seqs, HEAD_DIMENSION, cols), jnp.float32),
        ],
        compiler_params=pltpu.CompilerParams(vmem_limit_bytes=VMEM_LIMIT),
        cost_estimate=pl.CostEstimate(flops=20 * 10**9, bytes_accessed=12 * 2**20, transcendentals=9 * 10**6),
    )(slots, grad_rows, cosine, sine, q_pad, out_full, lse, *pieces)


CONTRACT_LAST = (((1,), (1,)), ((), ()))


def select_rows(place, tile_slots):
    slot_at = lax.broadcasted_iota(jnp.int32, (tile_slots, place.shape[1]), 0)
    return slot_at == place


def expert_kernel(grad_at, moe, carried, place, gates, w_in, w_out, kept_in, kept_act, kept_grad, kept_gu, out, back):
    expert = pl.program_id(0)
    tiles, tile_tokens, width = moe.shape
    experts = place.shape[0]
    slots = kept_in.shape[1] // tiles

    x_tiles, g_tiles = [], []
    for j in range(tiles):
        hit = select_rows(place[expert, j], slots)
        pick = jnp.where(hit, 1.0, 0.0).astype(jnp.bfloat16)
        weight = jnp.sum(jnp.where(hit, gates[expert, j], 0.0), axis=1, keepdims=True)
        rows = jnp.dot(pick, moe[j], preferred_element_type=jnp.float32).astype(jnp.bfloat16)
        kept_in[0, j * slots : (j + 1) * slots, :] = rows
        pair = [carried[2 * j + i, grad_at : grad_at + tile_tokens // 2] for i in range(2)]
        rows = jnp.dot(pick, jnp.concatenate(pair, axis=0), preferred_element_type=jnp.float32)
        kept_grad[0, j * slots : (j + 1) * slots, :] = (rows * weight).astype(jnp.bfloat16)
    hidden = w_out.shape[1]
    gate_up = jnp.dot(kept_in[0], w_in[0], preferred_element_type=jnp.float32)
    grad_act = lax.dot_general(
        kept_grad[0], w_out[0], CONTRACT_LAST, preferred_element_type=jnp.float32
    )
    gate, up = gate_up[:, :hidden], gate_up[:, hidden:]
    sigmoid = 1.0 / (1.0 + jnp.exp(-gate))
    silu = gate * sigmoid
    kept_act[0] = (silu * up).astype(jnp.bfloat16)
    kept_gu[0, :, :hidden] = (grad_act * up * (sigmoid * (1.0 + gate * (1.0 - sigmoid)))).astype(jnp.bfloat16)
    kept_gu[0, :, hidden:] = (grad_act * silu).astype(jnp.bfloat16)
    grad_rows = lax.dot_general(
        kept_gu[0], w_in[0], CONTRACT_LAST, preferred_element_type=jnp.float32
    ).astype(jnp.bfloat16)
    for j in range(tiles):
        back[expert, j] = grad_rows[j * slots : (j + 1) * slots]

    @pl.when(expert == experts - 1)
    def _():
        for j in range(tiles):
            scatter_rows(place, [back[e, j] for e in range(experts)], j, slots, out)


def scatter_rows(place, rows, j, slots, out):
    picks = [
        jnp.where(select_rows(place[e, j], slots), 1.0, 0.0) for e in range(len(rows))
    ]
    pick = jnp.concatenate(picks, axis=0).T.astype(jnp.bfloat16)
    stacked = jnp.concatenate(rows, axis=0)
    out[j] = jnp.dot(pick, stacked, preferred_element_type=jnp.float32).astype(jnp.bfloat16)


def expert_pass(grad_at, moe, carried, place, gates, w_in, w_out):
    tiles, tile_tokens, width = moe.shape
    experts, _, hidden2 = w_in.shape
    hidden = hidden2 // 2
    slots = CAP * tile_tokens // 128
    rows = tiles * slots
    whole = pl.BlockSpec(memory_space=pltpu.VMEM)
    each = lambda shape: pl.BlockSpec((1,) + shape, lambda e: (e, 0, 0))
    return pl.pallas_call(
        functools.partial(expert_kernel, grad_at),
        name="expert_pass",
        grid=(experts,),
        out_shape=(
            jax.ShapeDtypeStruct((experts, rows, width), jnp.bfloat16),
            jax.ShapeDtypeStruct((experts, rows, hidden), jnp.bfloat16),
            jax.ShapeDtypeStruct((experts, rows, width), jnp.bfloat16),
            jax.ShapeDtypeStruct((experts, rows, hidden2), jnp.bfloat16),
            jax.ShapeDtypeStruct(moe.shape, jnp.bfloat16),
        ),
        in_specs=[whole] * 4 + [each((width, hidden2)), each((hidden, width))],
        out_specs=(
            each((rows, width)),
            each((rows, hidden)),
            each((rows, width)),
            each((rows, hidden2)),
            whole,
        ),
        scratch_shapes=[pltpu.VMEM((experts, tiles, slots, width), jnp.bfloat16)],
        compiler_params=pltpu.CompilerParams(vmem_limit_bytes=VMEM_LIMIT),
        cost_estimate=pl.CostEstimate(flops=12 * 10**9, bytes_accessed=28 * 2**20, transcendentals=10**6),
    )(moe, carried, place, gates, w_in, w_out)


def weight_kernel(own_z, place, gates, kept_in, kept_act, kept_grad, kept_gu, w_out, out, grads, back):
    expert = pl.program_id(0)
    experts, tiles = place.shape[:2]
    slots = kept_in.shape[1] // tiles
    made = jnp.dot(kept_act[0], w_out[0], preferred_element_type=jnp.float32)
    for j in range(tiles):
        hit = select_rows(place[expert, j], slots)
        weight = jnp.sum(jnp.where(hit, gates[expert, j], 0.0), axis=1, keepdims=True)
        back[expert, j] = (made[j * slots : (j + 1) * slots] * weight).astype(jnp.bfloat16)
    line, _, _, _, width = grads.shape
    in_rows, hidden = kept_in.shape[2] // (2 * line), kept_act.shape[2]
    grad_in = jnp.dot(kept_in[0].T, kept_gu[0], preferred_element_type=jnp.float32)
    grad_in = grad_in.astype(jnp.bfloat16).reshape(2, line, in_rows, width)
    grad_out = jnp.dot(kept_act[0].T, kept_grad[0], preferred_element_type=jnp.float32)
    grad_out = grad_out.astype(jnp.bfloat16).reshape(2, line, hidden // (2 * line), width)
    for z in range(2):
        away = own_z[0] ^ z
        grads[:, away, 0, :in_rows] = grad_in[z]
        grads[:, away, 0, in_rows:] = grad_out[z]

    @pl.when(expert == experts - 1)
    def _():
        for j in range(tiles):
            scatter_rows(place, [back[e, j] for e in range(experts)], j, slots, out)


def weight_pass(own_z, place, gates, kept_in, kept_act, kept_grad, kept_gu, w_out, shares):
    experts, hidden, width = w_out.shape
    tiles = place.shape[1]
    tile_tokens = place.shape[3]
    rows = kept_in.shape[1]
    whole = pl.BlockSpec(memory_space=pltpu.VMEM)
    each = lambda shape: pl.BlockSpec((1,) + shape, lambda e: (e, 0, 0))
    return pl.pallas_call(
        weight_kernel,
        name="weight_pass",
        grid=(experts,),
        out_shape=(
            jax.ShapeDtypeStruct((tiles, tile_tokens, width), jnp.bfloat16),
            jax.ShapeDtypeStruct((shares // 2, 2, experts, (width + hidden) // shares, width), jnp.bfloat16),
        ),
        in_specs=[pl.BlockSpec(memory_space=pltpu.SMEM)]
        + [whole] * 2
        + [each((rows, width)), each((rows, hidden)), each((rows, width)), each((rows, 2 * hidden)), each((hidden, width))],
        out_specs=(
            whole,
            pl.BlockSpec((shares // 2, 2, 1, (width + hidden) // shares, width), lambda e: (0, 0, e, 0, 0)),
        ),
        scratch_shapes=[pltpu.VMEM((experts, tiles, rows // tiles, width), jnp.bfloat16)],
        compiler_params=pltpu.CompilerParams(vmem_limit_bytes=VMEM_LIMIT),
        cost_estimate=pl.CostEstimate(flops=8 * 10**9, bytes_accessed=28 * 2**20, transcendentals=0),
    )(own_z, place, gates, kept_in, kept_act, kept_grad, kept_gu, w_out)

EXPERTS = 32
TOP = 8
SEQUENCE_COUNT = 2
NORM_EPS = 1e-06
ROPE_BASE = 10000.0
META_ROWS = 16

SWAP_CORE = [(c, c ^ 1) for c in range(16)]
SWAP_Z = [(c, c ^ 8) for c in range(16)]
SAME_Z = [list(range(8)), list(range(8, 16))]


def shift_x(step):
    return [(c, ((c // 8) * 4 + (c // 2 % 4 + step) % 4) * 2 + c % 2) for c in range(16)]


def up(values):
    return lax.ppermute(values, "ctx", shift_x(1))


def down(values):
    return lax.ppermute(values, "ctx", shift_x(-1))


def swap_core(values):
    return lax.ppermute(values, "ctx", SWAP_CORE)


def swap_z(values):
    return lax.ppermute(values, "ctx", SWAP_Z)


def wide(values):
    return values.astype(jnp.float32)


def low(values):
    return values.astype(jnp.bfloat16)


def exchange(values, axis):
    return lax.all_to_all(values, axis, split_axis=0, concat_axis=0, tiled=True)


def gather_ep(own):
    return exchange(jnp.broadcast_to(own[None], (lax.axis_size("ep"),) + own.shape), "ep")


def gather_ctx(own):
    z = swap_z(own)
    left, right = up(own), down(own)
    z_left, z_right = up(z), down(z)
    far, z_far = up(left), down(z_right)
    near = [own, z, right, z_right, far, z_far, left, z_left]
    return near + [swap_core(block) for block in near]


def scatter_ctx(parts):
    sums = {}
    for k in (4, 5, 3, 6, 2, 7, 1, 0):
        sums[k] = wide(parts[k]) + wide(swap_core(parts[8 + k]))
    far, z_far = up(low(sums[4])), down(low(sums[5]))
    z_right, left = up(low(sums[3])), down(low(sums[6]))
    right, z_left = up(low(sums[2] + wide(far))), down(low(sums[7] + wide(z_far)))
    own = sums[0] + wide(right) + wide(left)
    z = sums[1] + wide(z_right) + wide(z_left)
    return own, swap_z(low(z))


def turn_back_kernel(
    first, second, cosine, sine, grad_query, w_query, w_keyval, normed, gain, other_gain, out, payload
):
    half = HEAD_DIMENSION // 2
    lane = lax.broadcasted_iota(jnp.int32, (BLOCK, 2 * HEAD_DIMENSION), 1)
    shares, rows_each, width = payload.shape
    rows_each = out.shape[0] // shares
    per_block = BLOCK // rows_each
    gain_sum = jnp.zeros((1, width), jnp.float32)
    for s in range(first.shape[0]):
        for h in range(2):
            rows = slice(h * BLOCK, (h + 1) * BLOCK)
            u = first[s, h] + second[s, h].astype(jnp.float32)
            after = pltpu.roll(u, 2 * HEAD_DIMENSION - half, 1)
            before = pltpu.roll(u, half, 1)
            turned = jnp.where(lane < half, after, before)
            at = (2 * s + h) * BLOCK
            turned = (u * cosine[rows] + turned * sine[rows]).astype(jnp.bfloat16)
            out[at : at + BLOCK] = turned
            grads = lax.dot_general(turned, w_keyval[...], CONTRACT_LAST, preferred_element_type=jnp.float32)
            grads = grads + lax.dot_general(
                grad_query[at : at + BLOCK], w_query[...], CONTRACT_LAST, preferred_element_type=jnp.float32
            )
            gain_sum = gain_sum + jnp.sum(
                grads * normed[at : at + BLOCK].astype(jnp.float32), axis=0, keepdims=True
            )
            share = (2 * s + h) * per_block
            for i in range(per_block):
                payload[share + i, :rows_each] = grads[i * rows_each : (i + 1) * rows_each].astype(jnp.bfloat16)
    gain_sum = gain_sum / gain[...]
    tail = []
    for part in (gain_sum, other_gain[...]):
        high = part.astype(jnp.bfloat16).astype(jnp.float32)
        tail += [high, part - high]
    tail = jnp.concatenate(tail + [jnp.zeros((META_ROWS - 4, width), jnp.float32)], axis=0)
    for share in range(shares):
        payload[share, rows_each:] = tail.astype(jnp.bfloat16)


def turn_back(first, second, cosine, sine, grad_query, w_query, w_keyval, normed, gain, other_gain):
    vmem = pl.BlockSpec(memory_space=pltpu.VMEM)
    rows, width = normed.shape
    shares = lax.axis_size("ep")
    return pl.pallas_call(
        turn_back_kernel,
        name="turn_back",
        out_shape=(
            jax.ShapeDtypeStruct((rows, 2 * HEAD_DIMENSION), jnp.bfloat16),
            jax.ShapeDtypeStruct((shares, rows // shares + META_ROWS, width), jnp.bfloat16),
        ),
        in_specs=[vmem] * 10,
        out_specs=(vmem,) * 2,
        compiler_params=pltpu.CompilerParams(vmem_limit_bytes=VMEM_LIMIT // 2),
        cost_estimate=pl.CostEstimate(flops=5 * 10**8, bytes_accessed=7 * 2**20, transcendentals=0),
    )(first, second, cosine, sine, grad_query, w_query, w_keyval, normed, gain, other_gain)


def two_terms(values):
    high = low(values)
    return jnp.stack([high, low(values - wide(high))])


def turn_lanes(u, cosine, sine):
    half = HEAD_DIMENSION // 2
    u1, u2 = u[:, :half], u[:, half:]
    return jnp.concatenate([u1 * cosine - u2 * sine, u2 * cosine + u1 * sine], axis=-1)


def body(
    layer_in,
    pair_of,
    routes,
    gate_weights,
    capacity,
    attn_gain,
    query_weight,
    key_value_weight,
    output_weight,
    moe_gain,
    expert_in,
    expert_out,
    out_grad,
):
    tok_rows, width = layer_in.shape
    ep_count = lax.axis_size("ep")
    ctx_count = lax.axis_size("ctx")
    ctx_rows = tok_rows * ep_count
    f32, bf16 = jnp.float32, jnp.bfloat16
    ctx_index = lax.axis_index("ctx")
    ep_index = lax.axis_index("ep")
    head_cols = query_weight.shape[1]
    flat_keyval = key_value_weight.reshape(width, 2 * HEAD_DIMENSION)

    device_ids = jnp.arange(ctx_count, dtype=jnp.int32)
    own_pair = jnp.sum(jnp.where(device_ids == ctx_index, pair_of, 0))
    holder = jnp.sum(jnp.where(pair_of[:, None] == device_ids[None, :], device_ids[:, None], 0), axis=0)
    holder = jnp.concatenate([holder, holder[::-1]])
    relative = (
        ((holder % 2) ^ (ctx_index % 2)) * 8
        + ((holder // 2 % 4 - ctx_index // 2 % 4) % 4) * 2
        + ((holder // 8) ^ (ctx_index // 8))
    )
    slots = jnp.concatenate([own_pair[None], relative]).astype(jnp.int32)
    starts = jnp.stack([own_pair, 2 * ctx_count - 1 - own_pair]) * BLOCK
    own_pos = (starts[:, None] + jnp.arange(BLOCK, dtype=jnp.int32)[None, :]).reshape(2 * BLOCK)
    freqs = ROPE_BASE ** (-2.0 * jnp.arange(HEAD_DIMENSION // 2, dtype=f32) / HEAD_DIMENSION)
    angles = freqs[:, None] * own_pos.astype(f32)[None, :]
    cosine, sine = jnp.cos(angles), jnp.sin(angles)
    cosine_rows = jnp.tile(cosine.T, (SEQUENCE_COUNT, 1))
    sine_rows = jnp.tile(sine.T, (SEQUENCE_COUNT, 1))
    rest = jnp.ones((2 * BLOCK, HEAD_DIMENSION), f32)
    cosine_lanes = jnp.concatenate([cosine.T, cosine.T, rest], axis=1)
    sine_lanes = jnp.concatenate([sine.T, -sine.T, 0.0 * rest], axis=1)

    x_float = layer_in.astype(f32)
    rms_attn = lax.rsqrt(jnp.mean(x_float * x_float, axis=-1, keepdims=True) + NORM_EPS)
    normed = gather_ep((x_float * rms_attn * attn_gain).astype(bf16)).reshape(ctx_rows, width)
    query_t = jnp.einsum("dq,rd->qr", query_weight, normed, preferred_element_type=f32)
    keyval = jnp.dot(normed, flat_keyval, preferred_element_type=f32)
    key = turn_lanes(keyval[:, :HEAD_DIMENSION], cosine_rows, sine_rows)
    keyval_low = jnp.concatenate([key, keyval[:, HEAD_DIMENSION:]], axis=-1).astype(bf16)

    expert_ids = jnp.arange(EXPERTS, dtype=jnp.int32)
    named = routes[:, :, None] == expert_ids
    member = jnp.sum(named.astype(f32), axis=1)
    before = jnp.tril(jnp.ones((tok_rows, tok_rows), bf16), -1)
    rank = jnp.dot(before, member.astype(bf16), preferred_element_type=f32)
    kept = (member > 0) & (rank < capacity.astype(f32)[None, :])
    place = jnp.where(kept, rank, -1.0).T
    gates = jnp.sum(jnp.where(named, gate_weights[:, :, None], 0.0), axis=1).T
    gates_high = gates.astype(bf16)
    gates_low = (gates - gates_high.astype(f32)).astype(bf16)
    meta = jnp.stack([place.astype(bf16), gates_high, gates_low]).reshape(-1, width)
    meta = jnp.pad(meta, ((0, META_ROWS - meta.shape[0]), (0, 0)))
    carried = jnp.concatenate([output_weight, out_grad, meta], axis=0)
    keyval_low, carried = lax.optimization_barrier((keyval_low, carried))
    carried_all = lax.all_gather(carried, "ep", axis=0)
    pieces = gather_ctx(keyval_low.reshape(SEQUENCE_COUNT, 2, BLOCK, 2 * HEAD_DIMENSION))
    attended, attended_full, lse, query_pad = attention_forward(slots, query_t, cosine, sine, pieces)

    merged = exchange(attended.reshape(ep_count, tok_rows, head_cols), "ep")
    projection = carried_all[:, :head_cols].reshape(ep_count * head_cols, width)
    merged = merged.transpose(1, 0, 2).reshape(tok_rows, ep_count * head_cols)
    residual = x_float + jnp.dot(merged, projection, preferred_element_type=f32)
    rms_moe = lax.rsqrt(jnp.mean(residual * residual, axis=-1, keepdims=True) + NORM_EPS)
    moe_in = gather_ep((residual * rms_moe * moe_gain).astype(bf16))

    tiles = ep_count // 2
    tile_tokens = 2 * tok_rows
    local_experts = expert_in.shape[0]
    meta_at = head_cols + tok_rows
    meta_all = carried_all[:, meta_at : meta_at + 3 * EXPERTS * tok_rows // width]
    meta_all = meta_all.reshape(tiles, 2, 3, EXPERTS, tok_rows)
    meta_all = wide(lax.dynamic_slice_in_dim(meta_all, ep_index * local_experts, local_experts, axis=3))
    place_all = meta_all[:, :, 0].astype(jnp.int32)
    place_all = jnp.where(place_all >= 0, place_all + jnp.arange(2, dtype=jnp.int32)[None, :, None, None] * CAP, -1)
    gates_all = meta_all[:, :, 1] + meta_all[:, :, 2]
    by_expert = lambda v: v.transpose(2, 0, 1, 3).reshape(local_experts, tiles, 1, tile_tokens)
    place_all, gates_all = by_expert(place_all), by_expert(gates_all)
    kept_in, kept_act, kept_grad, kept_gu, grad_moe = expert_pass(
        head_cols, moe_in.reshape(tiles, tile_tokens, width), carried_all, place_all, gates_all, expert_in, expert_out
    )
    grad_moe_in = jnp.sum(wide(exchange(grad_moe.reshape(ep_count, tok_rows, width), "ep")), axis=0)
    made, expert_grads = weight_pass(
        (ctx_index // 8)[None].astype(jnp.int32), place_all, gates_all, kept_in, kept_act, kept_grad, kept_gu, expert_out, ctx_count
    )

    expert_grads, grad_moe_in = lax.optimization_barrier((expert_grads, grad_moe_in))

    grad_top = out_grad.astype(f32)
    scaled = grad_moe_in * moe_gain
    moe_gain_part = jnp.sum(grad_moe_in * residual * rms_moe, axis=0)
    inner = jnp.mean(scaled * residual, axis=-1, keepdims=True)
    grad_res = grad_top + rms_moe * scaled - residual * (rms_moe * rms_moe * rms_moe) * inner
    grad_attn = grad_res.astype(bf16)

    grad_att = lax.dot_general(
        grad_attn, projection, (((1,), (1,)), ((), ())), preferred_element_type=f32
    ).astype(bf16)
    grad_att = grad_att.reshape(tok_rows, ep_count, head_cols).transpose(1, 0, 2)
    grad_att = exchange(grad_att, "ep").reshape(ctx_rows, head_cols)
    output_grad = lax.dot_general(
        merged, grad_attn, (((0,), (0,)), ((), ())), preferred_element_type=f32
    ).astype(bf16)
    expert_grads = lax.psum_scatter(
        expert_grads, "ctx", scatter_dimension=0, tiled=True, axis_index_groups=SAME_Z
    )[0]
    made, grad_att = lax.optimization_barrier((made, grad_att))
    made = exchange(made.reshape(ep_count, tok_rows, width), "ep")
    grad_query, *grad_pieces = attention_backward(
        slots, grad_att, cosine, sine, pieces, query_pad, attended_full, lse
    )
    made, output_grad, *grad_pieces = lax.optimization_barrier((made, output_grad, *grad_pieces))
    output_grad = exchange(output_grad.reshape(ep_count, head_cols, width), "ep")
    query_grad = jnp.einsum("rd,rq->dq", normed, grad_query, preferred_element_type=f32)
    own, from_z = scatter_ctx(grad_pieces)
    query_grad, output_grad, own, from_z = lax.optimization_barrier((query_grad, output_grad, own, from_z))
    grad_kv_low, payload = turn_back(
        own, from_z, cosine_lanes, sine_lanes, grad_query, query_weight, flat_keyval,
        normed, attn_gain[None], moe_gain_part[None],
    )
    payload = exchange(payload, "ep")
    expert_grads, payload = lax.optimization_barrier((expert_grads, payload))
    others_z = swap_z(expert_grads[1])

    keyval_grad = jnp.einsum("rd,rk->dk", normed, grad_kv_low, preferred_element_type=f32)
    in_rows = width // ctx_count
    extra = jnp.sum(wide(payload[:, tok_rows:]), axis=0)
    gains = two_terms(jnp.stack([extra[0] + extra[1], extra[2] + extra[3]])).reshape(-1, head_cols)
    output_grad = low(jnp.sum(wide(output_grad), axis=0)).T
    small = jnp.stack([low(query_grad), low(keyval_grad), output_grad]).reshape(3, ctx_count, in_rows, head_cols)
    small = small.transpose(1, 0, 2, 3).reshape(ctx_count, -1, head_cols)
    small = jnp.concatenate([small, jnp.broadcast_to(gains[None], (ctx_count,) + gains.shape)], axis=1)
    small = jnp.sum(wide(exchange(small, "ctx")), axis=0)
    gains = small[3 * in_rows :].reshape(2, 2, width)
    gains = gains[0] + gains[1]
    small = small[: 3 * in_rows].reshape(3, in_rows, head_cols)
    expert_grads = wide(expert_grads[0]) + wide(others_z)
    grad_normed = jnp.sum(wide(payload[:, :tok_rows]), axis=0)
    scaled = grad_normed * attn_gain
    inner = jnp.mean(scaled * x_float, axis=-1, keepdims=True)
    input_grad = grad_res + rms_attn * scaled - x_float * (rms_attn * rms_attn * rms_attn) * inner
    layer_out = (residual + jnp.sum(wide(made), axis=0)).astype(bf16)
    return (
        layer_out,
        input_grad,
        gains[0],
        small[0],
        small[1].reshape(in_rows, 1, 2 * HEAD_DIMENSION),
        small[2].T,
        gains[1],
        expert_grads[:, :in_rows],
        expert_grads[:, in_rows:],
    )


def solution(mesh):
    in_specs = (
        P(("ctx", "ep"), None),
        P(),
        P(("ctx", "ep"), None),
        P(("ctx", "ep"), None),
        P(),
        P(),
        P(None, "ep"),
        P(None, "ep", None),
        P("ep", None),
        P(),
        P("ep", None, None),
        P("ep", None, None),
        P(("ctx", "ep"), None),
    )
    out_specs = (
        P(("ctx", "ep"), None),
        P(("ctx", "ep"), None),
        P(),
        P("ctx", "ep"),
        P("ctx", "ep", None),
        P("ep", "ctx"),
        P(),
        P("ep", "ctx", None),
        P("ep", "ctx", None),
    )
    return jax.shard_map(body, mesh=mesh, in_specs=in_specs, out_specs=out_specs, check_vma=False)
```
